256 devices in a mesh: mod: 8 (over y, x_hi), row: 32 (over z, x_lo, core).
Axes of the slice: x: 4 (x_hi: 2, x_lo: 2; x = x_hi * 2 + x_lo), y: 4, z: 8, core: 2. Of those that a mesh axis runs over, the one named last changes fastest.
Arguments:
- image: bfloat16 [6144, 1024], P('row', 'mod'), may hold values from -16 to 16
- modality: bfloat16 [8, 6144, 1024], P('mod', 'row'), may hold values from -16 to 16
- pair_index: int32 [8, 6144], P('mod'), may hold values from 0 to 6143, each once within a row
Outputs:
- image_grad: float32 [6144, 1024], P('row', 'mod')
- modality_grad: float32 [8, 6144, 1024], P('mod', 'row')
- row_loss: float32 [8, 6144], P('mod', 'row')
- col_loss: float32 [8, 6144], P('mod', 'row')
The draws below stay inside these ranges and needn't reach their ends.
All inputs are finite; a program needn't handle non-finite values.
Results may differ from the reference program's by a relative error of at most 0.0015.
Values may be sent and summed in bfloat16 or wider, within the bound.
No kernel may reach another device: no remote copies, remote signals or barrier semaphores. Data moves between devices by JAX's collectives and lax.ppermute only.
A program may use at most 128 MiB of HBM per device.

```python
import math
import jax
import jax.numpy as jnp
from jax import lax

D = 1024
BATCH = 6144
MODS = 8


def draw_image(key, part):
    key = jax.random.fold_in(key, 11)
    first, second = jax.random.split(key)
    values = jnp.clip(jax.random.normal(first, (BATCH, D), jnp.float32), -4.0, 4.0)
    scales = jnp.exp(jax.random.uniform(second, (BATCH, 1), jnp.float32, math.log(0.6), math.log(3.2)))
    values = values * scales
    return values.astype(jnp.bfloat16)


def draw_modality(key, part):
    key = jax.random.fold_in(key, 12)
    first, second = jax.random.split(key)
    values = jnp.clip(jax.random.normal(first, (MODS, BATCH, D), jnp.float32), -4.0, 4.0)
    scales = jnp.exp(jax.random.uniform(second, (MODS, BATCH, 1), jnp.float32, math.log(0.6), math.log(3.2)))
    values = values * scales
    return values.astype(jnp.bfloat16)


def setup_inputs(seed: int = 0) -> dict:
    seeds = jax.random.split(jax.random.key(seed), 4)
    image = draw_image(jax.random.fold_in(seeds[3], 71), 0)
    modality = draw_modality(jax.random.fold_in(seeds[3], 71), 0)
    pair_index = jax.vmap(lambda own: jax.random.permutation(own, BATCH))(jax.random.split(seeds[2], MODS)).reshape((MODS, BATCH)).astype(jnp.int32)
    return dict(image=image, modality=modality, pair_index=pair_index)


def one_pair(image, keys, pairs):
    scale = D ** -0.5
    scores = jnp.dot(image, keys.T, preferred_element_type=jnp.float32) * scale
    columns = jnp.arange(BATCH, dtype=jnp.int32)
    target = pairs[:, None] == columns[None, :]
    row_max = jnp.max(scores, axis=1)
    lse_row = row_max + jnp.log(jnp.sum(jnp.exp(scores - row_max[:, None]), axis=1))
    col_max = jnp.max(scores, axis=0)
    lse_col = col_max + jnp.log(jnp.sum(jnp.exp(scores - col_max[None, :]), axis=0))
    picked = jnp.where(target, scores, jnp.float32(0.0))
    row_loss = lse_row - jnp.sum(picked, axis=1)
    col_loss = lse_col - jnp.sum(picked, axis=0)
    weights = (jnp.exp(scores - lse_row[:, None]) + jnp.exp(scores - lse_col[None, :])
               - jnp.where(target, jnp.float32(2.0), jnp.float32(0.0))).astype(jnp.bfloat16)
    image_term = jnp.dot(weights, keys, preferred_element_type=jnp.float32) * scale
    key_grad = jnp.dot(weights.T, image, preferred_element_type=jnp.float32) * scale
    return image_term, key_grad, row_loss, col_loss


def reference(image, modality, pair_index):
    def step(total, inputs):
        keys, pairs = inputs
        image_term, key_grad, row_loss, col_loss = one_pair(image, keys, pairs)
        return total + image_term, (key_grad, row_loss, col_loss)

    start = jnp.zeros((BATCH, D), jnp.float32)
    image_grad, (modality_grad, row_loss, col_loss) = lax.scan(step, start, (modality, pair_index))
    return image_grad, modality_grad, row_loss, col_loss
```

```python
import functools
import jax
import jax.numpy as jnp
from jax import lax
from jax.experimental import pallas as pl
from jax.experimental.pallas import tpu as pltpu
from jax.sharding import Mesh, PartitionSpec as P

LAST = (((1,), (1,)), ((), ()))
FIRST = (((0,), (0,)), ((), ()))
F32, BF16, I16 = jnp.float32, jnp.bfloat16, jnp.int16
PAD = 16


def call(kernel, out, name, mib, **kw):
    return pl.pallas_call(
        kernel,
        out_shape=out,
        compiler_params=pltpu.CompilerParams(vmem_limit_bytes=mib * 2**20),
        cost_estimate=pl.CostEstimate(flops=1000, bytes_accessed=1000, transcendentals=0),
        name=name,
        **kw,
    )


def shape(s, t):
    return jax.ShapeDtypeStruct(s, t)


def eye(n):
    return lax.broadcasted_iota(jnp.int32, (n, n), 0) == lax.broadcasted_iota(jnp.int32, (n, n), 1)


def to_lanes(v):
    n = v.shape[0]
    parts = []
    for a in range(0, n, 128):
        w = min(128, n - a)
        parts.append(jnp.sum(jnp.where(eye(w), v[a : a + w], F32(0)), axis=0, keepdims=True))
    return jnp.concatenate(parts, axis=1)


def to_rows(v):
    n = v.shape[1]
    parts = []
    for a in range(0, n, 128):
        w = min(128, n - a)
        parts.append(jnp.sum(jnp.where(eye(w), v[:, a : a + w], F32(0)), axis=1, keepdims=True))
    return jnp.concatenate(parts, axis=0)


def power_of(x):
    top = jnp.max(jnp.abs(x), axis=0, keepdims=True)
    return jnp.ceil(jnp.log2(jnp.maximum(top, F32(1e-30)))) - 14.0


def fixed(x):
    return x.astype(jnp.int32).astype(I16)


def encode(x, ref):
    rows, cols = x.shape
    power = power_of(x)
    ref[:rows, :] = fixed(jnp.round(x * jnp.exp2(-power)))
    ref[rows:, :] = fixed(jnp.broadcast_to(power, (PAD, cols)))


def floats(c):
    return c.astype(jnp.int32).astype(F32)


def decode(c, tiles=1):
    f = floats(c)
    rows = c.shape[-2] - PAD
    n = rows // tiles
    parts = [f[..., i * n : (i + 1) * n, :] * jnp.exp2(f[..., rows + i : rows + i + 1, :]) for i in range(tiles)]
    return parts[0] if tiles == 1 else jnp.concatenate(parts, axis=-2)


def join_kernel(idx, after, *refs):
    del after
    keys, out = refs[:4], refs[4]
    rows = keys[0].shape[0]
    for d in range(4):
        out[pl.ds(pl.multiple_of((idx[0] ^ d) * rows, 16), rows), :] = keys[d][...]


def scores_kernel(scale, tile, idx, ks0, ks1, i0, i1, i3, ia, ib, pairs, cols, s_ref, im, rs, cs):
    y = idx[1]
    nzh, rows, width = ia.shape
    n_im = im.shape[0]
    half = ks0.shape[0]

    def place(k, xh, ref, first):
        at = pl.multiple_of((lax.rem(y + 4 - k, 4) * 2 + xh) * width, 128)
        for zh in range(nzh):
            im[zh * rows : (zh + 1) * rows, pl.ds(at, width)] = ref[first + zh]

    for k, ref in ((0, i0), (1, i1), (3, i3)):
        for xh in range(2):
            place(k, xh, ref, xh * nzh)
    place(2, 0, ia, 0)
    place(2, 1, ib, 0)

    rows_of = [slice(r, r + tile) for r in range(0, n_im, tile)]
    col_top, col_sum, col_pick = [None] * 2, [None] * 2, [None] * 2
    row_state = [None] * len(rows_of)

    def online(s, state, axis):
        top = jnp.max(s, axis=axis, keepdims=True)
        if state is None:
            return top, jnp.sum(jnp.exp(s - top), axis=axis, keepdims=True)
        new = jnp.maximum(state[0], top)
        return new, state[1] * jnp.exp(state[0] - new) + jnp.sum(jnp.exp(s - new), axis=axis, keepdims=True)

    def stats(h, r):
        lanes = slice(h * half, (h + 1) * half)
        s = s_ref[rows_of[r], lanes]
        picked = jnp.where(to_rows(pairs[:, rows_of[r]]) == cols[:, lanes], s, F32(0))
        old = row_state[r]
        top, total = online(s, old and old[:2], 1)
        pick = jnp.sum(picked, axis=1, keepdims=True)
        row_state[r] = (top, total, pick if old is None else old[2] + pick)
        state = None if col_top[h] is None else (col_top[h], col_sum[h])
        col_top[h], col_sum[h] = online(s, state, 0)
        pick = jnp.sum(picked, axis=0, keepdims=True)
        col_pick[h] = pick if col_pick[h] is None else col_pick[h] + pick

    before = None
    for h, ks in enumerate((ks0, ks1)):
        for r in range(len(rows_of)):
            s = lax.dot_general(im[rows_of[r], :], ks[...], LAST, preferred_element_type=F32)
            s_ref[rows_of[r], h * half : (h + 1) * half] = s * scale
            if before:
                stats(*before)
            before = (h, r)
    stats(*before)
    for r, (top, total, pick) in enumerate(row_state):
        rs[0:1, rows_of[r]] = to_lanes(top + jnp.log(total))
        rs[1:2, rows_of[r]] = to_lanes(pick)
    for h in range(2):
        cs[0:1, h * half : (h + 1) * half] = col_top[h] + jnp.log(col_sum[h])
        cs[1:2, h * half : (h + 1) * half] = col_pick[h]


def merge(parts):
    top = functools.reduce(jnp.maximum, parts)
    return top + jnp.log(sum(jnp.exp(p - top) for p in parts))


def meet(x, y):
    return jnp.concatenate([merge([x[0:1], y[0:1]]), x[1:2] + y[1:2]], axis=0)


def meet_first_kernel(c, c_other, r, r_other, c_out, r_out):
    half = c.shape[1] // 2
    other = c_other[...]
    c_out[...] = meet(c[...], jnp.concatenate([other[:, half:], other[:, :half]], axis=1))
    r_out[...] = meet(r[...], r_other[...])


def meet_kernel(a, b, out):
    out[...] = meet(a[...], b[...])


def weights_kernel(scale, tile, idx, r0, r1, c0, c1, pairs, cols, s_ref, ks0, ks1, w_ref, own, p1, p3, o2a, o2b, rl, cl, total):
    n_im, n_ks = s_ref.shape
    half = n_ks // 2
    width = own.shape[1]
    cstat = meet(c0[...], c1[...])
    lse_col = cstat[0:1]
    cl[...] = lse_col - cstat[1:2]
    rstat = meet(r0[...], r1[...])
    lse_row = rstat[0:1]
    rl[...] = lse_row - rstat[1:2]

    def weigh(a):
        rows = slice(a, a + tile)
        s = s_ref[rows, :]
        two = jnp.where(to_rows(pairs[:, rows]) == cols[...], F32(2), F32(0))
        w = jnp.exp(s - to_rows(lse_row[:, rows])) + jnp.exp(s - lse_col) - two
        w_ref[rows, :] = w.astype(BF16)

    def term(a):
        rows = slice(a, a + tile)
        x = jnp.dot(w_ref[rows, :half], ks0[...], preferred_element_type=F32)
        x += jnp.dot(w_ref[rows, half:], ks1[...], preferred_element_type=F32)
        total[rows, :] = x * scale

    tiles = range(0, n_im, tile)
    weigh(0)
    for a in tiles:
        if a + tile < n_im:
            weigh(a + tile)
        term(a)
    for k, out in ((2, None), (1, p1), (3, p3), (0, own)):
        lanes = pl.ds(pl.multiple_of(lax.rem(idx[1] + k, 4) * width, 128), width)
        if k == 2:
            encode(total[: n_im // 2, lanes], o2a)
            encode(total[n_im // 2 :, lanes], o2b)
        else:
            out[...] = total[:, lanes]


def relay_kernel(after, p1, p3, got_a, got_b, o1, o3):
    del after
    n = p1.shape[0] // 2
    encode(jnp.concatenate([p1[:n, :] + decode(got_a[...]), p1[n:, :]], axis=0), o1)
    encode(jnp.concatenate([p3[:n, :], p3[n:, :] + decode(got_b[...])], axis=0), o3)


def key_kernel(scale, w, im, own, out):
    half = w.shape[1] // 2
    rows = half // 4
    other = lax.dot_general(w[:, half:], im[...], FIRST, preferred_element_type=F32) * scale
    for p in range(4):
        encode(other[p * rows : (p + 1) * rows, :], out.at[p])
    own[...] = lax.dot_general(w[:, :half], im[...], FIRST, preferred_element_type=F32) * scale


def key_sum_kernel(idx, after, mine, got, own, *outs):
    del after
    rows = own.shape[0]
    for d in (3, 1, 2, 0):
        p = idx[0] ^ d
        x = mine[pl.ds(pl.multiple_of(p * rows, 16), rows), :] + decode(got[p])
        if d:
            encode(x, outs[d - 1])
        else:
            own[...] = x


def image_sum_kernel(after, own, *refs):
    del after
    got, out = refs[:-1], refs[-1]
    rows = out.shape[1] - PAD
    width = out.shape[2]
    n = out.shape[0] // 2
    total = own[...] + sum(decode(g[...]) for g in got)
    for xh in range(2):
        for zh in range(n):
            encode(total[zh * rows : (zh + 1) * rows, xh * width : (xh + 1) * width], out.at[xh * n + zh])


def shift(x, axis, n, k):
    return lax.ppermute(x, axis, [(i, (i + k) % n) for i in range(n)])


def flip(x, axis, n, d):
    return lax.ppermute(x, axis, [(i, i ^ d) for i in range(n)])


def on_device(image, modality, pair_index):
    keys = modality[0]
    rows, d = keys.shape
    width = image.shape[1]
    scale = d ** (-0.5)
    nzh = lax.axis_size("zh")
    zh, y, core = lax.axis_index("zh"), lax.axis_index("y"), lax.axis_index("core")
    zx = lax.axis_index(("zl", "xl"))
    t = lax.axis_index(("zl", "xl", "core"))
    n_im, n_ks = nzh * rows, 8 * rows
    half = n_ks // 2
    smem = pl.BlockSpec(memory_space=pltpu.SMEM)
    vmem = pl.BlockSpec(memory_space=pltpu.VMEM)
    late = pl.BlockSpec(memory_space=pl.ANY)
    idx = jnp.stack([zx, y]).astype(jnp.int32)

    def flip4(x, k):
        return flip(x, ("zl", "xl"), 4, k)

    same = [keys] + [flip4(keys, k) for k in (1, 2, 3)]
    i0 = lax.all_to_all(jnp.broadcast_to(image, (2 * nzh, rows, width)), ("xh", "zh"), 0, 0)
    i1, i3 = shift(i0, "y", 4, 1), shift(i0, "y", 4, 3)
    ia, ib = shift(i1[:nzh], "y", 4, 1), shift(i3[nzh:], "y", 4, 3)
    ks0 = call(join_kernel, shape((half, d), BF16), "join", 8, in_specs=[smem, late] + [vmem] * 4)(idx, i0, *same)
    ks1 = flip(ks0, "core", 2, 1)

    pairs = lax.dynamic_index_in_dim(pair_index.reshape(nzh, 8, rows), t, axis=1, keepdims=False)
    pairs = pairs.reshape(1, n_im).astype(F32)
    p = jnp.arange(n_ks, dtype=jnp.int32)
    cols = zh * n_ks + (p % half // rows * 2 + (core ^ (p // half))) * rows + p % rows
    cols = cols.reshape(1, n_ks).astype(F32)

    tile = min(256, n_im)
    scores, im, rs, cs = call(
        functools.partial(scores_kernel, scale, tile),
        [shape((n_im, n_ks), F32), shape((n_im, d), BF16), shape((2, n_im), F32), shape((2, n_ks), F32)],
        "scores",
        28,
        in_specs=[smem] + [vmem] * 9,
    )(idx, ks0, ks1, i0, i1, i3, ia, ib, pairs, cols)
    cs, rs = call(meet_first_kernel, [shape((2, n_ks), F32), shape((2, n_im), F32)], "meet", 4, in_specs=[vmem] * 4)(
        cs, flip(cs, "core", 2, 1), rs, flip(rs, "zh", 4, 1)
    )
    rs_other = flip(rs, "zh", 4, 3)
    cs = call(meet_kernel, shape((2, n_ks), F32), "meet_x", 4, in_specs=[vmem] * 2)(cs, flip(cs, "xl", 2, 1))
    cs_other = flip(cs, "zl", 2, 1)
    outs = [shape((n_im, n_ks), BF16)] + [shape((n_im, 2 * width), F32)] * 3
    outs += [shape((n_im // 2 + PAD, 2 * width), I16)] * 2 + [shape((1, n_im), F32), shape((1, n_ks), F32)]
    weights, own, p1, p3, q2a, q2b, row_loss, col_loss = call(
        functools.partial(weights_kernel, scale, tile),
        outs,
        "weights",
        28,
        in_specs=[smem] + [vmem] * 9,
        scratch_shapes=[pltpu.VMEM((n_im, d), F32)],
    )(idx, rs, rs_other, cs, cs_other, pairs, cols, scores, ks0, ks1)
    q2a, q2b = shift(q2a, "y", 4, 1), shift(q2b, "y", 4, 3)
    mine, sent = call(
        functools.partial(key_kernel, scale),
        [shape((half, d), F32), shape((4, rows + PAD, d), I16)],
        "key_term",
        24,
        in_specs=[vmem] * 2,
    )(weights, im)
    got = flip(sent, "core", 2, 1)
    q1, q3 = call(
        relay_kernel,
        [shape((n_im + PAD, 2 * width), I16)] * 2,
        "relay",
        12,
        in_specs=[late] + [vmem] * 4,
    )(mine, p1, p3, q2a, q2b)
    own_key, *pieces = call(
        key_sum_kernel,
        [shape((rows, d), F32)] + [shape((rows + PAD, d), I16)] * 3,
        "key_sum",
        16,
        in_specs=[smem, late] + [vmem] * 2,
    )(idx, q1, mine, got)
    q1, q3 = shift(q1, "y", 4, 1), shift(q3, "y", 4, 3)
    pieces = [flip4(x, k + 1) for k, x in enumerate(pieces)]
    eighths = call(
        image_sum_kernel,
        shape((2 * nzh, rows + PAD, width), I16),
        "image_sum",
        12,
        in_specs=[late] + [vmem] * 3,
    )(own_key, own, q1, q3)
    eighths = lax.all_to_all(eighths, ("xh", "zh"), 0, 0)
    modality_grad = own_key + sum(decode(x) for x in pieces)
    image_grad = jnp.sum(decode(eighths), axis=0)
    row_loss = lax.dynamic_slice_in_dim(row_loss, zh * rows, rows, axis=1)
    col_loss = lax.dynamic_slice_in_dim(col_loss, zx * rows, rows, axis=1)
    return (image_grad, modality_grad[None], row_loss, col_loss)


def solution(mesh):
    ny = mesh.devices.shape[0] // 2
    nzh = mesh.devices.shape[1] // 8
    names = ("y", "xh", "zh", "zl", "xl", "core")
    fine = Mesh(mesh.devices.reshape(ny, 2, nzh, 2, 2, 2), names)
    mod, rows = names[:2], names[2:]
    in_specs = (P(rows, mod), P(mod, rows, None), P(mod, None))
    out_specs = (P(rows, mod), P(mod, rows, None), P(mod, rows), P(mod, rows))
    return jax.shard_map(
        on_device, mesh=fine, in_specs=in_specs, out_specs=out_specs, check_vma=False
    )
```

```python
import functools
import jax
import jax.numpy as jnp
from jax import lax
from jax.experimental import pallas as pl
from jax.experimental.pallas import tpu as pltpu
from jax.sharding import Mesh, PartitionSpec as P

LAST = (((1,), (1,)), ((), ()))
FIRST = (((0,), (0,)), ((), ()))
F32, BF16, I16 = jnp.float32, jnp.bfloat16, jnp.int16
PAD = 16


def call(kernel, out, name, mib, **kw):
    return pl.pallas_call(
        kernel,
        out_shape=out,
        compiler_params=pltpu.CompilerParams(vmem_limit_bytes=mib * 2**20),
        cost_estimate=pl.CostEstimate(flops=1000, bytes_accessed=1000, transcendentals=0),
        name=name,
        **kw,
    )


def shape(s, t):
    return jax.ShapeDtypeStruct(s, t)


def eye(n):
    return lax.broadcasted_iota(jnp.int32, (n, n), 0) == lax.broadcasted_iota(jnp.int32, (n, n), 1)


def to_lanes(v):
    n = v.shape[0]
    parts = []
    for a in range(0, n, 128):
        w = min(128, n - a)
        parts.append(jnp.sum(jnp.where(eye(w), v[a : a + w], F32(0)), axis=0, keepdims=True))
    return jnp.concatenate(parts, axis=1)


def to_rows(v):
    n = v.shape[1]
    parts = []
    for a in range(0, n, 128):
        w = min(128, n - a)
        parts.append(jnp.sum(jnp.where(eye(w), v[:, a : a + w], F32(0)), axis=1, keepdims=True))
    return jnp.concatenate(parts, axis=0)


def power_of(x):
    top = jnp.max(jnp.abs(x), axis=0, keepdims=True)
    return jnp.ceil(jnp.log2(jnp.maximum(top, F32(1e-30)))) - 14.0


def fixed(x):
    return x.astype(jnp.int32).astype(I16)


def encode(x, ref):
    rows, cols = x.shape
    power = power_of(x)
    ref[:rows, :] = fixed(jnp.round(x * jnp.exp2(-power)))
    ref[rows:, :] = fixed(jnp.broadcast_to(power, (PAD, cols)))


def floats(c):
    return c.astype(jnp.int32).astype(F32)


def decode(c, tiles=1):
    f = floats(c)
    rows = c.shape[-2] - PAD
    n = rows // tiles
    parts = [f[..., i * n : (i + 1) * n, :] * jnp.exp2(f[..., rows + i : rows + i + 1, :]) for i in range(tiles)]
    return parts[0] if tiles == 1 else jnp.concatenate(parts, axis=-2)


def join_kernel(idx, own, beside, *refs):
    out = refs[-1]
    rows = own.shape[0]
    out[pl.ds(pl.multiple_of(idx[0] * rows, 16), rows), :] = own[...]
    out[pl.ds(pl.multiple_of((1 - idx[0]) * rows, 16), rows), :] = beside[...]


def stack_kernel(n, *refs):
    for j in range(n):
        refs[-1][j] = refs[j][...]


def stack_hold_kernel(n, *refs):
    stack_kernel(n, *refs[:n], refs[-2])
    refs[-1][...] = refs[n][...]


def scores_kernel(scale, tile, idx, *refs):
    keys, blocks, (pairs, cols, s_ref, im, rs, cs) = refs[:4], refs[4:12], refs[12:]
    y, zh, xh = idx[1], idx[2], idx[3]
    nzh, rows, width = blocks[0].shape
    n_im = im.shape[0]
    part = keys[0].shape[0]
    for k in range(4):
        for other in range(2):
            at = pl.multiple_of((lax.rem(y + 4 - k, 4) * 2 + (xh ^ other)) * width, 128)
            for j in range(nzh):
                row = pl.multiple_of(lax.rem(zh + nzh - j, nzh) * rows, 16)
                im[pl.ds(row, rows), pl.ds(at, width)] = blocks[2 * k + other][j]

    rows_of = [slice(r, r + tile) for r in range(0, n_im, tile)]
    col_top, col_sum, col_pick = [None] * 4, [None] * 4, [None] * 4
    row_state = [None] * len(rows_of)

    def online(s, state, axis):
        top = jnp.max(s, axis=axis, keepdims=True)
        if state is None:
            return top, jnp.sum(jnp.exp(s - top), axis=axis, keepdims=True)
        new = jnp.maximum(state[0], top)
        return new, state[1] * jnp.exp(state[0] - new) + jnp.sum(jnp.exp(s - new), axis=axis, keepdims=True)

    def stats(h, r):
        lanes = slice(h * part, (h + 1) * part)
        s = s_ref[rows_of[r], lanes]
        picked = jnp.where(to_rows(pairs[:, rows_of[r]]) == cols[:, lanes], s, F32(0))
        old = row_state[r]
        top, total = online(s, old and old[:2], 1)
        pick = jnp.sum(picked, axis=1, keepdims=True)
        row_state[r] = (top, total, pick if old is None else old[2] + pick)
        state = None if col_top[h] is None else (col_top[h], col_sum[h])
        col_top[h], col_sum[h] = online(s, state, 0)
        pick = jnp.sum(picked, axis=0, keepdims=True)
        col_pick[h] = pick if col_pick[h] is None else col_pick[h] + pick

    before = None
    for h, ks in enumerate(keys):
        for r in range(len(rows_of)):
            s = lax.dot_general(im[rows_of[r], :], ks[...], LAST, preferred_element_type=F32)
            s_ref[rows_of[r], h * part : (h + 1) * part] = s * scale
            if before:
                stats(*before)
            before = (h, r)
    stats(*before)
    for r, (top, total, pick) in enumerate(row_state):
        rs[0:1, rows_of[r]] = to_lanes(top + jnp.log(total))
        rs[1:2, rows_of[r]] = to_lanes(pick)
    for h in range(4):
        cs[0:1, h * part : (h + 1) * part] = col_top[h] + jnp.log(col_sum[h])
        cs[1:2, h * part : (h + 1) * part] = col_pick[h]


def merge(parts):
    top = functools.reduce(jnp.maximum, parts)
    return top + jnp.log(sum(jnp.exp(p - top) for p in parts))


def meet(x, y):
    return jnp.concatenate([merge([x[0:1], y[0:1]]), x[1:2] + y[1:2]], axis=0)


def turned(c, n):
    return jnp.concatenate([c[:, (k ^ 1) * n : ((k ^ 1) + 1) * n] for k in range(c.shape[1] // n)], axis=1)


def meet_first_kernel(c, c_other, r, r_other, c_out, r_out):
    c_out[...] = meet(c[...], turned(c_other[...], c.shape[1] // 2))
    r_out[...] = meet(r[...], r_other[...])


def meet_kernel(a, b, after, out):
    del after
    out[...] = meet(a[...], b[...])


def weights_kernel(scale, tile, idx, r0, r1, c0, c1, pairs, cols, s_ref, k0, k1, k2, k3, w_ref, own, p1, p3, o2a, o2b, rl, cl, total):
    n_im, n_ks = s_ref.shape
    keys = (k0, k1, k2, k3)
    part = n_ks // 4
    width = own.shape[1]
    cstat = meet(c0[...], turned(c1[...], part))
    lse_col = cstat[0:1]
    cl[...] = lse_col - cstat[1:2]
    rstat = meet(r0[...], r1[...])
    lse_row = rstat[0:1]
    rl[...] = lse_row - rstat[1:2]

    def weigh(a):
        rows = slice(a, a + tile)
        s = s_ref[rows, :]
        two = jnp.where(to_rows(pairs[:, rows]) == cols[...], F32(2), F32(0))
        w = jnp.exp(s - to_rows(lse_row[:, rows])) + jnp.exp(s - lse_col) - two
        w_ref[rows, :] = w.astype(BF16)

    def term(a):
        rows = slice(a, a + tile)
        x = sum(
            jnp.dot(w_ref[rows, k * part : (k + 1) * part], keys[k][...], preferred_element_type=F32) for k in range(4)
        )
        total[rows, :] = x * scale

    tiles = range(0, n_im, tile)
    weigh(0)
    for a in tiles:
        if a + tile < n_im:
            weigh(a + tile)
        term(a)
    for k, out in ((2, None), (1, p1), (3, p3), (0, own)):
        lanes = pl.ds(pl.multiple_of(lax.rem(idx[1] + k, 4) * width, 128), width)
        if k == 2:
            encode(total[: n_im // 2, lanes], o2a)
            encode(total[n_im // 2 :, lanes], o2b)
        else:
            out[...] = total[:, lanes]


def relay_kernel(p1, p3, got_a, got_b, o1, o3):
    n = p1.shape[0] // 2
    encode(jnp.concatenate([p1[:n, :] + decode(got_a[...]), p1[n:, :]], axis=0), o1)
    encode(jnp.concatenate([p3[:n, :], p3[n:, :] + decode(got_b[...])], axis=0), o3)


def key_kernel(scale, w, im, after, own, out):
    del after
    half = w.shape[1] // 2
    rows = half // 4
    other = lax.dot_general(w[:, half:], im[...], FIRST, preferred_element_type=F32) * scale
    for p in range(4):
        encode(other[p * rows : (p + 1) * rows, :], out.at[p])
    own[...] = lax.dot_general(w[:, :half], im[...], FIRST, preferred_element_type=F32) * scale


def key_sum_kernel(idx, mine, got, own, keep_x, keep_z, to_x, to_z):
    rows, d = own.shape
    n = d // 2

    def piece(k):
        p = idx[0] ^ k
        return mine[pl.ds(pl.multiple_of(p * rows, 16), rows), :] + decode(got[p])

    x, z, both = piece(1), piece(2), piece(3)
    encode(x[:, :n], to_x.at[0])
    encode(both[:, :n], to_x.at[1])
    encode(z[:, n:], to_z.at[0])
    encode(both[:, n:], to_z.at[1])
    keep_x[...] = x[:, n:]
    keep_z[...] = z[:, :n]
    own[...] = piece(0)


def key_relay_kernel(after, own, keep_x, keep_z, from_x, from_z, total, to_x, to_z):
    del after
    n = keep_x.shape[1]
    total[:, :n] = own[:, :n] + decode(from_x[0])
    total[:, n:] = own[:, n:] + decode(from_z[0])
    encode(keep_z[...] + decode(from_x[1]), to_z)
    encode(keep_x[...] + decode(from_z[1]), to_x)


def key_last_kernel(own, from_x, from_z, out):
    n = own.shape[1] // 2
    out[:, :n] = own[:, :n] + decode(from_z[...])
    out[:, n:] = own[:, n:] + decode(from_x[...])


def image_sum_kernel(idx, after, own, got1, got3, keep, to_a, to_b, total):
    del after
    zh, xh = idx[2], idx[3]
    rows, width = keep.shape[1:]
    n = own.shape[0] // rows
    total[...] = own[...] + decode(got1[...]) + decode(got3[...])

    def piece(o, j):
        row = pl.multiple_of(lax.rem(zh + j, n) * rows, 16)
        return total[pl.ds(row, rows), pl.ds(pl.multiple_of((xh ^ o) * width, 128), width)]

    encode(piece(0, 2), to_a)
    encode(piece(1, 2), to_b)
    for o in range(2):
        for at, j in enumerate((0, 1, n - 1)):
            keep[3 * o + at] = piece(o, j)


def image_relay_kernel(keep, got_a, got_b, up, down):
    encode(keep[1] + decode(got_a[...]), up.at[0])
    encode(keep[4], up.at[1])
    encode(keep[2], down.at[0])
    encode(keep[5] + decode(got_b[...]), down.at[1])


def image_twin_kernel(keep, up, down, own, to_twin):
    own[...] = keep[0] + decode(up[0]) + decode(down[0])
    encode(keep[3] + decode(up[1]) + decode(down[1]), to_twin)


def image_last_kernel(own, got, out):
    out[...] = own[...] + decode(got[...])


def shift(x, axis, n, k):
    return lax.ppermute(x, axis, [(i, (i + k) % n) for i in range(n)])


def flip(x, axis, n, d):
    return lax.ppermute(x, axis, [(i, i ^ d) for i in range(n)])


def on_device(image, modality, pair_index):
    keys = modality[0]
    rows, d = keys.shape
    width = image.shape[1]
    scale = d ** (-0.5)
    nzh = lax.axis_size("zh")
    zh, y, core = lax.axis_index("zh"), lax.axis_index("y"), lax.axis_index("core")
    zl, xl = lax.axis_index("zl"), lax.axis_index("xl")
    t = lax.axis_index(("zl", "xl", "core"))
    n_im, n_ks = nzh * rows, 8 * rows
    half = n_ks // 2
    smem = pl.BlockSpec(memory_space=pltpu.SMEM)
    vmem = pl.BlockSpec(memory_space=pltpu.VMEM)
    idx = jnp.stack([xl, y, zh, lax.axis_index("xh")]).astype(jnp.int32)

    def ring(x, axis):
        return shift(x, axis, 4, 1), shift(x, axis, 4, 3)

    a1, a3 = ring(image, "zh")
    a2 = shift(a1, "zh", 4, 1)
    twins = [flip(x, "xh", 2, 1) for x in (image, a1, a2, a3)]
    stacked = shape((4, rows, width), BF16)
    a0, held = call(
        functools.partial(stack_hold_kernel, 4), [stacked, shape((rows, d), BF16)], "stack_own", 8, in_specs=[vmem] * 5
    )(image, a1, a2, a3, keys)
    a1, a3 = ring(a0, "y")
    key_x = flip(held, "xl", 2, 1)
    key_z = flip(held, "zl", 2, 1)
    key_d = lax.ppermute(held, ("zl", "xl"), [(i, 3 - i) for i in range(4)])
    b0 = call(functools.partial(stack_kernel, 4), stacked, "stack_twin", 8, in_specs=[vmem] * 6)(*twins, a1, a3)
    b1, b3 = ring(b0, "y")
    a2, b2 = shift(a1, "y", 4, 1), shift(b3, "y", 4, 3)
    blocks = [a0, b0, a1, b1, a2, b2, a3, b3]

    def join(x, y, after, name):
        specs = [smem] + [vmem] * (2 + len(after))
        return call(join_kernel, shape((2 * rows, d), BF16), name, 12, in_specs=specs)(idx, x, y, *after)

    k0 = join(keys, key_x, [b1, b3], "join_near")
    k1 = join(key_z, key_d, [k0, a2], "join_far")
    ks = [k0, k1, flip(k0, "core", 2, 1), flip(k1, "core", 2, 1)]

    pairs = lax.dynamic_index_in_dim(pair_index.reshape(nzh, 8, rows), t, axis=1, keepdims=False)
    pairs = pairs.reshape(1, n_im).astype(F32)
    p = jnp.arange(n_ks, dtype=jnp.int32)
    block = ((zl ^ (p // (2 * rows) % 2)) * 2 + p // rows % 2) * 2 + (core ^ (p // half))
    cols = zh * n_ks + block * rows + p % rows
    cols = cols.reshape(1, n_ks).astype(F32)

    tile = min(256, n_im)
    scores, im, rs, cs = call(
        functools.partial(scores_kernel, scale, tile),
        [shape((n_im, n_ks), F32), shape((n_im, d), BF16), shape((2, n_im), F32), shape((2, n_ks), F32)],
        "scores",
        28,
        in_specs=[smem] + [vmem] * 14,
    )(idx, *ks, *blocks, pairs, cols)
    cs, rs = call(meet_first_kernel, [shape((2, n_ks), F32), shape((2, n_im), F32)], "meet", 4, in_specs=[vmem] * 4)(
        cs, flip(cs, "core", 2, 1), rs, flip(rs, "zh", 4, 1)
    )
    rs_other = flip(rs, "zh", 4, 3)
    cs = call(meet_kernel, shape((2, n_ks), F32), "meet_x", 4, in_specs=[vmem] * 3)(
        cs, flip(cs, "xl", 2, 1), rs_other
    )
    cs_other = flip(cs, "zl", 2, 1)
    outs = [shape((n_im, n_ks), BF16)] + [shape((n_im, 2 * width), F32)] * 3
    outs += [shape((n_im // 2 + PAD, 2 * width), I16)] * 2 + [shape((1, n_im), F32), shape((1, n_ks), F32)]
    weights, own, p1, p3, q2a, q2b, row_loss, col_loss = call(
        functools.partial(weights_kernel, scale, tile),
        outs,
        "weights",
        28,
        in_specs=[smem] + [vmem] * 11,
        scratch_shapes=[pltpu.VMEM((n_im, d), F32)],
    )(idx, rs, rs_other, cs, cs_other, pairs, cols, scores, *ks)
    q1, q3 = call(
        relay_kernel, [shape((n_im + PAD, 2 * width), I16)] * 2, "relay", 12, in_specs=[vmem] * 4
    )(p1, p3, shift(q2a, "y", 4, 1), shift(q2b, "y", 4, 3))
    mine, sent = call(
        functools.partial(key_kernel, scale),
        [shape((half, d), F32), shape((4, rows + PAD, d), I16)],
        "key_term",
        24,
        in_specs=[vmem] * 3,
    )(weights, im, q1)
    q1, q3 = shift(q1, "y", 4, 1), shift(q3, "y", 4, 3)
    own_key, keep_x, keep_z, to_x, to_z = call(
        key_sum_kernel,
        [shape((rows, d), F32)] + [shape((rows, d // 2), F32)] * 2 + [shape((2, rows + PAD, d // 2), I16)] * 2,
        "key_sum",
        16,
        in_specs=[smem] + [vmem] * 2,
    )(idx, mine, flip(sent, "core", 2, 1))
    from_x, from_z = flip(to_x, "xl", 2, 1), flip(to_z, "zl", 2, 1)
    coded = shape((rows + PAD, width), I16)
    coded2 = shape((2, rows + PAD, width), I16)
    keep, to_a, to_b = call(
        image_sum_kernel,
        [shape((6, rows, width), F32), coded, coded],
        "image_sum",
        12,
        in_specs=[smem] + [vmem] * 4,
        scratch_shapes=[pltpu.VMEM((n_im, 2 * width), F32)],
    )(idx, keep_z, own, q1, q3)
    up, down = call(image_relay_kernel, [coded2] * 2, "image_relay", 8, in_specs=[vmem] * 3)(
        keep, shift(to_a, "zh", 4, 1), shift(to_b, "zh", 4, 3)
    )
    own_key, to_x, to_z = call(
        key_relay_kernel,
        [shape((rows, d), F32)] + [shape((rows + PAD, d // 2), I16)] * 2,
        "key_relay",
        12,
        in_specs=[vmem] * 6,
    )(up, own_key, keep_x, keep_z, from_x, from_z)
    own, to_twin = call(image_twin_kernel, [shape((rows, width), F32), coded], "image_twin", 8, in_specs=[vmem] * 3)(
        keep, shift(up, "zh", 4, 1), shift(down, "zh", 4, 3)
    )
    modality_grad = call(key_last_kernel, shape((rows, d), F32), "key_last", 8, in_specs=[vmem] * 3)(
        own_key, flip(to_x, "xl", 2, 1), flip(to_z, "zl", 2, 1)
    )
    image_grad = call(image_last_kernel, shape((rows, width), F32), "image_last", 4, in_specs=[vmem] * 2)(
        own, flip(to_twin, "xh", 2, 1)
    )
    row_loss = lax.dynamic_slice_in_dim(row_loss, zh * rows, rows, axis=1)
    col_loss = lax.dynamic_slice_in_dim(col_loss, xl * rows, rows, axis=1)
    return (image_grad, modality_grad[None], row_loss, col_loss)


def solution(mesh):
    ny = mesh.devices.shape[0] // 2
    nzh = mesh.devices.shape[1] // 8
    names = ("y", "xh", "zh", "zl", "xl", "core")
    fine = Mesh(mesh.devices.reshape(ny, 2, nzh, 2, 2, 2), names)
    mod, rows = names[:2], names[2:]
    in_specs = (P(rows, mod), P(mod, rows, None), P(mod, None))
    out_specs = (P(rows, mod), P(mod, rows, None), P(mod, rows), P(mod, rows))
    return jax.shard_map(
        on_device, mesh=fine, in_specs=in_specs, out_specs=out_specs, check_vma=False
    )
```

```python
import functools
import jax
import jax.numpy as jnp
from jax import lax
from jax.experimental import pallas as pl
from jax.experimental.pallas import tpu as pltpu
from jax.sharding import Mesh, PartitionSpec as P

LAST = (((1,), (1,)), ((), ()))
FIRST = (((0,), (0,)), ((), ()))
F32, BF16, I16 = jnp.float32, jnp.bfloat16, jnp.int16
PAD = 16


def call(kernel, out, name, mib, **kw):
    return pl.pallas_call(
        kernel,
        out_shape=out,
        compiler_params=pltpu.CompilerParams(vmem_limit_bytes=mib * 2**20),
        cost_estimate=pl.CostEstimate(flops=1000, bytes_accessed=1000, transcendentals=0),
        name=name,
        **kw,
    )


def shape(s, t):
    return jax.ShapeDtypeStruct(s, t)


def eye(n):
    return lax.broadcasted_iota(jnp.int32, (n, n), 0) == lax.broadcasted_iota(jnp.int32, (n, n), 1)


def to_lanes(v):
    n = v.shape[0]
    parts = []
    for a in range(0, n, 128):
        w = min(128, n - a)
        parts.append(jnp.sum(jnp.where(eye(w), v[a : a + w], F32(0)), axis=0, keepdims=True))
    return jnp.concatenate(parts, axis=1)


def to_rows(v):
    n = v.shape[1]
    parts = []
    for a in range(0, n, 128):
        w = min(128, n - a)
        parts.append(jnp.sum(jnp.where(eye(w), v[:, a : a + w], F32(0)), axis=1, keepdims=True))
    return jnp.concatenate(parts, axis=0)


def power_of(x):
    top = jnp.max(jnp.abs(x), axis=0, keepdims=True)
    return jnp.ceil(jnp.log2(jnp.maximum(top, F32(1e-30)))) - 14.0


def fixed(x):
    return x.astype(jnp.int32).astype(I16)


def encode(x, ref):
    rows, cols = x.shape
    power = power_of(x)
    ref[:rows, :] = fixed(jnp.round(x * jnp.exp2(-power)))
    ref[rows:, :] = fixed(jnp.broadcast_to(power, (PAD, cols)))


def floats(c):
    return c.astype(jnp.int32).astype(F32)


def decode(c, tiles=1):
    f = floats(c)
    rows = c.shape[-2] - PAD
    n = rows // tiles
    parts = [f[..., i * n : (i + 1) * n, :] * jnp.exp2(f[..., rows + i : rows + i + 1, :]) for i in range(tiles)]
    return parts[0] if tiles == 1 else jnp.concatenate(parts, axis=-2)


def turn_left(v, n):
    lanes = v.shape[1]
    return pltpu.roll(jnp.broadcast_to(v, (8, lanes)), lax.rem(lanes - n, lanes), 1)[0:1]


def prep_kernel(pair_index, keys, pairs, cols, keys_out):
    keys_out[...] = keys[...]
    n_im, n_ks = pairs.shape[1], cols.shape[1]
    rows = n_ks // 8
    zl, xl, core = lax.axis_index("zl"), lax.axis_index("xl"), lax.axis_index("core")
    mine = turn_left(pair_index[...].astype(F32), ((zl * 2 + xl) * 2 + core) * rows)
    pairs[...] = jnp.concatenate([mine[:, a * n_ks : a * n_ks + rows] for a in range(n_im // rows)], axis=1)
    p = lax.broadcasted_iota(jnp.int32, (1, n_ks), 1)
    k = sum((p >= a * rows).astype(jnp.int32) for a in range(1, 8))
    block = ((zl ^ (k >> 1 & 1)) * 2 + (k & 1)) * 2 + (core ^ (k >> 2))
    cols[...] = (lax.axis_index("zh") * n_ks + (block - k) * rows + p).astype(F32)


def join_kernel(own, x, z, d, after_a, after_b, out):
    del after_a, after_b
    rows = own.shape[0]
    xl = lax.axis_index("xl")
    for k, (mine, beside) in enumerate(((own, x), (z, d))):
        out[pl.ds(pl.multiple_of((2 * k + xl) * rows, 16), rows), :] = mine[...]
        out[pl.ds(pl.multiple_of((2 * k + 1 - xl) * rows, 16), rows), :] = beside[...]


def hold_kernel(keys, after, out):
    del after
    out[...] = keys[...]


def turn_kernel(behind, ahead, half_a, half_b):
    n = half_a.shape[0]
    half_a[...] = behind[:n]
    half_b[...] = ahead[n:]


def scores_kernel(scale, tile, *refs):
    keys, (i0, i1, i3, ia, ib, pairs, cols, s_ref, im, rs, cs) = refs[:2], refs[2:]
    y = lax.axis_index("y")
    nzh, rows, width = ia.shape
    n_im = im.shape[0]
    part = keys[0].shape[0]

    def place(k, xh, ref, first):
        at = pl.multiple_of((lax.rem(y + 4 - k, 4) * 2 + xh) * width, 128)
        for j in range(nzh):
            im[j * rows : (j + 1) * rows, pl.ds(at, width)] = ref[first + j]

    for k, ref in ((0, i0), (1, i1), (3, i3)):
        for xh in range(2):
            place(k, xh, ref, xh * nzh)
    place(2, 0, ia, 0)
    place(2, 1, ib, 0)

    rows_of = [slice(r, r + tile) for r in range(0, n_im, tile)]
    col_top, col_sum, col_pick = [None] * 2, [None] * 2, [None] * 2
    row_state = [None] * len(rows_of)

    def online(s, state, axis):
        top = jnp.max(s, axis=axis, keepdims=True)
        if state is None:
            return top, jnp.sum(jnp.exp(s - top), axis=axis, keepdims=True)
        new = jnp.maximum(state[0], top)
        return new, state[1] * jnp.exp(state[0] - new) + jnp.sum(jnp.exp(s - new), axis=axis, keepdims=True)

    def stats(h, r):
        lanes = slice(h * part, (h + 1) * part)
        s = s_ref[rows_of[r], lanes]
        picked = jnp.where(to_rows(pairs[:, rows_of[r]]) == cols[:, lanes], s, F32(0))
        old = row_state[r]
        top, total = online(s, old and old[:2], 1)
        pick = jnp.sum(picked, axis=1, keepdims=True)
        row_state[r] = (top, total, pick if old is None else old[2] + pick)
        state = None if col_top[h] is None else (col_top[h], col_sum[h])
        col_top[h], col_sum[h] = online(s, state, 0)
        pick = jnp.sum(picked, axis=0, keepdims=True)
        col_pick[h] = pick if col_pick[h] is None else col_pick[h] + pick

    before = None
    for h, ks in enumerate(keys):
        for r in range(len(rows_of)):
            s = lax.dot_general(im[rows_of[r], :], ks[...], LAST, preferred_element_type=F32)
            s_ref[rows_of[r], h * part : (h + 1) * part] = s * scale
            if before:
                stats(*before)
            before = (h, r)
    stats(*before)
    for r, (top, total, pick) in enumerate(row_state):
        rs[0:1, rows_of[r]] = to_lanes(top + jnp.log(total))
        rs[1:2, rows_of[r]] = to_lanes(pick)
    for h in range(2):
        cs[0:1, h * part : (h + 1) * part] = col_top[h] + jnp.log(col_sum[h])
        cs[1:2, h * part : (h + 1) * part] = col_pick[h]


def merge(parts):
    top = functools.reduce(jnp.maximum, parts)
    return top + jnp.log(sum(jnp.exp(p - top) for p in parts))


def meet(parts):
    return jnp.concatenate([merge([p[0:1] for p in parts]), sum(p[1:2] for p in parts)], axis=0)


def turned(c, n):
    return jnp.concatenate([c[:, (k ^ 1) * n : ((k ^ 1) + 1) * n] for k in range(c.shape[1] // n)], axis=1)


def meet_kernel(c, c_other, out):
    out[...] = meet([c[...], turned(c_other[...], c.shape[1] // 2)])


def weights_kernel(scale, tile, *refs):
    rparts, cparts = refs[:4], refs[4:8]
    pairs, cols, s_ref, k0, k1, im, own, p1, p3, o2a, o2b, mine, sent, rl, cl, w_ref, total = refs[8:]
    n_im, n_ks = s_ref.shape
    keys = (k0, k1)
    half, part = n_ks // 2, n_ks // 4
    width = own.shape[1]
    cstat = meet([turned(c[...], part) if k >= 2 else c[...] for k, c in enumerate(cparts)])
    lse_col = cstat[0:1]
    rows = cl.shape[1]
    cl[...] = turn_left(lse_col - cstat[1:2], lax.axis_index("xl") * rows)[:, :rows]
    rstat = meet([r[...] for r in rparts])
    lse_row = rstat[0:1]
    rl[...] = turn_left(lse_row - rstat[1:2], lax.axis_index("zh") * rows)[:, :rows]

    def weigh(a):
        rows = slice(a, a + tile)
        s = s_ref[rows, :]
        two = jnp.where(to_rows(pairs[:, rows]) == cols[...], F32(2), F32(0))
        w = jnp.exp(s - to_rows(lse_row[:, rows])) + jnp.exp(s - lse_col) - two
        w_ref[rows, :] = w.astype(BF16)

    def term(a):
        rows = slice(a, a + tile)
        x = sum(
            jnp.dot(w_ref[rows, k * half : (k + 1) * half], keys[k][...], preferred_element_type=F32) for k in range(2)
        )
        total[rows, :] = x * scale

    tiles = range(0, n_im, tile)
    weigh(0)
    for a in tiles:
        if a + tile < n_im:
            weigh(a + tile)
        term(a)
    for k, out in ((2, None), (1, p1), (3, p3), (0, own)):
        lanes = pl.ds(pl.multiple_of(lax.rem(lax.axis_index("y") + k, 4) * width, 128), width)
        if k == 2:
            encode(total[: n_im // 2, lanes], o2a)
            encode(total[n_im // 2 :, lanes], o2b)
        else:
            out[...] = total[:, lanes]
    other = lax.dot_general(w_ref[:, half:], im[...], FIRST, preferred_element_type=F32) * scale
    for p in range(4):
        encode(other[p * rows : (p + 1) * rows, :], sent.at[p])
    mine[...] = lax.dot_general(w_ref[:, :half], im[...], FIRST, preferred_element_type=F32) * scale


def relay_kernel(p1, p3, got_a, got_b, o1, o3):
    n = p1.shape[0] // 2
    encode(jnp.concatenate([p1[:n, :] + decode(got_a[...]), p1[n:, :]], axis=0), o1)
    encode(jnp.concatenate([p3[:n, :], p3[n:, :] + decode(got_b[...])], axis=0), o3)


def key_sum_kernel(mine, got, own, keep_x, keep_z, to_x, to_z):
    rows, d = own.shape
    n = d // 2
    xl = lax.axis_index("xl")

    def piece(k):
        p = xl ^ k
        return mine[pl.ds(pl.multiple_of(p * rows, 16), rows), :] + decode(got[p])

    x, z, both = piece(1), piece(2), piece(3)
    encode(x[:, :n], to_x.at[0])
    encode(both[:, :n], to_x.at[1])
    encode(z[:, n:], to_z.at[0])
    encode(both[:, n:], to_z.at[1])
    keep_x[...] = x[:, n:]
    keep_z[...] = z[:, :n]
    own[...] = piece(0)


def key_relay_kernel(after, own, keep_x, keep_z, from_x, from_z, total, to_x, to_z):
    del after
    n = keep_x.shape[1]
    total[:, :n] = own[:, :n] + decode(from_x[0])
    total[:, n:] = own[:, n:] + decode(from_z[0])
    encode(keep_z[...] + decode(from_x[1]), to_z)
    encode(keep_x[...] + decode(from_z[1]), to_x)


def last_kernel(own_key, from_x, from_z, own, twin, key_out, image_out):
    n = own_key.shape[1] // 2
    key_out[:, :n] = own_key[:, :n] + decode(from_z[...])
    key_out[:, n:] = own_key[:, n:] + decode(from_x[...])
    image_out[...] = own[...] + decode(twin[...])


def image_sum_kernel(after, own, got1, got3, keep, to_a, to_b, total):
    del after
    zh, xh = lax.axis_index("zh"), lax.axis_index("xh")
    rows, width = keep.shape[1:]
    n = own.shape[0] // rows
    total[...] = own[...] + decode(got1[...]) + decode(got3[...])

    def piece(o, j):
        row = pl.multiple_of(lax.rem(zh + j, n) * rows, 16)
        return total[pl.ds(row, rows), pl.ds(pl.multiple_of((xh ^ o) * width, 128), width)]

    encode(piece(0, 2), to_a)
    encode(piece(1, 2), to_b)
    for o in range(2):
        for at, j in enumerate((0, 1, n - 1)):
            keep[3 * o + at] = piece(o, j)


def image_relay_kernel(after, keep, got_a, got_b, up, down):
    del after
    encode(keep[1] + decode(got_a[...]), up.at[0])
    encode(keep[4], up.at[1])
    encode(keep[2], down.at[0])
    encode(keep[5] + decode(got_b[...]), down.at[1])


def image_twin_kernel(keep, up, down, own, to_twin):
    own[...] = keep[0] + decode(up[0]) + decode(down[0])
    encode(keep[3] + decode(up[1]) + decode(down[1]), to_twin)


def shift(x, axis, n, k):
    return lax.ppermute(x, axis, [(i, (i + k) % n) for i in range(n)])


def flip(x, axis, n, d):
    return lax.ppermute(x, axis, [(i, i ^ d) for i in range(n)])


def on_device(image, modality, pair_index):
    keys = modality[0]
    rows, d = keys.shape
    width = image.shape[1]
    scale = d ** (-0.5)
    nzh = lax.axis_size("zh")
    n_im, n_ks = nzh * rows, 8 * rows
    half = n_ks // 2
    vmem = pl.BlockSpec(memory_space=pltpu.VMEM)
    pairs, cols, held = call(
        prep_kernel,
        [shape((1, n_im), F32), shape((1, n_ks), F32), shape((rows, d), BF16)],
        "prep",
        8,
        in_specs=[vmem] * 2,
    )(pair_index, keys)
    i0 = lax.all_to_all(jnp.broadcast_to(image, (2 * nzh, rows, width)), ("xh", "zh"), 0, 0)
    i1, i3 = shift(i0, "y", 4, 1), shift(i0, "y", 4, 3)
    held = call(hold_kernel, shape((rows, d), BF16), "hold", 8, in_specs=[vmem] * 2)(held, i0)
    key_x = flip(held, "xl", 2, 1)
    key_z = flip(held, "zl", 2, 1)
    key_d = lax.ppermute(held, ("zl", "xl"), [(i, 3 - i) for i in range(4)])
    half_block = shape((nzh, rows, width), BF16)
    ia, ib = call(turn_kernel, [half_block] * 2, "turn", 12, in_specs=[vmem] * 2)(i1, i3)
    ia, ib = shift(ia, "y", 4, 1), shift(ib, "y", 4, 3)
    k0 = call(join_kernel, shape((half, d), BF16), "join", 12, in_specs=[vmem] * 6)(held, key_x, key_z, key_d, ia, ib)
    ks = [k0, flip(k0, "core", 2, 1)]

    tile = min(256, n_im)
    scores, im, rs, cs = call(
        functools.partial(scores_kernel, scale, tile),
        [shape((n_im, n_ks), F32), shape((n_im, d), BF16), shape((2, n_im), F32), shape((2, n_ks), F32)],
        "scores",
        28,
        in_specs=[vmem] * 9,
    )(*ks, i0, i1, i3, ia, ib, pairs, cols)
    rstats = [rs] + [shift(rs, "zh", 4, k) for k in (1, 2, 3)]
    cs = call(meet_kernel, shape((2, n_ks), F32), "meet", 4, in_specs=[vmem] * 2)(cs, flip(cs, "core", 2, 1))
    cstats = [cs] + [lax.ppermute(cs, ("zl", "xl"), [(i, i ^ k) for i in range(4)]) for k in (1, 2, 3)]
    outs = [shape((n_im, 2 * width), F32)] * 3 + [shape((n_im // 2 + PAD, 2 * width), I16)] * 2
    outs += [shape((half, d), F32), shape((4, rows + PAD, d), I16)] + [shape((1, rows), F32)] * 2
    own, p1, p3, q2a, q2b, mine, sent, row_loss, col_loss = call(
        functools.partial(weights_kernel, scale, tile),
        outs,
        "weights",
        36,
        in_specs=[vmem] * 14,
        scratch_shapes=[pltpu.VMEM((n_im, n_ks), BF16), pltpu.VMEM((n_im, d), F32)],
    )(*rstats, *cstats, pairs, cols, scores, *ks, im)
    q1, q3 = call(
        relay_kernel, [shape((n_im + PAD, 2 * width), I16)] * 2, "relay", 12, in_specs=[vmem] * 4
    )(p1, p3, shift(q2a, "y", 4, 1), shift(q2b, "y", 4, 3))
    q1, q3 = shift(q1, "y", 4, 1), shift(q3, "y", 4, 3)
    own_key, keep_x, keep_z, to_x, to_z = call(
        key_sum_kernel,
        [shape((rows, d), F32)] + [shape((rows, d // 2), F32)] * 2 + [shape((2, rows + PAD, d // 2), I16)] * 2,
        "key_sum",
        16,
        in_specs=[vmem] * 2,
    )(mine, flip(sent, "core", 2, 1))
    from_x, from_z = flip(to_x, "xl", 2, 1), flip(to_z, "zl", 2, 1)
    coded = shape((rows + PAD, width), I16)
    coded2 = shape((2, rows + PAD, width), I16)
    keep, to_a, to_b = call(
        image_sum_kernel,
        [shape((6, rows, width), F32), coded, coded],
        "image_sum",
        12,
        in_specs=[vmem] * 4,
        scratch_shapes=[pltpu.VMEM((n_im, 2 * width), F32)],
    )(keep_z, own, q1, q3)
    own_key, to_x, to_z = call(
        key_relay_kernel,
        [shape((rows, d), F32)] + [shape((rows + PAD, d // 2), I16)] * 2,
        "key_relay",
        12,
        in_specs=[vmem] * 6,
    )(to_a, own_key, keep_x, keep_z, from_x, from_z)
    up, down = call(image_relay_kernel, [coded2] * 2, "image_relay", 8, in_specs=[vmem] * 4)(
        to_x, keep, shift(to_a, "zh", 4, 1), shift(to_b, "zh", 4, 3)
    )
    own, to_twin = call(image_twin_kernel, [shape((rows, width), F32), coded], "image_twin", 8, in_specs=[vmem] * 3)(
        keep, shift(up, "zh", 4, 1), shift(down, "zh", 4, 3)
    )
    modality_grad, image_grad = call(
        last_kernel, [shape((rows, d), F32), shape((rows, width), F32)], "last", 8, in_specs=[vmem] * 5
    )(own_key, flip(to_x, "xl", 2, 1), flip(to_z, "zl", 2, 1), own, flip(to_twin, "xh", 2, 1))
    return (image_grad, modality_grad[None], row_loss, col_loss)


def solution(mesh):
    ny = mesh.devices.shape[0] // 2
    nzh = mesh.devices.shape[1] // 8
    names = ("y", "xh", "zh", "zl", "xl", "core")
    fine = Mesh(mesh.devices.reshape(ny, 2, nzh, 2, 2, 2), names)
    mod, rows = names[:2], names[2:]
    in_specs = (P(rows, mod), P(mod, rows, None), P(mod, None))
    out_specs = (P(rows, mod), P(mod, rows, None), P(mod, rows), P(mod, rows))
    return jax.shard_map(
        on_device, mesh=fine, in_specs=in_specs, out_specs=out_specs, check_vma=False
    )
```

```python
import functools
import jax
import jax.numpy as jnp
from jax import lax
from jax.experimental import pallas as pl
from jax.experimental.pallas import tpu as pltpu
from jax.sharding import Mesh, PartitionSpec as P

LAST = (((1,), (1,)), ((), ()))
FIRST = (((0,), (0,)), ((), ()))
F32, BF16, I16 = jnp.float32, jnp.bfloat16, jnp.int16
PAD = 16


def call(kernel, out, name, mib, **kw):
    return pl.pallas_call(
        kernel,
        out_shape=out,
        compiler_params=pltpu.CompilerParams(vmem_limit_bytes=mib * 2**20),
        cost_estimate=pl.CostEstimate(flops=1000, bytes_accessed=1000, transcendentals=0),
        name=name,
        **kw,
    )


def shape(s, t):
    return jax.ShapeDtypeStruct(s, t)


def eye(n):
    return lax.broadcasted_iota(jnp.int32, (n, n), 0) == lax.broadcasted_iota(jnp.int32, (n, n), 1)


def to_lanes(v):
    n = v.shape[0]
    parts = []
    for a in range(0, n, 128):
        w = min(128, n - a)
        parts.append(jnp.sum(jnp.where(eye(w), v[a : a + w], F32(0)), axis=0, keepdims=True))
    return jnp.concatenate(parts, axis=1)


def to_rows(v):
    n = v.shape[1]
    parts = []
    for a in range(0, n, 128):
        w = min(128, n - a)
        parts.append(jnp.sum(jnp.where(eye(w), v[:, a : a + w], F32(0)), axis=1, keepdims=True))
    return jnp.concatenate(parts, axis=0)


def power_of(x):
    top = jnp.max(jnp.abs(x), axis=0, keepdims=True)
    return jnp.ceil(jnp.log2(jnp.maximum(top, F32(1e-30)))) - 14.0


def fixed(x):
    return x.astype(jnp.int32).astype(I16)


def encode(x, ref):
    rows, cols = x.shape
    power = power_of(x)
    ref[:rows, :] = fixed(jnp.round(x * jnp.exp2(-power)))
    ref[rows:, :] = fixed(jnp.broadcast_to(power, (PAD, cols)))


def floats(c):
    return c.astype(jnp.int32).astype(F32)


def decode(c, tiles=1):
    f = floats(c)
    rows = c.shape[-2] - PAD
    n = rows // tiles
    parts = [f[..., i * n : (i + 1) * n, :] * jnp.exp2(f[..., rows + i : rows + i + 1, :]) for i in range(tiles)]
    return parts[0] if tiles == 1 else jnp.concatenate(parts, axis=-2)


def turn_left(v, n):
    lanes = v.shape[1]
    return pltpu.roll(jnp.broadcast_to(v, (8, lanes)), lax.rem(lanes - n, lanes), 1)[0:1]


def prep_kernel(pair_index, keys, pairs, cols, keys_out):
    keys_out[...] = keys[...]
    n_im, n_ks = pairs.shape[1], cols.shape[1]
    rows = n_ks // 8
    zl, xl, core = lax.axis_index("zl"), lax.axis_index("xl"), lax.axis_index("core")
    mine = turn_left(pair_index[...].astype(F32), ((zl * 2 + xl) * 2 + core) * rows)
    pairs[...] = jnp.concatenate([mine[:, a * n_ks : a * n_ks + rows] for a in range(n_im // rows)], axis=1)
    p = lax.broadcasted_iota(jnp.int32, (1, n_ks), 1)
    k = sum((p >= a * rows).astype(jnp.int32) for a in range(1, 8))
    block = ((zl ^ (k >> 1 & 1)) * 2 + (k & 1)) * 2 + (core ^ (k >> 2))
    cols[...] = (lax.axis_index("zh") * n_ks + (block - k) * rows + p).astype(F32)


def join_kernel(own, x, z, d_top, d_low, after_a, after_b, out):
    del after_a, after_b
    rows = own.shape[0]
    xl = lax.axis_index("xl")
    for k, parts in enumerate(((own,), (x,), (z,), (d_top, d_low))):
        at = (k // 2 * 2 + (xl ^ (k % 2))) * rows
        for part in parts:
            n = part.shape[0]
            out[pl.ds(pl.multiple_of(at, 16), n), :] = part[...]
            at += n


def hold_kernel(x, z, after, z_top, x_low):
    del after
    n = z_top.shape[0]
    z_top[...] = z[:n, :]
    x_low[...] = x[n:, :]


def turn_kernel(behind, ahead, half_a, half_b):
    n = half_a.shape[0]
    half_a[...] = behind[:n]
    half_b[...] = ahead[n:]


def scores_kernel(scale, *refs):
    keys, (i0, i1, i3, ia, ib, pairs, cols, s_ref, im, rs, cs) = refs[:2], refs[2:]
    y = lax.axis_index("y")
    nzh, rows, width = ia.shape
    n_im = im.shape[0]
    part = keys[0].shape[0]

    def place(k, xh, ref, first):
        at = pl.multiple_of((lax.rem(y + 4 - k, 4) * 2 + xh) * width, 128)
        for j in range(nzh):
            im[j * rows : (j + 1) * rows, pl.ds(at, width)] = ref[first + j]

    for k, ref in ((0, i0), (1, i1), (3, i3)):
        for xh in range(2):
            place(k, xh, ref, xh * nzh)
    place(2, 0, ia, 0)
    place(2, 1, ib, 0)

    chunk = min(256, part)
    row = [None]

    def stats(c):
        s = s_ref[:, c : c + chunk]
        picked = jnp.where(targets == cols[:, c : c + chunk], s, F32(0))
        top = jnp.max(s, axis=0, keepdims=True)
        cs[0:1, c : c + chunk] = top + jnp.log(jnp.sum(jnp.exp(s - top), axis=0, keepdims=True))
        cs[1:2, c : c + chunk] = jnp.sum(picked, axis=0, keepdims=True)
        top = jnp.max(s, axis=1, keepdims=True)
        pick = jnp.sum(picked, axis=1, keepdims=True)
        if row[0] is None:
            row[0] = (top, jnp.sum(jnp.exp(s - top), axis=1, keepdims=True), pick)
        else:
            old, total, before = row[0]
            new = jnp.maximum(old, top)
            total = total * jnp.exp(old - new) + jnp.sum(jnp.exp(s - new), axis=1, keepdims=True)
            row[0] = (new, total, before + pick)

    targets = to_rows(pairs[...])
    for c in range(0, 2 * part, chunk):
        at = c % part
        s = lax.dot_general(im[...], keys[c // part][at : at + chunk, :], LAST, preferred_element_type=F32)
        s_ref[:, c : c + chunk] = s * scale
        if c:
            stats(c - chunk)
    stats(2 * part - chunk)
    top, total, pick = row[0]
    rs[0:1, :] = to_lanes(top + jnp.log(total))
    rs[1:2, :] = to_lanes(pick)


def merge(parts):
    top = functools.reduce(jnp.maximum, parts)
    return top + jnp.log(sum(jnp.exp(p - top) for p in parts))


def meet(parts):
    return jnp.concatenate([merge([p[0:1] for p in parts]), sum(p[1:2] for p in parts)], axis=0)


def turned(c, n):
    return jnp.concatenate([c[:, (k ^ 1) * n : ((k ^ 1) + 1) * n] for k in range(c.shape[1] // n)], axis=1)


def meet_kernel(c, c_other, out):
    out[...] = meet([c[...], turned(c_other[...], c.shape[1] // 2)])


def weights_kernel(scale, tile, *refs):
    rparts, cparts = refs[:4], refs[4:8]
    pairs, cols, s_ref, k0, k1, im, own, p1, p3, o2a, o2b, mine, sent, rl, cl, w_ref, total = refs[8:]
    n_im, n_ks = s_ref.shape
    keys = (k0, k1)
    half, part = n_ks // 2, n_ks // 4
    width = own.shape[1]
    cstat = meet([turned(c[...], part) if k >= 2 else c[...] for k, c in enumerate(cparts)])
    lse_col = cstat[0:1]
    rows = cl.shape[1]
    cl[...] = turn_left(lse_col - cstat[1:2], lax.axis_index("xl") * rows)[:, :rows]
    rstat = meet([r[...] for r in rparts])
    lse_row = rstat[0:1]
    rl[...] = turn_left(lse_row - rstat[1:2], lax.axis_index("zh") * rows)[:, :rows]

    def weigh(a):
        rows = slice(a, a + tile)
        s = s_ref[rows, :]
        two = jnp.where(to_rows(pairs[:, rows]) == cols[...], F32(2), F32(0))
        w = jnp.exp(s - to_rows(lse_row[:, rows])) + jnp.exp(s - lse_col) - two
        w_ref[rows, :] = w.astype(BF16)

    def term(a):
        rows = slice(a, a + tile)
        x = sum(
            jnp.dot(w_ref[rows, k * half : (k + 1) * half], keys[k][...], preferred_element_type=F32) for k in range(2)
        )
        total[rows, :] = x * scale

    tiles = range(0, n_im, tile)
    weigh(0)
    for a in tiles:
        if a + tile < n_im:
            weigh(a + tile)
        term(a)
    for k, out in ((2, None), (1, p1), (3, p3), (0, own)):
        lanes = pl.ds(pl.multiple_of(lax.rem(lax.axis_index("y") + k, 4) * width, 128), width)
        if k == 2:
            encode(total[: n_im // 2, lanes], o2a)
            encode(total[n_im // 2 :, lanes], o2b)
        else:
            out[...] = total[:, lanes]
    other = lax.dot_general(w_ref[:, half:], im[...], FIRST, preferred_element_type=F32) * scale
    for p in range(4):
        encode(other[p * rows : (p + 1) * rows, :], sent.at[p])
    mine[...] = lax.dot_general(w_ref[:, :half], im[...], FIRST, preferred_element_type=F32) * scale


def relay_kernel(p1, p3, got_a, got_b, o1, o3):
    n = p1.shape[0] // 2
    encode(jnp.concatenate([p1[:n, :] + decode(got_a[...]), p1[n:, :]], axis=0), o1)
    encode(jnp.concatenate([p3[:n, :], p3[n:, :] + decode(got_b[...])], axis=0), o3)


def key_sum_kernel(mine, got, own, keep_x, keep_z, to_x, to_z):
    rows, d = own.shape
    n = d // 2
    xl = lax.axis_index("xl")

    def piece(k):
        p = xl ^ k
        return mine[pl.ds(pl.multiple_of(p * rows, 16), rows), :] + decode(got[p])

    x, z, both = piece(1), piece(2), piece(3)
    encode(x[:, :n], to_x.at[0])
    encode(both[:, :n], to_x.at[1])
    encode(z[:, n:], to_z.at[0])
    encode(both[:, n:], to_z.at[1])
    keep_x[...] = x[:, n:]
    keep_z[...] = z[:, :n]
    own[...] = piece(0)


def key_relay_kernel(after, own, keep_x, keep_z, from_x, from_z, total, to_x, to_z):
    del after
    n = keep_x.shape[1]
    total[:, :n] = own[:, :n] + decode(from_x[0])
    total[:, n:] = own[:, n:] + decode(from_z[0])
    encode(keep_z[...] + decode(from_x[1]), to_z)
    encode(keep_x[...] + decode(from_z[1]), to_x)


def last_kernel(own_key, from_x, from_z, own, twin, key_out, image_out):
    n = own_key.shape[1] // 2
    key_out[:, :n] = own_key[:, :n] + decode(from_z[...])
    key_out[:, n:] = own_key[:, n:] + decode(from_x[...])
    image_out[...] = own[...] + decode(twin[...])


def image_sum_kernel(after, own, got1, got3, keep, to_a, to_b, total):
    del after
    zh, xh = lax.axis_index("zh"), lax.axis_index("xh")
    rows, width = keep.shape[1:]
    n = own.shape[0] // rows
    total[...] = own[...] + decode(got1[...]) + decode(got3[...])

    def piece(o, j):
        row = pl.multiple_of(lax.rem(zh + j, n) * rows, 16)
        return total[pl.ds(row, rows), pl.ds(pl.multiple_of((xh ^ o) * width, 128), width)]

    encode(piece(0, 2), to_a)
    encode(piece(1, 2), to_b)
    for o in range(2):
        for at, j in enumerate((0, 1, n - 1)):
            keep[3 * o + at] = piece(o, j)


def image_relay_kernel(after, keep, got_a, got_b, up, down):
    del after
    encode(keep[1] + decode(got_a[...]), up.at[0])
    encode(keep[4], up.at[1])
    encode(keep[2], down.at[0])
    encode(keep[5] + decode(got_b[...]), down.at[1])


def image_twin_kernel(keep, up, down, own, to_twin):
    own[...] = keep[0] + decode(up[0]) + decode(down[0])
    encode(keep[3] + decode(up[1]) + decode(down[1]), to_twin)


def shift(x, axis, n, k):
    return lax.ppermute(x, axis, [(i, (i + k) % n) for i in range(n)])


def flip(x, axis, n, d):
    return lax.ppermute(x, axis, [(i, i ^ d) for i in range(n)])


def on_device(image, modality, pair_index):
    keys = modality[0]
    rows, d = keys.shape
    width = image.shape[1]
    scale = d ** (-0.5)
    nzh = lax.axis_size("zh")
    n_im, n_ks = nzh * rows, 8 * rows
    half = n_ks // 2
    vmem = pl.BlockSpec(memory_space=pltpu.VMEM)
    pairs, cols, held = call(
        prep_kernel,
        [shape((1, n_im), F32), shape((1, n_ks), F32), shape((rows, d), BF16)],
        "prep",
        8,
        in_specs=[vmem] * 2,
    )(pair_index, keys)
    i0 = lax.all_to_all(jnp.broadcast_to(image, (2 * nzh, rows, width)), ("xh", "zh"), 0, 0)
    i1, i3 = shift(i0, "y", 4, 1), shift(i0, "y", 4, 3)
    key_x = flip(keys, "xl", 2, 1)
    key_z = flip(keys, "zl", 2, 1)
    quarter = shape((rows // 2, d), BF16)
    d_top, d_low = call(hold_kernel, [quarter] * 2, "hold", 8, in_specs=[vmem] * 3)(key_x, key_z, i0)
    d_top, d_low = flip(d_top, "xl", 2, 1), flip(d_low, "zl", 2, 1)
    half_block = shape((nzh, rows, width), BF16)
    ia, ib = call(turn_kernel, [half_block] * 2, "turn", 12, in_specs=[vmem] * 2)(i1, i3)
    ia, ib = shift(ia, "y", 4, 1), shift(ib, "y", 4, 3)
    k0 = call(join_kernel, shape((half, d), BF16), "join", 12, in_specs=[vmem] * 7)(
        held, key_x, key_z, d_top, d_low, ia, ib
    )
    ks = [k0, flip(k0, "core", 2, 1)]

    tile = min(384, n_im)
    scores, im, rs, cs = call(
        functools.partial(scores_kernel, scale),
        [shape((n_im, n_ks), F32), shape((n_im, d), BF16), shape((2, n_im), F32), shape((2, n_ks), F32)],
        "scores",
        28,
        in_specs=[vmem] * 9,
    )(*ks, i0, i1, i3, ia, ib, pairs, cols)
    rstats = [rs] + [shift(rs, "zh", 4, k) for k in (1, 2, 3)]
    cs = call(meet_kernel, shape((2, n_ks), F32), "meet", 4, in_specs=[vmem] * 2)(cs, flip(cs, "core", 2, 1))
    cstats = [cs] + [lax.ppermute(cs, ("zl", "xl"), [(i, i ^ k) for i in range(4)]) for k in (1, 2, 3)]
    outs = [shape((n_im, 2 * width), F32)] * 3 + [shape((n_im // 2 + PAD, 2 * width), I16)] * 2
    outs += [shape((half, d), F32), shape((4, rows + PAD, d), I16)] + [shape((1, rows), F32)] * 2
    own, p1, p3, q2a, q2b, mine, sent, row_loss, col_loss = call(
        functools.partial(weights_kernel, scale, tile),
        outs,
        "weights",
        36,
        in_specs=[vmem] * 14,
        scratch_shapes=[pltpu.VMEM((n_im, n_ks), BF16), pltpu.VMEM((n_im, d), F32)],
    )(*rstats, *cstats, pairs, cols, scores, *ks, im)
    q1, q3 = call(
        relay_kernel, [shape((n_im + PAD, 2 * width), I16)] * 2, "relay", 12, in_specs=[vmem] * 4
    )(p1, p3, shift(q2a, "y", 4, 1), shift(q2b, "y", 4, 3))
    q1, q3 = shift(q1, "y", 4, 1), shift(q3, "y", 4, 3)
    own_key, keep_x, keep_z, to_x, to_z = call(
        key_sum_kernel,
        [shape((rows, d), F32)] + [shape((rows, d // 2), F32)] * 2 + [shape((2, rows + PAD, d // 2), I16)] * 2,
        "key_sum",
        16,
        in_specs=[vmem] * 2,
    )(mine, flip(sent, "core", 2, 1))
    from_x, from_z = flip(to_x, "xl", 2, 1), flip(to_z, "zl", 2, 1)
    coded = shape((rows + PAD, width), I16)
    coded2 = shape((2, rows + PAD, width), I16)
    keep, to_a, to_b = call(
        image_sum_kernel,
        [shape((6, rows, width), F32), coded, coded],
        "image_sum",
        12,
        in_specs=[vmem] * 4,
        scratch_shapes=[pltpu.VMEM((n_im, 2 * width), F32)],
    )(keep_z, own, q1, q3)
    own_key, to_x, to_z = call(
        key_relay_kernel,
        [shape((rows, d), F32)] + [shape((rows + PAD, d // 2), I16)] * 2,
        "key_relay",
        12,
        in_specs=[vmem] * 6,
    )(to_a, own_key, keep_x, keep_z, from_x, from_z)
    up, down = call(image_relay_kernel, [coded2] * 2, "image_relay", 8, in_specs=[vmem] * 4)(
        to_x, keep, shift(to_a, "zh", 4, 1), shift(to_b, "zh", 4, 3)
    )
    own, to_twin = call(image_twin_kernel, [shape((rows, width), F32), coded], "image_twin", 8, in_specs=[vmem] * 3)(
        keep, shift(up, "zh", 4, 1), shift(down, "zh", 4, 3)
    )
    modality_grad, image_grad = call(
        last_kernel, [shape((rows, d), F32), shape((rows, width), F32)], "last", 8, in_specs=[vmem] * 5
    )(own_key, flip(to_x, "xl", 2, 1), flip(to_z, "zl", 2, 1), own, flip(to_twin, "xh", 2, 1))
    return (image_grad, modality_grad[None], row_loss, col_loss)


def solution(mesh):
    ny = mesh.devices.shape[0] // 2
    nzh = mesh.devices.shape[1] // 8
    names = ("y", "xh", "zh", "zl", "xl", "core")
    fine = Mesh(mesh.devices.reshape(ny, 2, nzh, 2, 2, 2), names)
    mod, rows = names[:2], names[2:]
    in_specs = (P(rows, mod), P(mod, rows, None), P(mod, None))
    out_specs = (P(rows, mod), P(mod, rows, None), P(mod, rows), P(mod, rows))
    return jax.shard_map(
        on_device, mesh=fine, in_specs=in_specs, out_specs=out_specs, check_vma=False
    )
```

```python
import functools
import jax
import jax.numpy as jnp
from jax import lax
from jax.experimental import pallas as pl
from jax.experimental.pallas import tpu as pltpu
from jax.sharding import Mesh, PartitionSpec as P

LAST = (((1,), (1,)), ((), ()))
FIRST = (((0,), (0,)), ((), ()))
F32, BF16, I16 = jnp.float32, jnp.bfloat16, jnp.int16
PAD = 16


def call(kernel, out, name, mib, **kw):
    return pl.pallas_call(
        kernel,
        out_shape=out,
        compiler_params=pltpu.CompilerParams(vmem_limit_bytes=mib * 2**20),
        cost_estimate=pl.CostEstimate(flops=1000, bytes_accessed=1000, transcendentals=0),
        name=name,
        **kw,
    )


def shape(s, t):
    return jax.ShapeDtypeStruct(s, t)


def eye(n):
    return lax.broadcasted_iota(jnp.int32, (n, n), 0) == lax.broadcasted_iota(jnp.int32, (n, n), 1)


def to_lanes(v):
    n = v.shape[0]
    parts = []
    for a in range(0, n, 128):
        w = min(128, n - a)
        parts.append(jnp.sum(jnp.where(eye(w), v[a : a + w], F32(0)), axis=0, keepdims=True))
    return jnp.concatenate(parts, axis=1)


def to_rows(v):
    n = v.shape[1]
    parts = []
    for a in range(0, n, 128):
        w = min(128, n - a)
        parts.append(jnp.sum(jnp.where(eye(w), v[:, a : a + w], F32(0)), axis=1, keepdims=True))
    return jnp.concatenate(parts, axis=0)


def power_of(x):
    top = jnp.max(jnp.abs(x), axis=0, keepdims=True)
    return jnp.ceil(jnp.log2(jnp.maximum(top, F32(1e-30)))) - 14.0


def fixed(x):
    return x.astype(jnp.int32).astype(I16)


def encode(x, ref):
    rows, cols = x.shape
    power = power_of(x)
    ref[:rows, :] = fixed(jnp.round(x * jnp.exp2(-power)))
    ref[rows:, :] = fixed(jnp.broadcast_to(power, (PAD, cols)))


def floats(c):
    return c.astype(jnp.int32).astype(F32)


def decode(c, tiles=1):
    f = floats(c)
    rows = c.shape[-2] - PAD
    n = rows // tiles
    parts = [f[..., i * n : (i + 1) * n, :] * jnp.exp2(f[..., rows + i : rows + i + 1, :]) for i in range(tiles)]
    return parts[0] if tiles == 1 else jnp.concatenate(parts, axis=-2)


def turn_left(v, n):
    lanes = v.shape[1]
    return pltpu.roll(jnp.broadcast_to(v, (8, lanes)), lax.rem(lanes - n, lanes), 1)[0:1]


def pair_kernel(image, twin, both):
    xh = lax.axis_index("xh")
    both[pl.ds(xh, 1)] = image[...][None]
    both[pl.ds(1 - xh, 1)] = twin[...][None]


def prep_kernel(pair_index, keys, pairs, cols, keys_out):
    keys_out[...] = keys[...]
    n_im, n_ks = pairs.shape[1], cols.shape[1]
    rows = n_ks // 8
    zl, xl, core = lax.axis_index("zl"), lax.axis_index("xl"), lax.axis_index("core")
    mine = turn_left(pair_index[...].astype(F32), ((zl * 2 + xl) * 2 + core) * rows)
    pairs[...] = jnp.concatenate([mine[:, a * n_ks : a * n_ks + rows] for a in range(n_im // rows)], axis=1)
    p = lax.broadcasted_iota(jnp.int32, (1, n_ks), 1)
    k = sum((p >= a * rows).astype(jnp.int32) for a in range(1, 8))
    block = ((zl ^ (k >> 1 & 1)) * 2 + (k & 1)) * 2 + (core ^ (k >> 2))
    cols[...] = (lax.axis_index("zh") * n_ks + (block - k) * rows + p).astype(F32)


def join_kernel(own, x, z, d_top, d_low, after_a, after_b, out):
    del after_a, after_b
    rows = own.shape[0]
    xl = lax.axis_index("xl")
    for k, parts in enumerate(((own,), (x,), (z,), (d_top, d_low))):
        at = (k // 2 * 2 + (xl ^ (k % 2))) * rows
        for part in parts:
            n = part.shape[0]
            out[pl.ds(pl.multiple_of(at, 16), n), :] = part[...]
            at += n


def stack_kernel(both, b1, b2, b3, keys, out, held):
    zh = lax.axis_index("zh")
    for k, ref in enumerate((both, b1, b2, b3)):
        for xh in range(2):
            out[pl.ds(4 * xh + lax.rem(zh + 4 - k, 4), 1)] = ref[xh : xh + 1]
    held[...] = keys[...]


def hold_kernel(x, z, after, z_top, x_low):
    del after
    n = z_top.shape[0]
    z_top[...] = z[:n, :]
    x_low[...] = x[n:, :]


def turn_kernel(behind, ahead, half_a, half_b):
    n = half_a.shape[0]
    half_a[...] = behind[:n]
    half_b[...] = ahead[n:]


def scores_kernel(scale, *refs):
    keys, (i0, i1, i3, ia, ib, pairs, cols, s_ref, im, rs, cs) = refs[:2], refs[2:]
    y = lax.axis_index("y")
    nzh, rows, width = ia.shape
    n_im = im.shape[0]
    part = keys[0].shape[0]

    def place(k, xh, ref, first):
        at = pl.multiple_of((lax.rem(y + 4 - k, 4) * 2 + xh) * width, 128)
        for j in range(nzh):
            im[j * rows : (j + 1) * rows, pl.ds(at, width)] = ref[first + j]

    for k, ref in ((0, i0), (1, i1), (3, i3)):
        for xh in range(2):
            place(k, xh, ref, xh * nzh)
    place(2, 0, ia, 0)
    place(2, 1, ib, 0)

    chunk = min(256, part)
    row = [None]

    def stats(c):
        s = s_ref[:, c : c + chunk]
        picked = jnp.where(targets == cols[:, c : c + chunk], s, F32(0))
        top = jnp.max(s, axis=0, keepdims=True)
        cs[0:1, c : c + chunk] = top + jnp.log(jnp.sum(jnp.exp(s - top), axis=0, keepdims=True))
        cs[1:2, c : c + chunk] = jnp.sum(picked, axis=0, keepdims=True)
        top = jnp.max(s, axis=1, keepdims=True)
        pick = jnp.sum(picked, axis=1, keepdims=True)
        if row[0] is None:
            row[0] = (top, jnp.sum(jnp.exp(s - top), axis=1, keepdims=True), pick)
        else:
            old, total, before = row[0]
            new = jnp.maximum(old, top)
            total = total * jnp.exp(old - new) + jnp.sum(jnp.exp(s - new), axis=1, keepdims=True)
            row[0] = (new, total, before + pick)

    targets = to_rows(pairs[...])
    for c in range(0, 2 * part, chunk):
        at = c % part
        s = lax.dot_general(im[...], keys[c // part][at : at + chunk, :], LAST, preferred_element_type=F32)
        s_ref[:, c : c + chunk] = s * scale
        if c:
            stats(c - chunk)
    stats(2 * part - chunk)
    top, total, pick = row[0]
    rs[0:1, :] = to_lanes(top + jnp.log(total))
    rs[1:2, :] = to_lanes(pick)


def merge(parts):
    top = functools.reduce(jnp.maximum, parts)
    return top + jnp.log(sum(jnp.exp(p - top) for p in parts))


def meet(parts):
    return jnp.concatenate([merge([p[0:1] for p in parts]), sum(p[1:2] for p in parts)], axis=0)


def turned(c, n):
    return jnp.concatenate([c[:, (k ^ 1) * n : ((k ^ 1) + 1) * n] for k in range(c.shape[1] // n)], axis=1)


def meet_kernel(c, c_other, out):
    out[...] = meet([c[...], turned(c_other[...], c.shape[1] // 2)])


def weights_kernel(scale, tile, *refs):
    rparts, cparts = refs[:4], refs[4:8]
    pairs, cols, s_ref, k0, k1, im, own, p1, p3, o2a, o2b, mine, sent, rl, cl, w_ref, total = refs[8:]
    n_im, n_ks = s_ref.shape
    keys = (k0, k1)
    half, part = n_ks // 2, n_ks // 4
    width = own.shape[1]
    cstat = meet([turned(c[...], part) if k >= 2 else c[...] for k, c in enumerate(cparts)])
    lse_col = cstat[0:1]
    rows = cl.shape[1]
    cl[...] = turn_left(lse_col - cstat[1:2], lax.axis_index("xl") * rows)[:, :rows]
    rstat = meet([r[...] for r in rparts])
    lse_row = rstat[0:1]
    rl[...] = turn_left(lse_row - rstat[1:2], lax.axis_index("zh") * rows)[:, :rows]

    def weigh(a):
        rows = slice(a, a + tile)
        s = s_ref[rows, :]
        two = jnp.where(to_rows(pairs[:, rows]) == cols[...], F32(2), F32(0))
        w = jnp.exp(s - to_rows(lse_row[:, rows])) + jnp.exp(s - lse_col) - two
        w_ref[rows, :] = w.astype(BF16)

    def term(a):
        rows = slice(a, a + tile)
        x = sum(
            jnp.dot(w_ref[rows, k * half : (k + 1) * half], keys[k][...], preferred_element_type=F32) for k in range(2)
        )
        total[rows, :] = x * scale

    tiles = range(0, n_im, tile)
    weigh(0)
    for a in tiles:
        if a + tile < n_im:
            weigh(a + tile)
        term(a)
    for k, out in ((2, None), (1, p1), (3, p3), (0, own)):
        lanes = pl.ds(pl.multiple_of(lax.rem(lax.axis_index("y") + k, 4) * width, 128), width)
        if k == 2:
            encode(total[: n_im // 2, lanes], o2a)
            encode(total[n_im // 2 :, lanes], o2b)
        else:
            out[...] = total[:, lanes]
    other = lax.dot_general(w_ref[:, half:], im[...], FIRST, preferred_element_type=F32) * scale
    for p in range(4):
        encode(other[p * rows : (p + 1) * rows, :], sent.at[p])
    mine[...] = lax.dot_general(w_ref[:, :half], im[...], FIRST, preferred_element_type=F32) * scale


def relay_kernel(p1, p3, got_a, got_b, o1, o3):
    n = p1.shape[0] // 2
    encode(jnp.concatenate([p1[:n, :] + decode(got_a[...]), p1[n:, :]], axis=0), o1)
    encode(jnp.concatenate([p3[:n, :], p3[n:, :] + decode(got_b[...])], axis=0), o3)


def key_sum_kernel(mine, got, own, *outs):
    rows = own.shape[0]
    xl = lax.axis_index("xl")
    for k in (3, 1, 2, 0):
        p = xl ^ k
        x = mine[pl.ds(pl.multiple_of(p * rows, 16), rows), :] + decode(got[p])
        if k:
            encode(x, outs[k - 1])
        else:
            own[...] = x


def last_kernel(own_key, from_x, from_z, from_both, own, twin, key_out, image_out):
    key_out[...] = own_key[...] + decode(from_x[...]) + decode(from_z[...]) + decode(from_both[...])
    image_out[...] = own[...] + decode(twin[...])


def image_sum_kernel(after_x, after_z, after_both, own, got1, got3, keep, to1, to2, to3, total):
    del after_x, after_z, after_both
    zh, xh = lax.axis_index("zh"), lax.axis_index("xh")
    rows, width = keep.shape[1:]
    total[...] = own[...] + decode(got1[...]) + decode(got3[...])
    for k, out in ((2, to2), (1, to1), (3, to3), (0, keep)):
        row = pl.multiple_of(lax.rem(zh + k, 4) * rows, 16)
        for o in range(2):
            x = total[pl.ds(row, rows), pl.ds(pl.multiple_of((xh ^ o) * width, 128), width)]
            if k:
                encode(x, out.at[o])
            else:
                out[o] = x


def image_twin_kernel(keep, got1, got2, got3, own, to_twin):
    own[...] = keep[0] + decode(got1[0]) + decode(got2[0]) + decode(got3[0])
    encode(keep[1] + decode(got1[1]) + decode(got2[1]) + decode(got3[1]), to_twin)


def shift(x, axis, n, k):
    return lax.ppermute(x, axis, [(i, (i + k) % n) for i in range(n)])


def flip(x, axis, n, d):
    return lax.ppermute(x, axis, [(i, i ^ d) for i in range(n)])


def on_device(image, modality, pair_index):
    keys = modality[0]
    rows, d = keys.shape
    width = image.shape[1]
    scale = d ** (-0.5)
    nzh = lax.axis_size("zh")
    n_im, n_ks = nzh * rows, 8 * rows
    half = n_ks // 2
    vmem = pl.BlockSpec(memory_space=pltpu.VMEM)
    key_block = shape((rows, d), BF16)
    both = call(pair_kernel, shape((2, rows, width), BF16), "pair", 4, in_specs=[vmem] * 2)(image, flip(image, "xh", 2, 1))
    pairs, cols, held = call(
        prep_kernel, [shape((1, n_im), F32), shape((1, n_ks), F32), key_block], "prep", 8, in_specs=[vmem] * 2
    )(pair_index, keys)
    i0, held = call(stack_kernel, [shape((8, rows, width), BF16), key_block], "stack", 8, in_specs=[vmem] * 5)(
        both, *[shift(both, "zh", 4, k) for k in (1, 2, 3)], held
    )
    i1, i3 = shift(i0, "y", 4, 1), shift(i0, "y", 4, 3)
    key_x = flip(held, "xl", 2, 1)
    key_z = flip(held, "zl", 2, 1)
    quarter = shape((rows // 2, d), BF16)
    d_top, d_low = call(hold_kernel, [quarter] * 2, "hold", 8, in_specs=[vmem] * 3)(key_x, key_z, i0)
    d_top, d_low = flip(d_top, "xl", 2, 1), flip(d_low, "zl", 2, 1)
    half_block = shape((nzh, rows, width), BF16)
    ia, ib = call(turn_kernel, [half_block] * 2, "turn", 12, in_specs=[vmem] * 2)(i1, i3)
    ia, ib = shift(ia, "y", 4, 1), shift(ib, "y", 4, 3)
    k0 = call(join_kernel, shape((half, d), BF16), "join", 12, in_specs=[vmem] * 7)(
        held, key_x, key_z, d_top, d_low, ia, ib
    )
    ks = [k0, flip(k0, "core", 2, 1)]

    tile = min(384, n_im)
    scores, im, rs, cs = call(
        functools.partial(scores_kernel, scale),
        [shape((n_im, n_ks), F32), shape((n_im, d), BF16), shape((2, n_im), F32), shape((2, n_ks), F32)],
        "scores",
        28,
        in_specs=[vmem] * 9,
    )(*ks, i0, i1, i3, ia, ib, pairs, cols)
    rstats = [rs] + [shift(rs, "zh", 4, k) for k in (1, 2, 3)]
    cs = call(meet_kernel, shape((2, n_ks), F32), "meet", 4, in_specs=[vmem] * 2)(cs, flip(cs, "core", 2, 1))
    cstats = [cs] + [lax.ppermute(cs, ("zl", "xl"), [(i, i ^ k) for i in range(4)]) for k in (1, 2, 3)]
    outs = [shape((n_im, 2 * width), F32)] * 3 + [shape((n_im // 2 + PAD, 2 * width), I16)] * 2
    outs += [shape((half, d), F32), shape((4, rows + PAD, d), I16)] + [shape((1, rows), F32)] * 2
    own, p1, p3, q2a, q2b, mine, sent, row_loss, col_loss = call(
        functools.partial(weights_kernel, scale, tile),
        outs,
        "weights",
        36,
        in_specs=[vmem] * 14,
        scratch_shapes=[pltpu.VMEM((n_im, n_ks), BF16), pltpu.VMEM((n_im, d), F32)],
    )(*rstats, *cstats, pairs, cols, scores, *ks, im)
    q1, q3 = call(
        relay_kernel, [shape((n_im + PAD, 2 * width), I16)] * 2, "relay", 12, in_specs=[vmem] * 4
    )(p1, p3, shift(q2a, "y", 4, 1), shift(q2b, "y", 4, 3))
    q1, q3 = shift(q1, "y", 4, 1), shift(q3, "y", 4, 3)
    own_key, to_x, to_z, to_both = call(
        key_sum_kernel,
        [shape((rows, d), F32)] + [shape((rows + PAD, d), I16)] * 3,
        "key_sum",
        16,
        in_specs=[vmem] * 2,
    )(mine, flip(sent, "core", 2, 1))
    to_both = lax.ppermute(to_both, ("zl", "xl"), [(i, 3 - i) for i in range(4)])
    pieces = [flip(to_x, "xl", 2, 1), flip(to_z, "zl", 2, 1), to_both]
    coded = shape((2, rows + PAD, width), I16)
    keep, to1, to2, to3 = call(
        image_sum_kernel,
        [shape((2, rows, width), F32), coded, coded, coded],
        "image_sum",
        12,
        in_specs=[vmem] * 6,
        scratch_shapes=[pltpu.VMEM((n_im, 2 * width), F32)],
    )(*pieces, own, q1, q3)
    to2, to1, to3 = shift(to2, "zh", 4, 2), shift(to1, "zh", 4, 1), shift(to3, "zh", 4, 3)
    own, to_twin = call(
        image_twin_kernel,
        [shape((rows, width), F32), shape((rows + PAD, width), I16)],
        "image_twin",
        8,
        in_specs=[vmem] * 4,
    )(keep, to1, to2, to3)
    modality_grad, image_grad = call(
        last_kernel, [shape((rows, d), F32), shape((rows, width), F32)], "last", 8, in_specs=[vmem] * 6
    )(own_key, *pieces, own, flip(to_twin, "xh", 2, 1))
    return (image_grad, modality_grad[None], row_loss, col_loss)


def solution(mesh):
    ny = mesh.devices.shape[0] // 2
    nzh = mesh.devices.shape[1] // 8
    names = ("y", "xh", "zh", "zl", "xl", "core")
    fine = Mesh(mesh.devices.reshape(ny, 2, nzh, 2, 2, 2), names)
    mod, rows = names[:2], names[2:]
    in_specs = (P(rows, mod), P(mod, rows, None), P(mod, None))
    out_specs = (P(rows, mod), P(mod, rows, None), P(mod, rows), P(mod, rows))
    return jax.shard_map(
        on_device, mesh=fine, in_specs=in_specs, out_specs=out_specs, check_vma=False
    )
```

```python
import functools
import jax
import jax.numpy as jnp
from jax import lax
from jax.experimental import pallas as pl
from jax.experimental.pallas import tpu as pltpu
from jax.sharding import Mesh, PartitionSpec as P

LAST = (((1,), (1,)), ((), ()))
FIRST = (((0,), (0,)), ((), ()))
F32, BF16, I16 = jnp.float32, jnp.bfloat16, jnp.int16
PAD = 16


def call(kernel, out, name, mib, **kw):
    return pl.pallas_call(
        kernel,
        out_shape=out,
        compiler_params=pltpu.CompilerParams(vmem_limit_bytes=mib * 2**20),
        cost_estimate=pl.CostEstimate(flops=1000, bytes_accessed=1000, transcendentals=0),
        name=name,
        **kw,
    )


def shape(s, t):
    return jax.ShapeDtypeStruct(s, t)


def eye(n):
    return lax.broadcasted_iota(jnp.int32, (n, n), 0) == lax.broadcasted_iota(jnp.int32, (n, n), 1)


def to_lanes(v):
    n = v.shape[0]
    parts = []
    for a in range(0, n, 128):
        w = min(128, n - a)
        parts.append(jnp.sum(jnp.where(eye(w), v[a : a + w], F32(0)), axis=0, keepdims=True))
    return jnp.concatenate(parts, axis=1)


def to_rows(v):
    n = v.shape[1]
    parts = []
    for a in range(0, n, 128):
        w = min(128, n - a)
        parts.append(jnp.sum(jnp.where(eye(w), v[:, a : a + w], F32(0)), axis=1, keepdims=True))
    return jnp.concatenate(parts, axis=0)


def power_of(x):
    top = jnp.max(jnp.abs(x), axis=0, keepdims=True)
    return jnp.ceil(jnp.log2(jnp.maximum(top, F32(1e-30)))) - 14.0


def fixed(x):
    return x.astype(jnp.int32).astype(I16)


def encode(x, ref):
    rows, cols = x.shape
    power = power_of(x)
    ref[:rows, :] = fixed(jnp.round(x * jnp.exp2(-power)))
    ref[rows:, :] = fixed(jnp.broadcast_to(power, (PAD, cols)))


def floats(c):
    return c.astype(jnp.int32).astype(F32)


def decode(c, tiles=1):
    f = floats(c)
    rows = c.shape[-2] - PAD
    n = rows // tiles
    parts = [f[..., i * n : (i + 1) * n, :] * jnp.exp2(f[..., rows + i : rows + i + 1, :]) for i in range(tiles)]
    return parts[0] if tiles == 1 else jnp.concatenate(parts, axis=-2)


def turn_left(v, n):
    lanes = v.shape[1]
    return pltpu.roll(jnp.broadcast_to(v, (8, lanes)), lax.rem(lanes - n, lanes), 1)[0:1]


def pair_kernel(image, twin, both):
    xh = lax.axis_index("xh")
    both[pl.ds(xh, 1)] = image[...][None]
    both[pl.ds(1 - xh, 1)] = twin[...][None]


def prep_kernel(pair_index, keys, pairs, cols, keys_out):
    keys_out[...] = keys[...]
    n_im, n_ks = pairs.shape[1], cols.shape[1]
    rows = n_ks // 8
    zl, xl, core = lax.axis_index("zl"), lax.axis_index("xl"), lax.axis_index("core")
    mine = turn_left(pair_index[...].astype(F32), ((zl * 2 + xl) * 2 + core) * rows)
    pairs[...] = jnp.concatenate([mine[:, a * n_ks : a * n_ks + rows] for a in range(n_im // rows)], axis=1)
    p = lax.broadcasted_iota(jnp.int32, (1, n_ks), 1)
    k = sum((p >= a * rows).astype(jnp.int32) for a in range(1, 8))
    block = ((zl ^ (k >> 1 & 1)) * 2 + (k & 1)) * 2 + (core ^ (k >> 2))
    cols[...] = (lax.axis_index("zh") * n_ks + (block - k) * rows + p).astype(F32)


def join_kernel(own, x, z, d_top, d_low, after_a, after_b, out):
    del after_a, after_b
    rows = own.shape[0]
    xl = lax.axis_index("xl")
    for k, parts in enumerate(((own,), (x,), (z,), (d_top, d_low))):
        at = (k // 2 * 2 + (xl ^ (k % 2))) * rows
        for part in parts:
            n = part.shape[0]
            out[pl.ds(pl.multiple_of(at, 16), n), :] = part[...]
            at += n


def stack_kernel(both, b1, b2, b3, keys, out, held):
    zh = lax.axis_index("zh")
    for k, ref in enumerate((both, b1, b2, b3)):
        for xh in range(2):
            out[pl.ds(4 * xh + lax.rem(zh + 4 - k, 4), 1)] = ref[xh : xh + 1]
    held[...] = keys[...]


def hold_kernel(x, z, after, z_top, x_low):
    del after
    n = z_top.shape[0]
    z_top[...] = z[:n, :]
    x_low[...] = x[n:, :]


def turn_kernel(behind, ahead, half_a, half_b):
    n = half_a.shape[0]
    half_a[...] = behind[:n]
    half_b[...] = ahead[n:]


def scores_kernel(scale, *refs):
    keys, (i0, i1, i3, ia, ib, pairs, cols, s_ref, im, rs, cs) = refs[:2], refs[2:]
    y = lax.axis_index("y")
    nzh, rows, width = ia.shape
    n_im = im.shape[0]
    part = keys[0].shape[0]

    def place(k, xh, ref, first):
        at = pl.multiple_of((lax.rem(y + 4 - k, 4) * 2 + xh) * width, 128)
        for j in range(nzh):
            im[j * rows : (j + 1) * rows, pl.ds(at, width)] = ref[first + j]

    for k, ref in ((0, i0), (1, i1), (3, i3)):
        for xh in range(2):
            place(k, xh, ref, xh * nzh)
    place(2, 0, ia, 0)
    place(2, 1, ib, 0)

    chunk = min(256, part)
    row = [None]

    def stats(c):
        s = s_ref[:, c : c + chunk]
        picked = jnp.where(targets == cols[:, c : c + chunk], s, F32(0))
        top = jnp.max(s, axis=0, keepdims=True)
        cs[0:1, c : c + chunk] = top + jnp.log(jnp.sum(jnp.exp(s - top), axis=0, keepdims=True))
        cs[1:2, c : c + chunk] = jnp.sum(picked, axis=0, keepdims=True)
        top = jnp.max(s, axis=1, keepdims=True)
        pick = jnp.sum(picked, axis=1, keepdims=True)
        if row[0] is None:
            row[0] = (top, jnp.sum(jnp.exp(s - top), axis=1, keepdims=True), pick)
        else:
            old, total, before = row[0]
            new = jnp.maximum(old, top)
            total = total * jnp.exp(old - new) + jnp.sum(jnp.exp(s - new), axis=1, keepdims=True)
            row[0] = (new, total, before + pick)

    targets = to_rows(pairs[...])
    for c in range(0, 2 * part, chunk):
        at = c % part
        s = lax.dot_general(im[...], keys[c // part][at : at + chunk, :], LAST, preferred_element_type=F32)
        s_ref[:, c : c + chunk] = s * scale
        if c:
            stats(c - chunk)
    stats(2 * part - chunk)
    top, total, pick = row[0]
    lse, pick = to_lanes(top + jnp.log(total)), to_lanes(pick)
    for k in range(rs.shape[0]):
        rs[k, 0:1, :] = lse
        rs[k, 1:2, :] = pick


def merge(parts):
    top = functools.reduce(jnp.maximum, parts)
    return top + jnp.log(sum(jnp.exp(p - top) for p in parts))


def meet(parts):
    return jnp.concatenate([merge([p[0:1] for p in parts]), sum(p[1:2] for p in parts)], axis=0)


def turned(c, n):
    return jnp.concatenate([c[:, (k ^ 1) * n : ((k ^ 1) + 1) * n] for k in range(c.shape[1] // n)], axis=1)


def meet_kernel(c, c_other, out):
    out[...] = meet([c[...], turned(c_other[...], c.shape[1] // 2)])


def weights_kernel(scale, tile, *refs):
    rparts, cparts = refs[0], refs[1:5]
    pairs, cols, s_ref, k0, k1, im, own, p1, p3, o2a, o2b, mine, sent, rl, cl, w_ref, total = refs[5:]
    n_im, n_ks = s_ref.shape
    keys = (k0, k1)
    half, part = n_ks // 2, n_ks // 4
    width = own.shape[1]
    cstat = meet([turned(c[...], part) if k >= 2 else c[...] for k, c in enumerate(cparts)])
    lse_col = cstat[0:1]
    rows = cl.shape[1]
    cl[...] = turn_left(lse_col - cstat[1:2], lax.axis_index("xl") * rows)[:, :rows]
    rstat = meet([rparts[k] for k in range(rparts.shape[0])])
    lse_row = rstat[0:1]
    rl[...] = turn_left(lse_row - rstat[1:2], lax.axis_index("zh") * rows)[:, :rows]

    def weigh(a):
        rows = slice(a, a + tile)
        s = s_ref[rows, :]
        two = jnp.where(to_rows(pairs[:, rows]) == cols[...], F32(2), F32(0))
        w = jnp.exp(s - to_rows(lse_row[:, rows])) + jnp.exp(s - lse_col) - two
        w_ref[rows, :] = w.astype(BF16)

    def term(a):
        rows = slice(a, a + tile)
        x = sum(
            jnp.dot(w_ref[rows, k * half : (k + 1) * half], keys[k][...], preferred_element_type=F32) for k in range(2)
        )
        total[rows, :] = x * scale

    tiles = range(0, n_im, tile)
    weigh(0)
    for a in tiles:
        if a + tile < n_im:
            weigh(a + tile)
        term(a)
    for k, out in ((2, None), (1, p1), (3, p3), (0, own)):
        lanes = pl.ds(pl.multiple_of(lax.rem(lax.axis_index("y") + k, 4) * width, 128), width)
        if k == 2:
            encode(total[: n_im // 2, lanes], o2a)
            encode(total[n_im // 2 :, lanes], o2b)
        else:
            out[...] = total[:, lanes]
    other = lax.dot_general(w_ref[:, half:], im[...], FIRST, preferred_element_type=F32) * scale
    for p in range(4):
        encode(other[p * rows : (p + 1) * rows, :], sent.at[p])
    mine[...] = lax.dot_general(w_ref[:, :half], im[...], FIRST, preferred_element_type=F32) * scale


def relay_kernel(p1, p3, got_a, got_b, o1, o3):
    n = p1.shape[0] // 2
    encode(jnp.concatenate([p1[:n, :] + decode(got_a[...]), p1[n:, :]], axis=0), o1)
    encode(jnp.concatenate([p3[:n, :], p3[n:, :] + decode(got_b[...])], axis=0), o3)


def key_sum_kernel(mine, got, own, *outs):
    rows = own.shape[0]
    xl = lax.axis_index("xl")
    for k in (3, 1, 2, 0):
        p = xl ^ k
        x = mine[pl.ds(pl.multiple_of(p * rows, 16), rows), :] + decode(got[p])
        if k:
            encode(x, outs[k - 1])
        else:
            own[...] = x


def last_kernel(own_key, from_x, from_z, from_both, own, twin, key_out, image_out):
    key_out[...] = own_key[...] + decode(from_x[...]) + decode(from_z[...]) + decode(from_both[...])
    image_out[...] = own[...] + decode(twin[...])


def image_sum_kernel(own, got1, got3, keep, to1, to2, to3, total):
    zh, xh = lax.axis_index("zh"), lax.axis_index("xh")
    rows, width = keep.shape[1:]
    total[...] = own[...] + decode(got1[...]) + decode(got3[...])
    for k, out in ((2, to2), (1, to1), (3, to3), (0, keep)):
        row = pl.multiple_of(lax.rem(zh + k, 4) * rows, 16)
        for o in range(2):
            x = total[pl.ds(row, rows), pl.ds(pl.multiple_of((xh ^ o) * width, 128), width)]
            if k:
                encode(x, out.at[o])
            else:
                out[o] = x


def image_twin_kernel(after_x, after_z, after_both, keep, got1, got2, got3, own, to_twin):
    del after_x, after_z, after_both
    own[...] = keep[0] + decode(got1[0]) + decode(got2[0]) + decode(got3[0])
    encode(keep[1] + decode(got1[1]) + decode(got2[1]) + decode(got3[1]), to_twin)


def shift(x, axis, n, k):
    return lax.ppermute(x, axis, [(i, (i + k) % n) for i in range(n)])


def flip(x, axis, n, d):
    return lax.ppermute(x, axis, [(i, i ^ d) for i in range(n)])


def on_device(image, modality, pair_index):
    keys = modality[0]
    rows, d = keys.shape
    width = image.shape[1]
    scale = d ** (-0.5)
    nzh = lax.axis_size("zh")
    n_im, n_ks = nzh * rows, 8 * rows
    half = n_ks // 2
    vmem = pl.BlockSpec(memory_space=pltpu.VMEM)
    key_block = shape((rows, d), BF16)
    both = call(pair_kernel, shape((2, rows, width), BF16), "pair", 4, in_specs=[vmem] * 2)(image, flip(image, "xh", 2, 1))
    pairs, cols, held = call(
        prep_kernel, [shape((1, n_im), F32), shape((1, n_ks), F32), key_block], "prep", 8, in_specs=[vmem] * 2
    )(pair_index, keys)
    i0, held = call(stack_kernel, [shape((8, rows, width), BF16), key_block], "stack", 8, in_specs=[vmem] * 5)(
        both, *[shift(both, "zh", 4, k) for k in (1, 2, 3)], held
    )
    i1, i3 = shift(i0, "y", 4, 1), shift(i0, "y", 4, 3)
    key_x = flip(held, "xl", 2, 1)
    key_z = flip(held, "zl", 2, 1)
    quarter = shape((rows // 2, d), BF16)
    d_top, d_low = call(hold_kernel, [quarter] * 2, "hold", 8, in_specs=[vmem] * 3)(key_x, key_z, i0)
    d_top, d_low = flip(d_top, "xl", 2, 1), flip(d_low, "zl", 2, 1)
    half_block = shape((nzh, rows, width), BF16)
    ia, ib = call(turn_kernel, [half_block] * 2, "turn", 12, in_specs=[vmem] * 2)(i1, i3)
    ia, ib = shift(ia, "y", 4, 1), shift(ib, "y", 4, 3)
    k0 = call(join_kernel, shape((half, d), BF16), "join", 12, in_specs=[vmem] * 7)(
        held, key_x, key_z, d_top, d_low, ia, ib
    )
    ks = [k0, flip(k0, "core", 2, 1)]

    tile = min(384, n_im)
    scores, im, rs, cs = call(
        functools.partial(scores_kernel, scale),
        [shape((n_im, n_ks), F32), shape((n_im, d), BF16), shape((nzh, 2, n_im), F32), shape((2, n_ks), F32)],
        "scores",
        28,
        in_specs=[vmem] * 9,
    )(*ks, i0, i1, i3, ia, ib, pairs, cols)
    rs = lax.all_to_all(rs, "zh", 0, 0)
    cs = call(meet_kernel, shape((2, n_ks), F32), "meet", 4, in_specs=[vmem] * 2)(cs, flip(cs, "core", 2, 1))
    cstats = [cs] + [lax.ppermute(cs, ("zl", "xl"), [(i, i ^ k) for i in range(4)]) for k in (1, 2, 3)]
    outs = [shape((n_im, 2 * width), F32)] * 3 + [shape((n_im // 2 + PAD, 2 * width), I16)] * 2
    outs += [shape((half, d), F32), shape((4, rows + PAD, d), I16)] + [shape((1, rows), F32)] * 2
    own, p1, p3, q2a, q2b, mine, sent, row_loss, col_loss = call(
        functools.partial(weights_kernel, scale, tile),
        outs,
        "weights",
        36,
        in_specs=[vmem] * 11,
        scratch_shapes=[pltpu.VMEM((n_im, n_ks), BF16), pltpu.VMEM((n_im, d), F32)],
    )(rs, *cstats, pairs, cols, scores, *ks, im)
    q1, q3 = call(
        relay_kernel, [shape((n_im + PAD, 2 * width), I16)] * 2, "relay", 12, in_specs=[vmem] * 4
    )(p1, p3, shift(q2a, "y", 4, 1), shift(q2b, "y", 4, 3))
    q1, q3 = shift(q1, "y", 4, 1), shift(q3, "y", 4, 3)
    own_key, to_x, to_z, to_both = call(
        key_sum_kernel,
        [shape((rows, d), F32)] + [shape((rows + PAD, d), I16)] * 3,
        "key_sum",
        16,
        in_specs=[vmem] * 2,
    )(mine, flip(sent, "core", 2, 1))
    to_both = lax.ppermute(to_both, ("zl", "xl"), [(i, 3 - i) for i in range(4)])
    pieces = [flip(to_x, "xl", 2, 1), flip(to_z, "zl", 2, 1), to_both]
    coded = shape((2, rows + PAD, width), I16)
    keep, to1, to2, to3 = call(
        image_sum_kernel,
        [shape((2, rows, width), F32), coded, coded, coded],
        "image_sum",
        12,
        in_specs=[vmem] * 3,
        scratch_shapes=[pltpu.VMEM((n_im, 2 * width), F32)],
    )(own, q1, q3)
    to2, to1, to3 = shift(to2, "zh", 4, 2), shift(to1, "zh", 4, 1), shift(to3, "zh", 4, 3)
    own, to_twin = call(
        image_twin_kernel,
        [shape((rows, width), F32), shape((rows + PAD, width), I16)],
        "image_twin",
        8,
        in_specs=[vmem] * 7,
    )(*pieces, keep, to1, to2, to3)
    modality_grad, image_grad = call(
        last_kernel, [shape((rows, d), F32), shape((rows, width), F32)], "last", 8, in_specs=[vmem] * 6
    )(own_key, *pieces, own, flip(to_twin, "xh", 2, 1))
    return (image_grad, modality_grad[None], row_loss, col_loss)


def solution(mesh):
    ny = mesh.devices.shape[0] // 2
    nzh = mesh.devices.shape[1] // 8
    names = ("y", "xh", "zh", "zl", "xl", "core")
    fine = Mesh(mesh.devices.reshape(ny, 2, nzh, 2, 2, 2), names)
    mod, rows = names[:2], names[2:]
    in_specs = (P(rows, mod), P(mod, rows, None), P(mod, None))
    out_specs = (P(rows, mod), P(mod, rows, None), P(mod, rows), P(mod, rows))
    return jax.shard_map(
        on_device, mesh=fine, in_specs=in_specs, out_specs=out_specs, check_vma=False
    )
```

```python
import functools
import jax
import jax.numpy as jnp
from jax import lax
from jax.experimental import pallas as pl
from jax.experimental.pallas import tpu as pltpu
from jax.sharding import Mesh, PartitionSpec as P

LAST = (((1,), (1,)), ((), ()))
FIRST = (((0,), (0,)), ((), ()))
F32, BF16, I16 = jnp.float32, jnp.bfloat16, jnp.int16
PAD = 16


def call(kernel, out, name, mib, **kw):
    return pl.pallas_call(
        kernel,
        out_shape=out,
        compiler_params=pltpu.CompilerParams(vmem_limit_bytes=mib * 2**20),
        cost_estimate=pl.CostEstimate(flops=1000, bytes_accessed=1000, transcendentals=0),
        name=name,
        **kw,
    )


def shape(s, t):
    return jax.ShapeDtypeStruct(s, t)


def eye(n):
    return lax.broadcasted_iota(jnp.int32, (n, n), 0) == lax.broadcasted_iota(jnp.int32, (n, n), 1)


def to_lanes(v):
    n = v.shape[0]
    parts = []
    for a in range(0, n, 128):
        w = min(128, n - a)
        parts.append(jnp.sum(jnp.where(eye(w), v[a : a + w], F32(0)), axis=0, keepdims=True))
    return jnp.concatenate(parts, axis=1)


def to_rows(v):
    n = v.shape[1]
    parts = []
    for a in range(0, n, 128):
        w = min(128, n - a)
        parts.append(jnp.sum(jnp.where(eye(w), v[:, a : a + w], F32(0)), axis=1, keepdims=True))
    return jnp.concatenate(parts, axis=0)


def power_of(x):
    top = jnp.max(jnp.abs(x), axis=0, keepdims=True)
    return jnp.ceil(jnp.log2(jnp.maximum(top, F32(1e-30)))) - 14.0


def fixed(x):
    return x.astype(jnp.int32).astype(I16)


def encode(x, ref):
    rows, cols = x.shape
    power = power_of(x)
    ref[:rows, :] = fixed(jnp.round(x * jnp.exp2(-power)))
    ref[rows:, :] = fixed(jnp.broadcast_to(power, (PAD, cols)))


def floats(c):
    return c.astype(jnp.int32).astype(F32)


def decode(c, tiles=1):
    f = floats(c)
    rows = c.shape[-2] - PAD
    n = rows // tiles
    parts = [f[..., i * n : (i + 1) * n, :] * jnp.exp2(f[..., rows + i : rows + i + 1, :]) for i in range(tiles)]
    return parts[0] if tiles == 1 else jnp.concatenate(parts, axis=-2)


def turn_left(v, n):
    lanes = v.shape[1]
    return pltpu.roll(jnp.broadcast_to(v, (8, lanes)), lax.rem(lanes - n, lanes), 1)[0:1]


def pair_kernel(image, twin, both):
    xh = lax.axis_index("xh")
    both[pl.ds(xh, 1)] = image[...][None]
    both[pl.ds(1 - xh, 1)] = twin[...][None]


def prep_kernel(pair_index, keys, pairs, cols, keys_out):
    keys_out[...] = keys[...]
    n_im, n_ks = pairs.shape[1], cols.shape[1]
    rows = n_ks // 8
    zl, xl, core = lax.axis_index("zl"), lax.axis_index("xl"), lax.axis_index("core")
    mine = turn_left(pair_index[...].astype(F32), ((zl * 2 + xl) * 2 + core) * rows)
    pairs[...] = jnp.concatenate([mine[:, a * n_ks : a * n_ks + rows] for a in range(n_im // rows)], axis=1)
    p = lax.broadcasted_iota(jnp.int32, (1, n_ks), 1)
    k = sum((p >= a * rows).astype(jnp.int32) for a in range(1, 8))
    block = ((zl ^ (k >> 1 & 1)) * 2 + (k & 1)) * 2 + (core ^ (k >> 2))
    cols[...] = (lax.axis_index("zh") * n_ks + (block - k) * rows + p).astype(F32)


def join_kernel(own, x, z, d_top, d_low, after_a, after_b, out):
    del after_a, after_b
    rows = own.shape[0]
    xl = lax.axis_index("xl")
    for k, parts in enumerate(((own,), (x,), (z,), (d_top, d_low))):
        at = (k // 2 * 2 + (xl ^ (k % 2))) * rows
        for part in parts:
            n = part.shape[0]
            out[pl.ds(pl.multiple_of(at, 16), n), :] = part[...]
            at += n


def copy_kernel(keys, after, out):
    del after
    out[...] = keys[...]


def stack_kernel(both, b1, b2, b3, out):
    zh = lax.axis_index("zh")
    for k, ref in enumerate((both, b1, b2, b3)):
        for xh in range(2):
            out[pl.ds(4 * xh + lax.rem(zh + 4 - k, 4), 1)] = ref[xh : xh + 1]


def hold_kernel(x, z, after, z_top, x_low):
    del after
    n = z_top.shape[0]
    z_top[...] = z[:n, :]
    x_low[...] = x[n:, :]


def turn_kernel(behind, ahead, half_a, half_b):
    n = half_a.shape[0]
    half_a[...] = behind[:n]
    half_b[...] = ahead[n:]


def scores_kernel(scale, *refs):
    keys, (i0, i1, i3, ia, ib, pairs, cols, s_ref, im, rs, cs) = refs[:2], refs[2:]
    y = lax.axis_index("y")
    nzh, rows, width = ia.shape
    n_im = im.shape[0]
    part = keys[0].shape[0]

    def place(k, xh, ref, first):
        at = pl.multiple_of((lax.rem(y + 4 - k, 4) * 2 + xh) * width, 128)
        for j in range(nzh):
            im[j * rows : (j + 1) * rows, pl.ds(at, width)] = ref[first + j]

    for k, ref in ((0, i0), (1, i1), (3, i3)):
        for xh in range(2):
            place(k, xh, ref, xh * nzh)
    place(2, 0, ia, 0)
    place(2, 1, ib, 0)

    chunk = min(256, part)
    row = [None]

    def stats(c):
        s = s_ref[:, c : c + chunk]
        picked = jnp.where(targets == cols[:, c : c + chunk], s, F32(0))
        top = jnp.max(s, axis=0, keepdims=True)
        cs[0:1, c : c + chunk] = top + jnp.log(jnp.sum(jnp.exp(s - top), axis=0, keepdims=True))
        cs[1:2, c : c + chunk] = jnp.sum(picked, axis=0, keepdims=True)
        top = jnp.max(s, axis=1, keepdims=True)
        pick = jnp.sum(picked, axis=1, keepdims=True)
        if row[0] is None:
            row[0] = (top, jnp.sum(jnp.exp(s - top), axis=1, keepdims=True), pick)
        else:
            old, total, before = row[0]
            new = jnp.maximum(old, top)
            total = total * jnp.exp(old - new) + jnp.sum(jnp.exp(s - new), axis=1, keepdims=True)
            row[0] = (new, total, before + pick)

    targets = to_rows(pairs[...])
    for c in range(0, 2 * part, chunk):
        at = c % part
        s = lax.dot_general(im[...], keys[c // part][at : at + chunk, :], LAST, preferred_element_type=F32)
        s_ref[:, c : c + chunk] = s * scale
        if c:
            stats(c - chunk)
    stats(2 * part - chunk)
    top, total, pick = row[0]
    rs[0:1, :] = to_lanes(top + jnp.log(total))
    rs[1:2, :] = to_lanes(pick)


def merge(parts):
    top = functools.reduce(jnp.maximum, parts)
    return top + jnp.log(sum(jnp.exp(p - top) for p in parts))


def meet(parts):
    return jnp.concatenate([merge([p[0:1] for p in parts]), sum(p[1:2] for p in parts)], axis=0)


def turned(c, n):
    return jnp.concatenate([c[:, (k ^ 1) * n : ((k ^ 1) + 1) * n] for k in range(c.shape[1] // n)], axis=1)


def meet_kernel(c, c_other, out):
    out[...] = meet([c[...], turned(c_other[...], c.shape[1] // 2)])


def weights_kernel(scale, tile, *refs):
    rparts, cparts = refs[:4], refs[4:8]
    pairs, cols, s_ref, k0, k1, im, own, p1, p3, o2a, o2b, mine, sent, rl, cl, w_ref, total = refs[8:]
    n_ks = s_ref.shape[1]
    keys = (k0, k1)
    half, part = n_ks // 2, n_ks // 4
    width = own.shape[1]
    cstat = meet([turned(c[...], part) if k >= 2 else c[...] for k, c in enumerate(cparts)])
    lse_col = cstat[0:1]
    rows = cl.shape[1]
    cl[...] = turn_left(lse_col - cstat[1:2], lax.axis_index("xl") * rows)[:, :rows]
    rstat = meet([r[...] for r in rparts])
    lse_row = rstat[0:1]
    rl[...] = turn_left(lse_row - rstat[1:2], lax.axis_index("zh") * rows)[:, :rows]

    lse_rows, targets = to_rows(lse_row), to_rows(pairs[...])

    def weigh(a, n):
        x = s_ref[a : a + n, :]
        two = jnp.where(targets[a : a + n] == cols[...], F32(2), F32(0))
        w = jnp.exp(x - lse_rows[a : a + n]) + jnp.exp(x - lse_col) - two
        w_ref[a : a + n, :] = w.astype(BF16)

    def term(a, f):
        lanes = slice(f * width, (f + 1) * width)
        x = sum(
            jnp.dot(
                w_ref[a : a + tile, k * half : (k + 1) * half], keys[k][:, lanes], preferred_element_type=F32
            )
            for k in range(2)
        )
        total[a : a + tile, lanes] = x * scale

    def quarter(k):
        return pl.ds(pl.multiple_of(lax.rem(lax.axis_index("y") + k, 4) * width, 128), width)

    def key_part(a):
        return lax.dot_general(w_ref[:, a : a + tile], im[...], FIRST, preferred_element_type=F32) * scale

    def send(x, first):
        for p in range(tile // rows):
            encode(x[p * rows : (p + 1) * rows, :], sent.at[first + p])

    weigh(0, tile)
    for f in range(4):
        term(0, f)
        weigh(tile + f * (tile // 4), tile // 4)
    for f in range(4):
        term(tile, f)
        if f == 0:
            encode(total[:tile, quarter(2)], o2a)
        else:
            ((own, 0), (p1, 1), (p3, 3))[f - 1][0][:tile, :] = total[:tile, quarter((0, 1, 3)[f - 1])]
    first = key_part(half)
    encode(total[tile:, quarter(2)], o2b)
    second = key_part(half + tile)
    send(first, 0)
    mine[:tile, :] = key_part(0)
    send(second, tile // rows)
    mine[tile:, :] = key_part(tile)
    for out, k in ((own, 0), (p1, 1), (p3, 3)):
        out[tile:, :] = total[tile:, quarter(k)]


def relay_kernel(p1, p3, got_a, got_b, o1, o3):
    n = p1.shape[0] // 2
    encode(jnp.concatenate([p1[:n, :] + decode(got_a[...]), p1[n:, :]], axis=0), o1)
    encode(jnp.concatenate([p3[:n, :], p3[n:, :] + decode(got_b[...])], axis=0), o3)


def key_sum_kernel(mine, got, own, *outs):
    rows = own.shape[0]
    xl = lax.axis_index("xl")
    for k in (3, 1, 2, 0):
        p = xl ^ k
        x = mine[pl.ds(pl.multiple_of(p * rows, 16), rows), :] + decode(got[p])
        if k:
            encode(x, outs[k - 1])
        else:
            own[...] = x


def last_kernel(own_key, from_x, from_z, from_both, own, twin, key_out, image_out):
    key_out[...] = own_key[...] + decode(from_x[...]) + decode(from_z[...]) + decode(from_both[...])
    image_out[...] = own[...] + decode(twin[...])


def image_sum_kernel(own, got1, got3, keep, to_a, to_b, total):
    zh, xh = lax.axis_index("zh"), lax.axis_index("xh")
    rows, width = keep.shape[1:]
    total[...] = own[...] + decode(got1[...]) + decode(got3[...])

    def piece(o, j):
        row = pl.multiple_of(lax.rem(zh + j, 4) * rows, 16)
        return total[pl.ds(row, rows), pl.ds(pl.multiple_of((xh ^ o) * width, 128), width)]

    encode(piece(0, 2), to_a)
    encode(piece(1, 2), to_b)
    for o in range(2):
        for at, j in enumerate((0, 1, 3)):
            keep[3 * o + at] = piece(o, j)


def image_relay_kernel(keep, got_a, got_b, up, down):
    encode(keep[1] + decode(got_a[...]), up.at[0])
    encode(keep[4], up.at[1])
    encode(keep[2], down.at[0])
    encode(keep[5] + decode(got_b[...]), down.at[1])


def image_twin_kernel(after_x, after_z, after_both, keep, up, down, own, to_twin):
    del after_x, after_z, after_both
    own[...] = keep[0] + decode(up[0]) + decode(down[0])
    encode(keep[3] + decode(up[1]) + decode(down[1]), to_twin)


def shift(x, axis, n, k):
    return lax.ppermute(x, axis, [(i, (i + k) % n) for i in range(n)])


def flip(x, axis, n, d):
    return lax.ppermute(x, axis, [(i, i ^ d) for i in range(n)])


def on_device(image, modality, pair_index):
    keys = modality[0]
    rows, d = keys.shape
    width = image.shape[1]
    scale = d ** (-0.5)
    nzh = lax.axis_size("zh")
    n_im, n_ks = nzh * rows, 8 * rows
    half = n_ks // 2
    vmem = pl.BlockSpec(memory_space=pltpu.VMEM)
    key_block = shape((rows, d), BF16)
    both = call(pair_kernel, shape((2, rows, width), BF16), "pair", 4, in_specs=[vmem] * 2)(image, flip(image, "xh", 2, 1))
    pairs, cols, held = call(
        prep_kernel, [shape((1, n_im), F32), shape((1, n_ks), F32), key_block], "prep", 8, in_specs=[vmem] * 2
    )(pair_index, keys)
    i0 = call(stack_kernel, shape((8, rows, width), BF16), "stack", 8, in_specs=[vmem] * 4)(
        both, *[shift(both, "zh", 4, k) for k in (1, 2, 3)]
    )
    i1, i3 = shift(i0, "y", 4, 1), shift(i0, "y", 4, 3)
    held = call(copy_kernel, key_block, "copy", 8, in_specs=[vmem] * 2)(held, i0)
    key_x = flip(held, "xl", 2, 1)
    key_z = flip(held, "zl", 2, 1)
    quarter = shape((rows // 2, d), BF16)
    d_top, d_low = call(hold_kernel, [quarter] * 2, "hold", 8, in_specs=[vmem] * 3)(key_x, key_z, i0)
    d_top, d_low = flip(d_top, "xl", 2, 1), flip(d_low, "zl", 2, 1)
    half_block = shape((nzh, rows, width), BF16)
    ia, ib = call(turn_kernel, [half_block] * 2, "turn", 12, in_specs=[vmem] * 2)(i1, i3)
    ia, ib = shift(ia, "y", 4, 1), shift(ib, "y", 4, 3)
    k0 = call(join_kernel, shape((half, d), BF16), "join", 12, in_specs=[vmem] * 7)(
        held, key_x, key_z, d_top, d_low, ia, ib
    )
    ks = [k0, flip(k0, "core", 2, 1)]

    tile = n_im // 2
    scores, im, rs, cs = call(
        functools.partial(scores_kernel, scale),
        [shape((n_im, n_ks), F32), shape((n_im, d), BF16), shape((2, n_im), F32), shape((2, n_ks), F32)],
        "scores",
        28,
        in_specs=[vmem] * 9,
    )(*ks, i0, i1, i3, ia, ib, pairs, cols)
    rstats = [rs] + [shift(rs, "zh", 4, k) for k in (1, 2, 3)]
    cs = call(meet_kernel, shape((2, n_ks), F32), "meet", 4, in_specs=[vmem] * 2)(cs, flip(cs, "core", 2, 1))
    cstats = [cs] + [lax.ppermute(cs, ("zl", "xl"), [(i, i ^ k) for i in range(4)]) for k in (1, 2, 3)]
    outs = [shape((n_im, 2 * width), F32)] * 3 + [shape((n_im // 2 + PAD, 2 * width), I16)] * 2
    outs += [shape((half, d), F32), shape((4, rows + PAD, d), I16)] + [shape((1, rows), F32)] * 2
    own, p1, p3, q2a, q2b, mine, sent, row_loss, col_loss = call(
        functools.partial(weights_kernel, scale, tile),
        outs,
        "weights",
        36,
        in_specs=[vmem] * 14,
        scratch_shapes=[pltpu.VMEM((n_im, n_ks), BF16), pltpu.VMEM((n_im, d), F32)],
    )(*rstats, *cstats, pairs, cols, scores, *ks, im)
    q1, q3 = call(
        relay_kernel, [shape((n_im + PAD, 2 * width), I16)] * 2, "relay", 12, in_specs=[vmem] * 4
    )(p1, p3, shift(q2a, "y", 4, 1), shift(q2b, "y", 4, 3))
    q1, q3 = shift(q1, "y", 4, 1), shift(q3, "y", 4, 3)
    own_key, to_x, to_z, to_both = call(
        key_sum_kernel,
        [shape((rows, d), F32)] + [shape((rows + PAD, d), I16)] * 3,
        "key_sum",
        16,
        in_specs=[vmem] * 2,
    )(mine, flip(sent, "core", 2, 1))
    to_both = lax.ppermute(to_both, ("zl", "xl"), [(i, 3 - i) for i in range(4)])
    pieces = [flip(to_x, "xl", 2, 1), flip(to_z, "zl", 2, 1), to_both]
    coded, coded2 = shape((rows + PAD, width), I16), shape((2, rows + PAD, width), I16)
    keep, to_a, to_b = call(
        image_sum_kernel,
        [shape((6, rows, width), F32), coded, coded],
        "image_sum",
        12,
        in_specs=[vmem] * 3,
        scratch_shapes=[pltpu.VMEM((n_im, 2 * width), F32)],
    )(own, q1, q3)
    up, down = call(image_relay_kernel, [coded2] * 2, "image_relay", 8, in_specs=[vmem] * 3)(
        keep, shift(to_a, "zh", 4, 1), shift(to_b, "zh", 4, 3)
    )
    own, to_twin = call(image_twin_kernel, [shape((rows, width), F32), coded], "image_twin", 8, in_specs=[vmem] * 6)(
        *pieces, keep, shift(up, "zh", 4, 1), shift(down, "zh", 4, 3)
    )
    modality_grad, image_grad = call(
        last_kernel, [shape((rows, d), F32), shape((rows, width), F32)], "last", 8, in_specs=[vmem] * 6
    )(own_key, *pieces, own, flip(to_twin, "xh", 2, 1))
    return (image_grad, modality_grad[None], row_loss, col_loss)


def solution(mesh):
    ny = mesh.devices.shape[0] // 2
    nzh = mesh.devices.shape[1] // 8
    names = ("y", "xh", "zh", "zl", "xl", "core")
    fine = Mesh(mesh.devices.reshape(ny, 2, nzh, 2, 2, 2), names)
    mod, rows = names[:2], names[2:]
    in_specs = (P(rows, mod), P(mod, rows, None), P(mod, None))
    out_specs = (P(rows, mod), P(mod, rows, None), P(mod, rows), P(mod, rows))
    return jax.shard_map(
        on_device, mesh=fine, in_specs=in_specs, out_specs=out_specs, check_vma=False
    )
```

```python
import functools
import jax
import jax.numpy as jnp
from jax import lax
from jax.experimental import pallas as pl
from jax.experimental.pallas import tpu as pltpu
from jax.sharding import Mesh, PartitionSpec as P

LAST = (((1,), (1,)), ((), ()))
FIRST = (((0,), (0,)), ((), ()))
F32, BF16, I16 = jnp.float32, jnp.bfloat16, jnp.int16
PAD = 16


def call(kernel, out, name, mib, **kw):
    return pl.pallas_call(
        kernel,
        out_shape=out,
        compiler_params=pltpu.CompilerParams(vmem_limit_bytes=mib * 2**20),
        cost_estimate=pl.CostEstimate(flops=1000, bytes_accessed=1000, transcendentals=0),
        name=name,
        **kw,
    )


def shape(s, t):
    return jax.ShapeDtypeStruct(s, t)


def eye(n):
    return lax.broadcasted_iota(jnp.int32, (n, n), 0) == lax.broadcasted_iota(jnp.int32, (n, n), 1)


def to_lanes(v):
    n = v.shape[0]
    parts = []
    for a in range(0, n, 128):
        w = min(128, n - a)
        parts.append(jnp.sum(jnp.where(eye(w), v[a : a + w], F32(0)), axis=0, keepdims=True))
    return jnp.concatenate(parts, axis=1)


def to_rows(v):
    n = v.shape[1]
    parts = []
    for a in range(0, n, 128):
        w = min(128, n - a)
        parts.append(jnp.sum(jnp.where(eye(w), v[:, a : a + w], F32(0)), axis=1, keepdims=True))
    return jnp.concatenate(parts, axis=0)


def power_of(x):
    top = jnp.max(jnp.abs(x), axis=0, keepdims=True)
    return jnp.ceil(jnp.log2(jnp.maximum(top, F32(1e-30)))) - 14.0


def fixed(x):
    return x.astype(jnp.int32).astype(I16)


def encode(x, ref):
    rows, cols = x.shape
    power = power_of(x)
    ref[:rows, :] = fixed(jnp.round(x * jnp.exp2(-power)))
    ref[rows:, :] = fixed(jnp.broadcast_to(power, (PAD, cols)))


def floats(c):
    return c.astype(jnp.int32).astype(F32)


def decode(c, tiles=1):
    f = floats(c)
    rows = c.shape[-2] - PAD
    n = rows // tiles
    parts = [f[..., i * n : (i + 1) * n, :] * jnp.exp2(f[..., rows + i : rows + i + 1, :]) for i in range(tiles)]
    return parts[0] if tiles == 1 else jnp.concatenate(parts, axis=-2)


def turn_left(v, n):
    lanes = v.shape[1]
    return pltpu.roll(jnp.broadcast_to(v, (8, lanes)), lax.rem(lanes - n, lanes), 1)[0:1]


def pair_kernel(image, twin, both):
    xh = lax.axis_index("xh")
    both[pl.ds(xh, 1)] = image[...][None]
    both[pl.ds(1 - xh, 1)] = twin[...][None]


def prep_kernel(pair_index, keys, pairs, cols, keys_out):
    keys_out[...] = keys[...]
    n_im, n_ks = pairs.shape[1], cols.shape[1]
    rows = n_ks // 8
    zl, xl, core = lax.axis_index("zl"), lax.axis_index("xl"), lax.axis_index("core")
    mine = turn_left(pair_index[...].astype(F32), ((zl * 2 + xl) * 2 + core) * rows)
    pairs[...] = jnp.concatenate([mine[:, a * n_ks : a * n_ks + rows] for a in range(n_im // rows)], axis=1)
    p = lax.broadcasted_iota(jnp.int32, (1, n_ks), 1)
    k = sum((p >= a * rows).astype(jnp.int32) for a in range(1, 8))
    block = ((zl ^ (k >> 1 & 1)) * 2 + (k & 1)) * 2 + (core ^ (k >> 2))
    cols[...] = (lax.axis_index("zh") * n_ks + (block - k) * rows + p).astype(F32)


def join_kernel(own, x, z, d_top, d_low, after_a, after_b, out):
    del after_a, after_b
    rows = own.shape[0]
    xl = lax.axis_index("xl")
    for k, parts in enumerate(((own,), (x,), (z,), (d_top, d_low))):
        at = (k // 2 * 2 + (xl ^ (k % 2))) * rows
        for part in parts:
            n = part.shape[0]
            out[pl.ds(pl.multiple_of(at, 16), n), :] = part[...]
            at += n


def copy_kernel(keys, after, out):
    del after
    out[...] = keys[...]


def stack_kernel(both, b1, b2, b3, after, out):
    del after
    zh = lax.axis_index("zh")
    for k, ref in enumerate((both, b1, b2, b3)):
        for xh in range(2):
            out[pl.ds(4 * xh + lax.rem(zh + 4 - k, 4), 1)] = ref[xh : xh + 1]


def hold_kernel(x, z, after, z_top, x_low):
    del after
    n = z_top.shape[0]
    z_top[...] = z[:n, :]
    x_low[...] = x[n:, :]


def turn_kernel(behind, ahead, half_a, half_b):
    n = half_a.shape[0]
    half_a[...] = behind[:n]
    half_b[...] = ahead[n:]


def scores_kernel(scale, *refs):
    keys, (i0, i1, i3, ia, ib, pairs, cols, s_ref, im, rs, cs) = refs[:2], refs[2:]
    y = lax.axis_index("y")
    nzh, rows, width = ia.shape
    n_im = im.shape[0]
    part = keys[0].shape[0]

    def place(k, xh, ref, first):
        at = pl.multiple_of((lax.rem(y + 4 - k, 4) * 2 + xh) * width, 128)
        for j in range(nzh):
            im[j * rows : (j + 1) * rows, pl.ds(at, width)] = ref[first + j]

    for k, ref in ((0, i0), (1, i1), (3, i3)):
        for xh in range(2):
            place(k, xh, ref, xh * nzh)
    place(2, 0, ia, 0)
    place(2, 1, ib, 0)

    chunk = min(256, part)
    row = [None]

    def stats(c):
        s = s_ref[:, c : c + chunk]
        picked = jnp.where(targets == cols[:, c : c + chunk], s, F32(0))
        top = jnp.max(s, axis=0, keepdims=True)
        cs[0:1, c : c + chunk] = top + jnp.log(jnp.sum(jnp.exp(s - top), axis=0, keepdims=True))
        cs[1:2, c : c + chunk] = jnp.sum(picked, axis=0, keepdims=True)
        top = jnp.max(s, axis=1, keepdims=True)
        pick = jnp.sum(picked, axis=1, keepdims=True)
        if row[0] is None:
            row[0] = (top, jnp.sum(jnp.exp(s - top), axis=1, keepdims=True), pick)
        else:
            old, total, before = row[0]
            new = jnp.maximum(old, top)
            total = total * jnp.exp(old - new) + jnp.sum(jnp.exp(s - new), axis=1, keepdims=True)
            row[0] = (new, total, before + pick)

    targets = to_rows(pairs[...])
    for c in range(0, 2 * part, chunk):
        at = c % part
        s = lax.dot_general(im[...], keys[c // part][at : at + chunk, :], LAST, preferred_element_type=F32)
        s_ref[:, c : c + chunk] = s * scale
        if c:
            stats(c - chunk)
    stats(2 * part - chunk)
    top, total, pick = row[0]
    rs[0:1, :] = to_lanes(top + jnp.log(total))
    rs[1:2, :] = to_lanes(pick)


def merge(parts):
    top = functools.reduce(jnp.maximum, parts)
    return top + jnp.log(sum(jnp.exp(p - top) for p in parts))


def meet(parts):
    return jnp.concatenate([merge([p[0:1] for p in parts]), sum(p[1:2] for p in parts)], axis=0)


def turned(c, n):
    return jnp.concatenate([c[:, (k ^ 1) * n : ((k ^ 1) + 1) * n] for k in range(c.shape[1] // n)], axis=1)


def meet_kernel(c, c_other, out):
    out[...] = meet([c[...], turned(c_other[...], c.shape[1] // 2)])


def weights_kernel(scale, tile, *refs):
    rparts, cparts = refs[:4], refs[4:8]
    pairs, cols, s_ref, k0, k1, im, own, p1, p3, o2a, o2b, mine, sent, rl, cl, w_ref, total = refs[8:]
    n_im, n_ks = s_ref.shape
    keys = (k0, k1)
    half, part = n_ks // 2, n_ks // 4
    width = own.shape[1]
    cstat = meet([turned(c[...], part) if k >= 2 else c[...] for k, c in enumerate(cparts)])
    lse_col = cstat[0:1]
    rows = cl.shape[1]
    cl[...] = turn_left(lse_col - cstat[1:2], lax.axis_index("xl") * rows)[:, :rows]
    rstat = meet([r[...] for r in rparts])
    lse_row = rstat[0:1]
    rl[...] = turn_left(lse_row - rstat[1:2], lax.axis_index("zh") * rows)[:, :rows]

    def weigh(a):
        rows = slice(a, a + tile)
        s = s_ref[rows, :]
        two = jnp.where(to_rows(pairs[:, rows]) == cols[...], F32(2), F32(0))
        w = jnp.exp(s - to_rows(lse_row[:, rows])) + jnp.exp(s - lse_col) - two
        w_ref[rows, :] = w.astype(BF16)

    def term(a):
        rows = slice(a, a + tile)
        x = sum(
            jnp.dot(w_ref[rows, k * half : (k + 1) * half], keys[k][...], preferred_element_type=F32) for k in range(2)
        )
        total[rows, :] = x * scale

    tiles = range(0, n_im, tile)
    weigh(0)
    for a in tiles:
        if a + tile < n_im:
            weigh(a + tile)
        term(a)
    for k, out in ((2, None), (1, p1), (3, p3), (0, own)):
        lanes = pl.ds(pl.multiple_of(lax.rem(lax.axis_index("y") + k, 4) * width, 128), width)
        if k == 2:
            encode(total[: n_im // 2, lanes], o2a)
            encode(total[n_im // 2 :, lanes], o2b)
        else:
            out[...] = total[:, lanes]
    other = lax.dot_general(w_ref[:, half:], im[...], FIRST, preferred_element_type=F32) * scale
    for p in range(4):
        encode(other[p * rows : (p + 1) * rows, :], sent.at[p])
    mine[...] = lax.dot_general(w_ref[:, :half], im[...], FIRST, preferred_element_type=F32) * scale


def relay_kernel(after, p1, p3, got_a, got_b, o1, o3):
    del after
    n = p1.shape[0] // 2
    encode(jnp.concatenate([p1[:n, :] + decode(got_a[...]), p1[n:, :]], axis=0), o1)
    encode(jnp.concatenate([p3[:n, :], p3[n:, :] + decode(got_b[...])], axis=0), o3)


def key_sum_kernel(mine, got, own, *outs):
    rows = own.shape[0]
    xl = lax.axis_index("xl")
    for k in (3, 1, 2, 0):
        p = xl ^ k
        x = mine[pl.ds(pl.multiple_of(p * rows, 16), rows), :] + decode(got[p])
        if k:
            encode(x, outs[k - 1])
        else:
            own[...] = x


def last_kernel(own_key, from_x, from_z, from_both, own, twin, key_out, image_out):
    key_out[...] = own_key[...] + decode(from_x[...]) + decode(from_z[...]) + decode(from_both[...])
    image_out[...] = own[...] + decode(twin[...])


def image_sum_kernel(after_x, after_z, own, got1, got3, keep, to_a, to_b, total):
    del after_x, after_z
    zh, xh = lax.axis_index("zh"), lax.axis_index("xh")
    rows, width = keep.shape[1:]
    total[...] = own[...] + decode(got1[...]) + decode(got3[...])

    def piece(o, j):
        row = pl.multiple_of(lax.rem(zh + j, 4) * rows, 16)
        return total[pl.ds(row, rows), pl.ds(pl.multiple_of((xh ^ o) * width, 128), width)]

    encode(piece(0, 2), to_a)
    encode(piece(1, 2), to_b)
    for o in range(2):
        for at, j in enumerate((0, 1, 3)):
            keep[3 * o + at] = piece(o, j)


def image_relay_kernel(keep, got_a, got_b, up, down):
    encode(keep[1] + decode(got_a[...]), up.at[0])
    encode(keep[4], up.at[1])
    encode(keep[2], down.at[0])
    encode(keep[5] + decode(got_b[...]), down.at[1])


def image_twin_kernel(after, keep, up, down, own, to_twin):
    del after
    own[...] = keep[0] + decode(up[0]) + decode(down[0])
    encode(keep[3] + decode(up[1]) + decode(down[1]), to_twin)


def shift(x, axis, n, k):
    return lax.ppermute(x, axis, [(i, (i + k) % n) for i in range(n)])


def flip(x, axis, n, d):
    return lax.ppermute(x, axis, [(i, i ^ d) for i in range(n)])


def on_device(image, modality, pair_index):
    keys = modality[0]
    rows, d = keys.shape
    width = image.shape[1]
    scale = d ** (-0.5)
    nzh = lax.axis_size("zh")
    n_im, n_ks = nzh * rows, 8 * rows
    half = n_ks // 2
    vmem = pl.BlockSpec(memory_space=pltpu.VMEM)
    key_block = shape((rows, d), BF16)
    both = call(pair_kernel, shape((2, rows, width), BF16), "pair", 4, in_specs=[vmem] * 2)(image, flip(image, "xh", 2, 1))
    pairs, cols, held = call(
        prep_kernel, [shape((1, n_im), F32), shape((1, n_ks), F32), key_block], "prep", 8, in_specs=[vmem] * 2
    )(pair_index, keys)
    i0 = call(stack_kernel, shape((8, rows, width), BF16), "stack", 8, in_specs=[vmem] * 5)(
        both, *[shift(both, "zh", 4, k) for k in (1, 2, 3)], pairs
    )
    i1, i3 = shift(i0, "y", 4, 1), shift(i0, "y", 4, 3)
    held = call(copy_kernel, key_block, "copy", 8, in_specs=[vmem] * 2)(held, i0)
    key_x = flip(held, "xl", 2, 1)
    key_z = flip(held, "zl", 2, 1)
    quarter = shape((rows // 2, d), BF16)
    d_top, d_low = call(hold_kernel, [quarter] * 2, "hold", 8, in_specs=[vmem] * 3)(key_x, key_z, i0)
    d_top, d_low = flip(d_top, "xl", 2, 1), flip(d_low, "zl", 2, 1)
    half_block = shape((nzh, rows, width), BF16)
    ia, ib = call(turn_kernel, [half_block] * 2, "turn", 12, in_specs=[vmem] * 2)(i1, i3)
    ia, ib = shift(ia, "y", 4, 1), shift(ib, "y", 4, 3)
    k0 = call(join_kernel, shape((half, d), BF16), "join", 12, in_specs=[vmem] * 7)(
        held, key_x, key_z, d_top, d_low, ia, ib
    )
    ks = [k0, flip(k0, "core", 2, 1)]

    tile = min(384, n_im)
    scores, im, rs, cs = call(
        functools.partial(scores_kernel, scale),
        [shape((n_im, n_ks), F32), shape((n_im, d), BF16), shape((2, n_im), F32), shape((2, n_ks), F32)],
        "scores",
        28,
        in_specs=[vmem] * 9,
    )(*ks, i0, i1, i3, ia, ib, pairs, cols)
    rstats = [rs] + [shift(rs, "zh", 4, k) for k in (1, 2, 3)]
    cs = call(meet_kernel, shape((2, n_ks), F32), "meet", 4, in_specs=[vmem] * 2)(cs, flip(cs, "core", 2, 1))
    cstats = [cs] + [lax.ppermute(cs, ("zl", "xl"), [(i, i ^ k) for i in range(4)]) for k in (1, 2, 3)]
    outs = [shape((n_im, 2 * width), F32)] * 3 + [shape((n_im // 2 + PAD, 2 * width), I16)] * 2
    outs += [shape((half, d), F32), shape((4, rows + PAD, d), I16)] + [shape((1, rows), F32)] * 2
    own, p1, p3, q2a, q2b, mine, sent, row_loss, col_loss = call(
        functools.partial(weights_kernel, scale, tile),
        outs,
        "weights",
        36,
        in_specs=[vmem] * 14,
        scratch_shapes=[pltpu.VMEM((n_im, n_ks), BF16), pltpu.VMEM((n_im, d), F32)],
    )(*rstats, *cstats, pairs, cols, scores, *ks, im)
    own_key, to_x, to_z, to_both = call(
        key_sum_kernel,
        [shape((rows, d), F32)] + [shape((rows + PAD, d), I16)] * 3,
        "key_sum",
        16,
        in_specs=[vmem] * 2,
    )(mine, flip(sent, "core", 2, 1))
    to_both = lax.ppermute(to_both, ("zl", "xl"), [(i, 3 - i) for i in range(4)])
    pieces = [flip(to_x, "xl", 2, 1), flip(to_z, "zl", 2, 1), to_both]
    q1, q3 = call(
        relay_kernel, [shape((n_im + PAD, 2 * width), I16)] * 2, "relay", 12, in_specs=[vmem] * 5
    )(own_key, p1, p3, shift(q2a, "y", 4, 1), shift(q2b, "y", 4, 3))
    q1, q3 = shift(q1, "y", 4, 1), shift(q3, "y", 4, 3)
    coded, coded2 = shape((rows + PAD, width), I16), shape((2, rows + PAD, width), I16)
    keep, to_a, to_b = call(
        image_sum_kernel,
        [shape((6, rows, width), F32), coded, coded],
        "image_sum",
        12,
        in_specs=[vmem] * 5,
        scratch_shapes=[pltpu.VMEM((n_im, 2 * width), F32)],
    )(*pieces[:2], own, q1, q3)
    up, down = call(image_relay_kernel, [coded2] * 2, "image_relay", 8, in_specs=[vmem] * 3)(
        keep, shift(to_a, "zh", 4, 1), shift(to_b, "zh", 4, 3)
    )
    own, to_twin = call(image_twin_kernel, [shape((rows, width), F32), coded], "image_twin", 8, in_specs=[vmem] * 4)(
        pieces[2], keep, shift(up, "zh", 4, 1), shift(down, "zh", 4, 3)
    )
    modality_grad, image_grad = call(
        last_kernel, [shape((rows, d), F32), shape((rows, width), F32)], "last", 8, in_specs=[vmem] * 6
    )(own_key, *pieces, own, flip(to_twin, "xh", 2, 1))
    return (image_grad, modality_grad[None], row_loss, col_loss)


def solution(mesh):
    ny = mesh.devices.shape[0] // 2
    nzh = mesh.devices.shape[1] // 8
    names = ("y", "xh", "zh", "zl", "xl", "core")
    fine = Mesh(mesh.devices.reshape(ny, 2, nzh, 2, 2, 2), names)
    mod, rows = names[:2], names[2:]
    in_specs = (P(rows, mod), P(mod, rows, None), P(mod, None))
    out_specs = (P(rows, mod), P(mod, rows, None), P(mod, rows), P(mod, rows))
    return jax.shard_map(
        on_device, mesh=fine, in_specs=in_specs, out_specs=out_specs, check_vma=False
    )
```

```python
import functools
import jax
import jax.numpy as jnp
from jax import lax
from jax.experimental import pallas as pl
from jax.experimental.pallas import tpu as pltpu
from jax.sharding import Mesh, PartitionSpec as P

LAST = (((1,), (1,)), ((), ()))
FIRST = (((0,), (0,)), ((), ()))
F32, BF16, I16 = jnp.float32, jnp.bfloat16, jnp.int16
PAD = 16


def call(kernel, out, name, mib, **kw):
    return pl.pallas_call(
        kernel,
        out_shape=out,
        compiler_params=pltpu.CompilerParams(vmem_limit_bytes=mib * 2**20),
        cost_estimate=pl.CostEstimate(flops=1000, bytes_accessed=1000, transcendentals=0),
        name=name,
        **kw,
    )


def shape(s, t):
    return jax.ShapeDtypeStruct(s, t)


def eye(n):
    return lax.broadcasted_iota(jnp.int32, (n, n), 0) == lax.broadcasted_iota(jnp.int32, (n, n), 1)


def to_lanes(v):
    n = v.shape[0]
    parts = []
    for a in range(0, n, 128):
        w = min(128, n - a)
        parts.append(jnp.sum(jnp.where(eye(w), v[a : a + w], F32(0)), axis=0, keepdims=True))
    return jnp.concatenate(parts, axis=1)


def to_rows(v):
    n = v.shape[1]
    parts = []
    for a in range(0, n, 128):
        w = min(128, n - a)
        parts.append(jnp.sum(jnp.where(eye(w), v[:, a : a + w], F32(0)), axis=1, keepdims=True))
    return jnp.concatenate(parts, axis=0)


def power_of(x):
    top = jnp.max(jnp.abs(x), axis=0, keepdims=True)
    return jnp.ceil(jnp.log2(jnp.maximum(top, F32(1e-30)))) - 14.0


def fixed(x):
    return x.astype(jnp.int32).astype(I16)


def encode(x, ref):
    rows, cols = x.shape
    power = power_of(x)
    ref[:rows, :] = fixed(jnp.round(x * jnp.exp2(-power)))
    ref[rows:, :] = fixed(jnp.broadcast_to(power, (PAD, cols)))


def floats(c):
    return c.astype(jnp.int32).astype(F32)


def decode(c, tiles=1):
    f = floats(c)
    rows = c.shape[-2] - PAD
    n = rows // tiles
    parts = [f[..., i * n : (i + 1) * n, :] * jnp.exp2(f[..., rows + i : rows + i + 1, :]) for i in range(tiles)]
    return parts[0] if tiles == 1 else jnp.concatenate(parts, axis=-2)


def turn_left(v, n):
    lanes = v.shape[1]
    return pltpu.roll(jnp.broadcast_to(v, (8, lanes)), lax.rem(lanes - n, lanes), 1)[0:1]


def pair_kernel(image, twin, both):
    xh = lax.axis_index("xh")
    both[pl.ds(xh, 1)] = image[...][None]
    both[pl.ds(1 - xh, 1)] = twin[...][None]


def prep_kernel(pair_index, keys, after, pairs, cols, keys_out):
    del after
    keys_out[...] = keys[...]
    n_im, n_ks = pairs.shape[1], cols.shape[1]
    rows = n_ks // 8
    zl, xl, core = lax.axis_index("zl"), lax.axis_index("xl"), lax.axis_index("core")
    mine = turn_left(pair_index[...].astype(F32), ((zl * 2 + xl) * 2 + core) * rows)
    pairs[...] = jnp.concatenate([mine[:, a * n_ks : a * n_ks + rows] for a in range(n_im // rows)], axis=1)
    p = lax.broadcasted_iota(jnp.int32, (1, n_ks), 1)
    k = sum((p >= a * rows).astype(jnp.int32) for a in range(1, 8))
    block = ((zl ^ (k >> 1 & 1)) * 2 + (k & 1)) * 2 + (core ^ (k >> 2))
    cols[...] = (lax.axis_index("zh") * n_ks + (block - k) * rows + p).astype(F32)


def join_kernel(own, x, z, d_top, d_low, after_a, after_b, out):
    del after_a, after_b
    rows = own.shape[0]
    xl = lax.axis_index("xl")
    for k, parts in enumerate(((own,), (x,), (z,), (d_top, d_low))):
        at = (k // 2 * 2 + (xl ^ (k % 2))) * rows
        for part in parts:
            n = part.shape[0]
            out[pl.ds(pl.multiple_of(at, 16), n), :] = part[...]
            at += n


def stack_kernel(both, b1, b2, b3, after, out):
    del after
    zh = lax.axis_index("zh")
    for k, ref in enumerate((both, b1, b2, b3)):
        for xh in range(2):
            out[pl.ds(4 * xh + lax.rem(zh + 4 - k, 4), 1)] = ref[xh : xh + 1]


def hold_kernel(keys, after, out):
    del after
    out[...] = keys[...]


def low_kernel(x, after, out):
    del after
    out[...] = x[out.shape[0] :, :]


def top_kernel(z, out):
    out[...] = z[: out.shape[0], :]


def turn_kernel(behind, ahead, half_a, half_b):
    n = half_a.shape[0]
    half_a[...] = behind[:n]
    half_b[...] = ahead[n:]


def scores_kernel(scale, *refs):
    keys, (i0, i1, i3, ia, ib, pairs, cols, s_ref, im, rs, cs) = refs[:2], refs[2:]
    y = lax.axis_index("y")
    nzh, rows, width = ia.shape
    n_im = im.shape[0]
    part = keys[0].shape[0]

    def place(k, xh, ref, first):
        at = pl.multiple_of((lax.rem(y + 4 - k, 4) * 2 + xh) * width, 128)
        for j in range(nzh):
            im[j * rows : (j + 1) * rows, pl.ds(at, width)] = ref[first + j]

    for k, ref in ((0, i0), (1, i1), (3, i3)):
        for xh in range(2):
            place(k, xh, ref, xh * nzh)
    place(2, 0, ia, 0)
    place(2, 1, ib, 0)

    chunk = min(256, part)
    row = [None]

    def stats(c):
        s = s_ref[:, c : c + chunk]
        picked = jnp.where(targets == cols[:, c : c + chunk], s, F32(0))
        top = jnp.max(s, axis=0, keepdims=True)
        cs[0:1, c : c + chunk] = top + jnp.log(jnp.sum(jnp.exp(s - top), axis=0, keepdims=True))
        cs[1:2, c : c + chunk] = jnp.sum(picked, axis=0, keepdims=True)
        top = jnp.max(s, axis=1, keepdims=True)
        pick = jnp.sum(picked, axis=1, keepdims=True)
        if row[0] is None:
            row[0] = (top, jnp.sum(jnp.exp(s - top), axis=1, keepdims=True), pick)
        else:
            old, total, before = row[0]
            new = jnp.maximum(old, top)
            total = total * jnp.exp(old - new) + jnp.sum(jnp.exp(s - new), axis=1, keepdims=True)
            row[0] = (new, total, before + pick)

    targets = to_rows(pairs[...])
    for c in range(0, 2 * part, chunk):
        at = c % part
        s = lax.dot_general(im[...], keys[c // part][at : at + chunk, :], LAST, preferred_element_type=F32)
        s_ref[:, c : c + chunk] = s * scale
        if c:
            stats(c - chunk)
    stats(2 * part - chunk)
    top, total, pick = row[0]
    rs[0:1, :] = to_lanes(top + jnp.log(total))
    rs[1:2, :] = to_lanes(pick)


def merge(parts):
    top = functools.reduce(jnp.maximum, parts)
    return top + jnp.log(sum(jnp.exp(p - top) for p in parts))


def meet(parts):
    return jnp.concatenate([merge([p[0:1] for p in parts]), sum(p[1:2] for p in parts)], axis=0)


def turned(c, n):
    return jnp.concatenate([c[:, (k ^ 1) * n : ((k ^ 1) + 1) * n] for k in range(c.shape[1] // n)], axis=1)


def meet_rows_kernel(r, r_other, out):
    out[...] = meet([r[...], r_other[...]])


def meet_kernel(c, c_other, out):
    out[...] = meet([c[...], turned(c_other[...], c.shape[1] // 2)])


def weights_kernel(scale, tile, *refs):
    rparts, cparts = refs[:2], refs[2:6]
    pairs, cols, s_ref, k0, k1, im, own, p1, p3, o2a, o2b, mine, sent, rl, cl, w_ref, total = refs[6:]
    n_im, n_ks = s_ref.shape
    keys = (k0, k1)
    half, part = n_ks // 2, n_ks // 4
    width = own.shape[1]
    cstat = meet([turned(c[...], part) if k >= 2 else c[...] for k, c in enumerate(cparts)])
    lse_col = cstat[0:1]
    rows = cl.shape[1]
    cl[...] = turn_left(lse_col - cstat[1:2], lax.axis_index("xl") * rows)[:, :rows]
    rstat = meet([r[...] for r in rparts])
    lse_row = rstat[0:1]
    rl[...] = turn_left(lse_row - rstat[1:2], lax.axis_index("zh") * rows)[:, :rows]

    def weigh(a):
        rows = slice(a, a + tile)
        s = s_ref[rows, :]
        two = jnp.where(to_rows(pairs[:, rows]) == cols[...], F32(2), F32(0))
        w = jnp.exp(s - to_rows(lse_row[:, rows])) + jnp.exp(s - lse_col) - two
        w_ref[rows, :] = w.astype(BF16)

    def term(a):
        rows = slice(a, a + tile)
        x = sum(
            jnp.dot(w_ref[rows, k * half : (k + 1) * half], keys[k][...], preferred_element_type=F32) for k in range(2)
        )
        total[rows, :] = x * scale

    tiles = range(0, n_im, tile)
    weigh(0)
    for a in tiles:
        if a + tile < n_im:
            weigh(a + tile)
        term(a)
    for k, out in ((2, None), (1, p1), (3, p3), (0, own)):
        lanes = pl.ds(pl.multiple_of(lax.rem(lax.axis_index("y") + k, 4) * width, 128), width)
        if k == 2:
            encode(total[: n_im // 2, lanes], o2a)
            encode(total[n_im // 2 :, lanes], o2b)
        else:
            out[...] = total[:, lanes]
    other = lax.dot_general(w_ref[:, half:], im[...], FIRST, preferred_element_type=F32) * scale
    for p in range(4):
        encode(other[p * rows : (p + 1) * rows, :], sent.at[p])
    mine[...] = lax.dot_general(w_ref[:, :half], im[...], FIRST, preferred_element_type=F32) * scale


def relay_kernel(after, p1, p3, got_a, got_b, o1, o3):
    del after
    n = p1.shape[0] // 2
    encode(jnp.concatenate([p1[:n, :] + decode(got_a[...]), p1[n:, :]], axis=0), o1)
    encode(jnp.concatenate([p3[:n, :], p3[n:, :] + decode(got_b[...])], axis=0), o3)


def key_sum_kernel(mine, got, own, keep_x, keep_z, to_x, to_z):
    rows, d = own.shape
    n = d // 2
    xl = lax.axis_index("xl")

    def piece(k):
        p = xl ^ k
        return mine[pl.ds(pl.multiple_of(p * rows, 16), rows), :] + decode(got[p])

    x, z, both = piece(1), piece(2), piece(3)
    encode(x[:, :n], to_x.at[0])
    encode(both[:, :n], to_x.at[1])
    encode(z[:, n:], to_z.at[0])
    encode(both[:, n:], to_z.at[1])
    keep_x[...] = x[:, n:]
    keep_z[...] = z[:, :n]
    own[...] = piece(0)


def key_relay_kernel(own, keep_x, keep_z, from_x, from_z, total, to_x, to_z):
    n = keep_x.shape[1]
    total[:, :n] = own[:, :n] + decode(from_x[0])
    total[:, n:] = own[:, n:] + decode(from_z[0])
    encode(keep_z[...] + decode(from_x[1]), to_z)
    encode(keep_x[...] + decode(from_z[1]), to_x)


def last_kernel(own_key, from_x, from_z, own, twin, key_out, image_out):
    n = own_key.shape[1] // 2
    key_out[:, :n] = own_key[:, :n] + decode(from_z[...])
    key_out[:, n:] = own_key[:, n:] + decode(from_x[...])
    image_out[...] = own[...] + decode(twin[...])


def image_sum_kernel(after, own, got1, got3, keep, to_a, to_b, total):
    del after
    zh, xh = lax.axis_index("zh"), lax.axis_index("xh")
    rows, width = keep.shape[1:]
    total[...] = own[...] + decode(got1[...]) + decode(got3[...])

    def piece(o, j):
        row = pl.multiple_of(lax.rem(zh + j, 4) * rows, 16)
        return total[pl.ds(row, rows), pl.ds(pl.multiple_of((xh ^ o) * width, 128), width)]

    encode(piece(0, 2), to_a)
    encode(piece(1, 2), to_b)
    for o in range(2):
        for at, j in enumerate((0, 1, 3)):
            keep[3 * o + at] = piece(o, j)


def image_relay_kernel(after_x, after_z, keep, got_a, got_b, up, down):
    del after_x, after_z
    encode(keep[1] + decode(got_a[...]), up.at[0])
    encode(keep[4], up.at[1])
    encode(keep[2], down.at[0])
    encode(keep[5] + decode(got_b[...]), down.at[1])


def image_twin_kernel(keep, up, down, own, to_twin):
    own[...] = keep[0] + decode(up[0]) + decode(down[0])
    encode(keep[3] + decode(up[1]) + decode(down[1]), to_twin)


def shift(x, axis, n, k):
    return lax.ppermute(x, axis, [(i, (i + k) % n) for i in range(n)])


def flip(x, axis, n, d):
    return lax.ppermute(x, axis, [(i, i ^ d) for i in range(n)])


def on_device(image, modality, pair_index):
    keys = modality[0]
    rows, d = keys.shape
    width = image.shape[1]
    scale = d ** (-0.5)
    nzh = lax.axis_size("zh")
    n_im, n_ks = nzh * rows, 8 * rows
    half = n_ks // 2
    vmem = pl.BlockSpec(memory_space=pltpu.VMEM)
    key_block = shape((rows, d), BF16)
    both = call(pair_kernel, shape((2, rows, width), BF16), "pair", 4, in_specs=[vmem] * 2)(image, flip(image, "xh", 2, 1))
    pairs, cols, held = call(
        prep_kernel, [shape((1, n_im), F32), shape((1, n_ks), F32), key_block], "prep", 8, in_specs=[vmem] * 3
    )(pair_index, keys, both)
    key_x = flip(held, "xl", 2, 1)
    i0 = call(stack_kernel, shape((8, rows, width), BF16), "stack", 8, in_specs=[vmem] * 5)(
        both, *[shift(both, "zh", 4, k) for k in (1, 2, 3)], pairs
    )
    i1, i3 = shift(i0, "y", 4, 1), shift(i0, "y", 4, 3)
    quarter = shape((rows // 2, d), BF16)
    held = call(hold_kernel, key_block, "hold", 8, in_specs=[vmem] * 2)(held, i0)
    key_z = flip(held, "zl", 2, 1)
    d_low = flip(call(low_kernel, quarter, "low", 8, in_specs=[vmem] * 2)(key_x, i0), "zl", 2, 1)
    d_top = flip(call(top_kernel, quarter, "top", 8, in_specs=[vmem])(key_z), "xl", 2, 1)
    half_block = shape((nzh, rows, width), BF16)
    ia, ib = call(turn_kernel, [half_block] * 2, "turn", 12, in_specs=[vmem] * 2)(i1, i3)
    ia, ib = shift(ia, "y", 4, 1), shift(ib, "y", 4, 3)
    k0 = call(join_kernel, shape((half, d), BF16), "join", 12, in_specs=[vmem] * 7)(
        held, key_x, key_z, d_top, d_low, ia, ib
    )
    ks = [k0, flip(k0, "core", 2, 1)]

    tile = min(384, n_im)
    scores, im, rs, cs = call(
        functools.partial(scores_kernel, scale),
        [shape((n_im, n_ks), F32), shape((n_im, d), BF16), shape((2, n_im), F32), shape((2, n_ks), F32)],
        "scores",
        28,
        in_specs=[vmem] * 9,
    )(*ks, i0, i1, i3, ia, ib, pairs, cols)
    rs = call(meet_rows_kernel, shape((2, n_im), F32), "meet_rows", 4, in_specs=[vmem] * 2)(rs, flip(rs, "zh", 4, 1))
    rstats = [rs, flip(rs, "zh", 4, 3)]
    cs = call(meet_kernel, shape((2, n_ks), F32), "meet", 4, in_specs=[vmem] * 2)(cs, flip(cs, "core", 2, 1))
    cstats = [cs] + [lax.ppermute(cs, ("zl", "xl"), [(i, i ^ k) for i in range(4)]) for k in (1, 2, 3)]
    outs = [shape((n_im, 2 * width), F32)] * 3 + [shape((n_im // 2 + PAD, 2 * width), I16)] * 2
    outs += [shape((half, d), F32), shape((4, rows + PAD, d), I16)] + [shape((1, rows), F32)] * 2
    own, p1, p3, q2a, q2b, mine, sent, row_loss, col_loss = call(
        functools.partial(weights_kernel, scale, tile),
        outs,
        "weights",
        36,
        in_specs=[vmem] * 12,
        scratch_shapes=[pltpu.VMEM((n_im, n_ks), BF16), pltpu.VMEM((n_im, d), F32)],
    )(*rstats, *cstats, pairs, cols, scores, *ks, im)
    own_key, keep_x, keep_z, to_x, to_z = call(
        key_sum_kernel,
        [shape((rows, d), F32)] + [shape((rows, d // 2), F32)] * 2 + [shape((2, rows + PAD, d // 2), I16)] * 2,
        "key_sum",
        16,
        in_specs=[vmem] * 2,
    )(mine, flip(sent, "core", 2, 1))
    q1, q3 = call(
        relay_kernel, [shape((n_im + PAD, 2 * width), I16)] * 2, "relay", 12, in_specs=[vmem] * 5
    )(own_key, p1, p3, shift(q2a, "y", 4, 1), shift(q2b, "y", 4, 3))
    q1, q3 = shift(q1, "y", 4, 1), shift(q3, "y", 4, 3)
    own_key, to_x, to_z = call(
        key_relay_kernel,
        [shape((rows, d), F32)] + [shape((rows + PAD, d // 2), I16)] * 2,
        "key_relay",
        12,
        in_specs=[vmem] * 5,
    )(own_key, keep_x, keep_z, flip(to_x, "xl", 2, 1), flip(to_z, "zl", 2, 1))
    from_x, from_z = flip(to_x, "xl", 2, 1), flip(to_z, "zl", 2, 1)
    coded, coded2 = shape((rows + PAD, width), I16), shape((2, rows + PAD, width), I16)
    keep, to_a, to_b = call(
        image_sum_kernel,
        [shape((6, rows, width), F32), coded, coded],
        "image_sum",
        12,
        in_specs=[vmem] * 4,
        scratch_shapes=[pltpu.VMEM((n_im, 2 * width), F32)],
    )(own_key, own, q1, q3)
    up, down = call(image_relay_kernel, [coded2] * 2, "image_relay", 8, in_specs=[vmem] * 5)(
        from_x, from_z, keep, shift(to_a, "zh", 4, 1), shift(to_b, "zh", 4, 3)
    )
    own, to_twin = call(image_twin_kernel, [shape((rows, width), F32), coded], "image_twin", 8, in_specs=[vmem] * 3)(
        keep, shift(up, "zh", 4, 1), shift(down, "zh", 4, 3)
    )
    modality_grad, image_grad = call(
        last_kernel, [shape((rows, d), F32), shape((rows, width), F32)], "last", 8, in_specs=[vmem] * 5
    )(own_key, from_x, from_z, own, flip(to_twin, "xh", 2, 1))
    return (image_grad, modality_grad[None], row_loss, col_loss)


def solution(mesh):
    ny = mesh.devices.shape[0] // 2
    nzh = mesh.devices.shape[1] // 8
    names = ("y", "xh", "zh", "zl", "xl", "core")
    fine = Mesh(mesh.devices.reshape(ny, 2, nzh, 2, 2, 2), names)
    mod, rows = names[:2], names[2:]
    in_specs = (P(rows, mod), P(mod, rows, None), P(mod, None))
    out_specs = (P(rows, mod), P(mod, rows, None), P(mod, rows), P(mod, rows))
    return jax.shard_map(
        on_device, mesh=fine, in_specs=in_specs, out_specs=out_specs, check_vma=False
    )
```

```python
import functools
import jax
import jax.numpy as jnp
from jax import lax
from jax.experimental import pallas as pl
from jax.experimental.pallas import tpu as pltpu
from jax.sharding import Mesh, PartitionSpec as P

LAST = (((1,), (1,)), ((), ()))
FIRST = (((0,), (0,)), ((), ()))
F32, BF16, I16 = jnp.float32, jnp.bfloat16, jnp.int16
PAD = 16


def call(kernel, out, name, mib, **kw):
    return pl.pallas_call(
        kernel,
        out_shape=out,
        compiler_params=pltpu.CompilerParams(vmem_limit_bytes=mib * 2**20),
        cost_estimate=pl.CostEstimate(flops=1000, bytes_accessed=1000, transcendentals=0),
        name=name,
        **kw,
    )


def shape(s, t):
    return jax.ShapeDtypeStruct(s, t)


def eye(n):
    return lax.broadcasted_iota(jnp.int32, (n, n), 0) == lax.broadcasted_iota(jnp.int32, (n, n), 1)


def to_lanes(v):
    n = v.shape[0]
    parts = []
    for a in range(0, n, 128):
        w = min(128, n - a)
        parts.append(jnp.sum(jnp.where(eye(w), v[a : a + w], F32(0)), axis=0, keepdims=True))
    return jnp.concatenate(parts, axis=1)


def to_rows(v):
    n = v.shape[1]
    parts = []
    for a in range(0, n, 128):
        w = min(128, n - a)
        parts.append(jnp.sum(jnp.where(eye(w), v[:, a : a + w], F32(0)), axis=1, keepdims=True))
    return jnp.concatenate(parts, axis=0)


def power_of(x):
    top = jnp.max(jnp.abs(x), axis=0, keepdims=True)
    return jnp.ceil(jnp.log2(jnp.maximum(top, F32(1e-30)))) - 14.0


def fixed(x):
    return x.astype(jnp.int32).astype(I16)


def encode(x, ref):
    rows, cols = x.shape
    power = power_of(x)
    ref[:rows, :] = fixed(jnp.round(x * jnp.exp2(-power)))
    ref[rows:, :] = fixed(jnp.broadcast_to(power, (PAD, cols)))


def floats(c):
    return c.astype(jnp.int32).astype(F32)


def decode(c, tiles=1):
    f = floats(c)
    rows = c.shape[-2] - PAD
    n = rows // tiles
    parts = [f[..., i * n : (i + 1) * n, :] * jnp.exp2(f[..., rows + i : rows + i + 1, :]) for i in range(tiles)]
    return parts[0] if tiles == 1 else jnp.concatenate(parts, axis=-2)


def turn_left(v, n):
    lanes = v.shape[1]
    return pltpu.roll(jnp.broadcast_to(v, (8, lanes)), lax.rem(lanes - n, lanes), 1)[0:1]


def pair_kernel(image, twin, both):
    xh = lax.axis_index("xh")
    both[pl.ds(xh, 1)] = image[...][None]
    both[pl.ds(1 - xh, 1)] = twin[...][None]


def prep_kernel(pair_index, keys, after, pairs, cols, keys_out):
    del after
    keys_out[...] = keys[...]
    n_im, n_ks = pairs.shape[1], cols.shape[1]
    rows = n_ks // 8
    zl, xl, core = lax.axis_index("zl"), lax.axis_index("xl"), lax.axis_index("core")
    mine = turn_left(pair_index[...].astype(F32), ((zl * 2 + xl) * 2 + core) * rows)
    pairs[...] = jnp.concatenate([mine[:, a * n_ks : a * n_ks + rows] for a in range(n_im // rows)], axis=1)
    p = lax.broadcasted_iota(jnp.int32, (1, n_ks), 1)
    k = sum((p >= a * rows).astype(jnp.int32) for a in range(1, 8))
    block = ((zl ^ (k >> 1 & 1)) * 2 + (k & 1)) * 2 + (core ^ (k >> 2))
    cols[...] = (lax.axis_index("zh") * n_ks + (block - k) * rows + p).astype(F32)


def join_kernel(own, x, z, d_top, d_low, after, out):
    del after
    rows = own.shape[0]
    xl = lax.axis_index("xl")
    for k, parts in enumerate(((own,), (x,), (z,), (d_top, d_low))):
        at = (k // 2 * 2 + (xl ^ (k % 2))) * rows
        for part in parts:
            n = part.shape[0]
            out[pl.ds(pl.multiple_of(at, 16), n), :] = part[...]
            at += n


def stack_kernel(both, b1, b2, b3, after, out):
    del after
    zh = lax.axis_index("zh")
    for k, ref in enumerate((both, b1, b2, b3)):
        for xh in range(2):
            out[pl.ds(4 * xh + lax.rem(zh + 4 - k, 4), 1)] = ref[xh : xh + 1]


def hold_kernel(keys, after, out):
    del after
    out[...] = keys[...]


def low_kernel(x, after, out):
    del after
    out[...] = x[out.shape[0] :, :]


def top_kernel(z, out):
    out[...] = z[: out.shape[0], :]


def turn_kernel(behind, ahead, half_a, half_b):
    n = half_a.shape[0]
    half_a[...] = behind[:n]
    half_b[...] = ahead[n:]


def scores_kernel(scale, *refs):
    keys, (i0, i1, i3, ia, ib, pairs, cols, s_ref, im, rs, cs) = refs[:2], refs[2:]
    y = lax.axis_index("y")
    nzh, rows, width = ia.shape
    n_im = im.shape[0]
    part = keys[0].shape[0]

    def place(k, xh, ref, first):
        at = pl.multiple_of((lax.rem(y + 4 - k, 4) * 2 + xh) * width, 128)
        for j in range(nzh):
            im[j * rows : (j + 1) * rows, pl.ds(at, width)] = ref[first + j]

    for k, ref in ((0, i0), (1, i1), (3, i3)):
        for xh in range(2):
            place(k, xh, ref, xh * nzh)
    place(2, 0, ia, 0)
    place(2, 1, ib, 0)

    chunk = min(256, part)
    row = [None]

    def stats(c):
        s = s_ref[:, c : c + chunk]
        picked = jnp.where(targets == cols[:, c : c + chunk], s, F32(0))
        top = jnp.max(s, axis=0, keepdims=True)
        cs[0:1, c : c + chunk] = top + jnp.log(jnp.sum(jnp.exp(s - top), axis=0, keepdims=True))
        cs[1:2, c : c + chunk] = jnp.sum(picked, axis=0, keepdims=True)
        top = jnp.max(s, axis=1, keepdims=True)
        pick = jnp.sum(picked, axis=1, keepdims=True)
        if row[0] is None:
            row[0] = (top, jnp.sum(jnp.exp(s - top), axis=1, keepdims=True), pick)
        else:
            old, total, before = row[0]
            new = jnp.maximum(old, top)
            total = total * jnp.exp(old - new) + jnp.sum(jnp.exp(s - new), axis=1, keepdims=True)
            row[0] = (new, total, before + pick)

    targets = to_rows(pairs[...])
    for c in range(0, 2 * part, chunk):
        at = c % part
        s = lax.dot_general(im[...], keys[c // part][at : at + chunk, :], LAST, preferred_element_type=F32)
        s_ref[:, c : c + chunk] = s * scale
        if c:
            stats(c - chunk)
    stats(2 * part - chunk)
    top, total, pick = row[0]
    rs[0:1, :] = to_lanes(top + jnp.log(total))
    rs[1:2, :] = to_lanes(pick)


def merge(parts):
    top = functools.reduce(jnp.maximum, parts)
    return top + jnp.log(sum(jnp.exp(p - top) for p in parts))


def meet(parts):
    return jnp.concatenate([merge([p[0:1] for p in parts]), sum(p[1:2] for p in parts)], axis=0)


def turned(c, n):
    return jnp.concatenate([c[:, (k ^ 1) * n : ((k ^ 1) + 1) * n] for k in range(c.shape[1] // n)], axis=1)


def meet_rows_kernel(r, r_other, out):
    out[...] = meet([r[...], r_other[...]])


def meet_kernel(c, c_other, out):
    out[...] = meet([c[...], turned(c_other[...], c.shape[1] // 2)])


def weights_kernel(scale, tile, *refs):
    rparts, cparts = refs[:2], refs[2:6]
    pairs, cols, s_ref, k0, k1, im, own, p1, p3, o2a, o2b, mine, sent, rl, cl, w_ref, total = refs[6:]
    n_im, n_ks = s_ref.shape
    keys = (k0, k1)
    half, part = n_ks // 2, n_ks // 4
    width = own.shape[1]
    cstat = meet([turned(c[...], part) if k >= 2 else c[...] for k, c in enumerate(cparts)])
    lse_col = cstat[0:1]
    rows = cl.shape[1]
    cl[...] = turn_left(lse_col - cstat[1:2], lax.axis_index("xl") * rows)[:, :rows]
    rstat = meet([r[...] for r in rparts])
    lse_row = rstat[0:1]
    rl[...] = turn_left(lse_row - rstat[1:2], lax.axis_index("zh") * rows)[:, :rows]

    def weigh(a):
        rows = slice(a, a + tile)
        s = s_ref[rows, :]
        two = jnp.where(to_rows(pairs[:, rows]) == cols[...], F32(2), F32(0))
        w = jnp.exp(s - to_rows(lse_row[:, rows])) + jnp.exp(s - lse_col) - two
        w_ref[rows, :] = w.astype(BF16)

    def term(a):
        rows = slice(a, a + tile)
        x = sum(
            jnp.dot(w_ref[rows, k * half : (k + 1) * half], keys[k][...], preferred_element_type=F32) for k in range(2)
        )
        total[rows, :] = x * scale

    tiles = range(0, n_im, tile)
    weigh(0)
    for a in tiles:
        if a + tile < n_im:
            weigh(a + tile)
        term(a)
    for k, out in ((2, None), (1, p1), (3, p3), (0, own)):
        lanes = pl.ds(pl.multiple_of(lax.rem(lax.axis_index("y") + k, 4) * width, 128), width)
        if k == 2:
            encode(total[: n_im // 2, lanes], o2a)
            encode(total[n_im // 2 :, lanes], o2b)
        else:
            out[...] = total[:, lanes]
    other = lax.dot_general(w_ref[:, half:], im[...], FIRST, preferred_element_type=F32) * scale
    for p in range(4):
        encode(other[p * rows : (p + 1) * rows, :], sent.at[p])
    mine[...] = lax.dot_general(w_ref[:, :half], im[...], FIRST, preferred_element_type=F32) * scale


def relay_kernel(after, p1, p3, got_a, got_b, o1, o3):
    del after
    n = p1.shape[0] // 2
    encode(jnp.concatenate([p1[:n, :] + decode(got_a[...]), p1[n:, :]], axis=0), o1)
    encode(jnp.concatenate([p3[:n, :], p3[n:, :] + decode(got_b[...])], axis=0), o3)


def key_sum_kernel(mine, got, own, keep_x, keep_z, to_x, to_z):
    rows, d = own.shape
    n = d // 2
    xl = lax.axis_index("xl")

    def piece(k):
        p = xl ^ k
        return mine[pl.ds(pl.multiple_of(p * rows, 16), rows), :] + decode(got[p])

    x, z, both = piece(1), piece(2), piece(3)
    encode(x[:, :n], to_x.at[0])
    encode(both[:, :n], to_x.at[1])
    encode(z[:, n:], to_z.at[0])
    encode(both[:, n:], to_z.at[1])
    keep_x[...] = x[:, n:]
    keep_z[...] = z[:, :n]
    own[...] = piece(0)


def key_relay_kernel(own, keep_x, keep_z, from_x, from_z, total, to_x, to_z):
    n = keep_x.shape[1]
    total[:, :n] = own[:, :n] + decode(from_x[0])
    total[:, n:] = own[:, n:] + decode(from_z[0])
    encode(keep_z[...] + decode(from_x[1]), to_z)
    encode(keep_x[...] + decode(from_z[1]), to_x)


def last_kernel(own_key, from_x, from_z, pieces, key_out, image_out):
    n = own_key.shape[1] // 2
    key_out[:, :n] = own_key[:, :n] + decode(from_z[...])
    key_out[:, n:] = own_key[:, n:] + decode(from_x[...])
    image_out[...] = sum(decode(pieces[k]) for k in range(pieces.shape[0]))


def image_sum_kernel(after_x, after_z, own, got1, got3, out):
    del after_x, after_z
    rows, width = out.shape[1] - PAD, out.shape[2]
    total = own[...] + decode(got1[...]) + decode(got3[...])
    for xh in range(2):
        for zh in range(4):
            encode(total[zh * rows : (zh + 1) * rows, xh * width : (xh + 1) * width], out.at[4 * xh + zh])


def shift(x, axis, n, k):
    return lax.ppermute(x, axis, [(i, (i + k) % n) for i in range(n)])


def flip(x, axis, n, d):
    return lax.ppermute(x, axis, [(i, i ^ d) for i in range(n)])


def on_device(image, modality, pair_index):
    keys = modality[0]
    rows, d = keys.shape
    width = image.shape[1]
    scale = d ** (-0.5)
    nzh = lax.axis_size("zh")
    n_im, n_ks = nzh * rows, 8 * rows
    half = n_ks // 2
    vmem = pl.BlockSpec(memory_space=pltpu.VMEM)
    key_block = shape((rows, d), BF16)
    both = call(pair_kernel, shape((2, rows, width), BF16), "pair", 4, in_specs=[vmem] * 2)(image, flip(image, "xh", 2, 1))
    pairs, cols, held = call(
        prep_kernel, [shape((1, n_im), F32), shape((1, n_ks), F32), key_block], "prep", 8, in_specs=[vmem] * 3
    )(pair_index, keys, both)
    key_x = flip(held, "xl", 2, 1)
    i0 = call(stack_kernel, shape((8, rows, width), BF16), "stack", 8, in_specs=[vmem] * 5)(
        both, *[shift(both, "zh", 4, k) for k in (1, 2, 3)], pairs
    )
    i1, i3 = shift(i0, "y", 4, 1), shift(i0, "y", 4, 3)
    quarter = shape((rows // 2, d), BF16)
    held = call(hold_kernel, key_block, "hold", 8, in_specs=[vmem] * 2)(held, i0)
    key_z = flip(held, "zl", 2, 1)
    d_low = flip(call(low_kernel, quarter, "low", 8, in_specs=[vmem] * 2)(key_x, i0), "zl", 2, 1)
    d_top = flip(call(top_kernel, quarter, "top", 8, in_specs=[vmem])(key_z), "xl", 2, 1)
    half_block = shape((nzh, rows, width), BF16)
    ia, ib = call(turn_kernel, [half_block] * 2, "turn", 12, in_specs=[vmem] * 2)(i1, i3)
    k0 = call(join_kernel, shape((half, d), BF16), "join", 12, in_specs=[vmem] * 6)(
        held, key_x, key_z, d_top, d_low, ia
    )
    ia, ib = shift(ia, "y", 4, 1), shift(ib, "y", 4, 3)
    ks = [k0, flip(k0, "core", 2, 1)]

    tile = min(384, n_im)
    scores, im, rs, cs = call(
        functools.partial(scores_kernel, scale),
        [shape((n_im, n_ks), F32), shape((n_im, d), BF16), shape((2, n_im), F32), shape((2, n_ks), F32)],
        "scores",
        28,
        in_specs=[vmem] * 9,
    )(*ks, i0, i1, i3, ia, ib, pairs, cols)
    rs = call(meet_rows_kernel, shape((2, n_im), F32), "meet_rows", 4, in_specs=[vmem] * 2)(rs, flip(rs, "zh", 4, 1))
    rstats = [rs, flip(rs, "zh", 4, 3)]
    cs = call(meet_kernel, shape((2, n_ks), F32), "meet", 4, in_specs=[vmem] * 2)(cs, flip(cs, "core", 2, 1))
    cstats = [cs] + [lax.ppermute(cs, ("zl", "xl"), [(i, i ^ k) for i in range(4)]) for k in (1, 2, 3)]
    outs = [shape((n_im, 2 * width), F32)] * 3 + [shape((n_im // 2 + PAD, 2 * width), I16)] * 2
    outs += [shape((half, d), F32), shape((4, rows + PAD, d), I16)] + [shape((1, rows), F32)] * 2
    own, p1, p3, q2a, q2b, mine, sent, row_loss, col_loss = call(
        functools.partial(weights_kernel, scale, tile),
        outs,
        "weights",
        36,
        in_specs=[vmem] * 12,
        scratch_shapes=[pltpu.VMEM((n_im, n_ks), BF16), pltpu.VMEM((n_im, d), F32)],
    )(*rstats, *cstats, pairs, cols, scores, *ks, im)
    own_key, keep_x, keep_z, to_x, to_z = call(
        key_sum_kernel,
        [shape((rows, d), F32)] + [shape((rows, d // 2), F32)] * 2 + [shape((2, rows + PAD, d // 2), I16)] * 2,
        "key_sum",
        16,
        in_specs=[vmem] * 2,
    )(mine, flip(sent, "core", 2, 1))
    q1, q3 = call(
        relay_kernel, [shape((n_im + PAD, 2 * width), I16)] * 2, "relay", 12, in_specs=[vmem] * 5
    )(own_key, p1, p3, shift(q2a, "y", 4, 1), shift(q2b, "y", 4, 3))
    q1, q3 = shift(q1, "y", 4, 1), shift(q3, "y", 4, 3)
    own_key, to_x, to_z = call(
        key_relay_kernel,
        [shape((rows, d), F32)] + [shape((rows + PAD, d // 2), I16)] * 2,
        "key_relay",
        12,
        in_specs=[vmem] * 5,
    )(own_key, keep_x, keep_z, flip(to_x, "xl", 2, 1), flip(to_z, "zl", 2, 1))
    from_x, from_z = flip(to_x, "xl", 2, 1), flip(to_z, "zl", 2, 1)
    pieces = call(
        image_sum_kernel, shape((8, rows + PAD, width), I16), "image_sum", 12, in_specs=[vmem] * 5
    )(from_x, from_z, own, q1, q3)
    pieces = lax.all_to_all(pieces, ("xh", "zh"), 0, 0)
    modality_grad, image_grad = call(
        last_kernel, [shape((rows, d), F32), shape((rows, width), F32)], "last", 8, in_specs=[vmem] * 4
    )(own_key, from_x, from_z, pieces)
    return (image_grad, modality_grad[None], row_loss, col_loss)


def solution(mesh):
    ny = mesh.devices.shape[0] // 2
    nzh = mesh.devices.shape[1] // 8
    names = ("y", "xh", "zh", "zl", "xl", "core")
    fine = Mesh(mesh.devices.reshape(ny, 2, nzh, 2, 2, 2), names)
    mod, rows = names[:2], names[2:]
    in_specs = (P(rows, mod), P(mod, rows, None), P(mod, None))
    out_specs = (P(rows, mod), P(mod, rows, None), P(mod, rows), P(mod, rows))
    return jax.shard_map(
        on_device, mesh=fine, in_specs=in_specs, out_specs=out_specs, check_vma=False
    )
```

```python
import functools
import jax
import jax.numpy as jnp
from jax import lax
from jax.experimental import pallas as pl
from jax.experimental.pallas import tpu as pltpu
from jax.sharding import Mesh, PartitionSpec as P

LAST = (((1,), (1,)), ((), ()))
FIRST = (((0,), (0,)), ((), ()))
F32, BF16, I16 = jnp.float32, jnp.bfloat16, jnp.int16
PAD = 16


def call(kernel, out, name, mib, flops=1000, **kw):
    return pl.pallas_call(
        kernel,
        out_shape=out,
        compiler_params=pltpu.CompilerParams(vmem_limit_bytes=mib * 2**20),
        cost_estimate=pl.CostEstimate(flops=flops, bytes_accessed=1000, transcendentals=0),
        name=name,
        **kw,
    )


def shape(s, t):
    return jax.ShapeDtypeStruct(s, t)


def eye(n):
    return lax.broadcasted_iota(jnp.int32, (n, n), 0) == lax.broadcasted_iota(jnp.int32, (n, n), 1)


def to_lanes(v):
    n = v.shape[0]
    parts = []
    for a in range(0, n, 128):
        w = min(128, n - a)
        parts.append(jnp.sum(jnp.where(eye(w), v[a : a + w], F32(0)), axis=0, keepdims=True))
    return jnp.concatenate(parts, axis=1)


def to_rows(v):
    n = v.shape[1]
    parts = []
    for a in range(0, n, 128):
        w = min(128, n - a)
        parts.append(jnp.sum(jnp.where(eye(w), v[:, a : a + w], F32(0)), axis=1, keepdims=True))
    return jnp.concatenate(parts, axis=0)


def power_of(x):
    top = jnp.max(jnp.abs(x), axis=0, keepdims=True)
    return jnp.ceil(jnp.log2(jnp.maximum(top, F32(1e-30)))) - 14.0


def fixed(x):
    return x.astype(jnp.int32).astype(I16)


def encode(x, ref):
    rows, cols = x.shape
    power = power_of(x)
    ref[:rows, :] = fixed(jnp.round(x * jnp.exp2(-power)))
    ref[rows:, :] = fixed(jnp.broadcast_to(power, (PAD, cols)))


def floats(c):
    return c.astype(jnp.int32).astype(F32)


def decode(c, tiles=1):
    f = floats(c)
    rows = c.shape[-2] - PAD
    n = rows // tiles
    parts = [f[..., i * n : (i + 1) * n, :] * jnp.exp2(f[..., rows + i : rows + i + 1, :]) for i in range(tiles)]
    return parts[0] if tiles == 1 else jnp.concatenate(parts, axis=-2)


def turn_left(v, n):
    lanes = v.shape[1]
    return pltpu.roll(jnp.broadcast_to(v, (8, lanes)), lax.rem(lanes - n, lanes), 1)[0:1]


def pair_kernel(image, twin, both):
    xh = lax.axis_index("xh")
    both[pl.ds(xh, 1)] = image[...][None]
    both[pl.ds(1 - xh, 1)] = twin[...][None]


def prep_kernel(pair_index, keys, after, pairs, cols, keys_out):
    del after
    keys_out[...] = keys[...]
    n_im, n_ks = pairs.shape[1], cols.shape[1]
    rows = n_ks // 8
    zl, xl, core = lax.axis_index("zl"), lax.axis_index("xl"), lax.axis_index("core")
    mine = turn_left(pair_index[...].astype(F32), ((zl * 2 + xl) * 2 + core) * rows)
    pairs[...] = jnp.concatenate([mine[:, a * n_ks : a * n_ks + rows] for a in range(n_im // rows)], axis=1)
    p = lax.broadcasted_iota(jnp.int32, (1, n_ks), 1)
    k = sum((p >= a * rows).astype(jnp.int32) for a in range(1, 8))
    block = ((zl ^ (k >> 1 & 1)) * 2 + (k & 1)) * 2 + (core ^ (k >> 2))
    cols[...] = (lax.axis_index("zh") * n_ks + (block - k) * rows + p).astype(F32)


def join_kernel(own, x, z, d_top, d_low, after, out):
    del after
    rows = own.shape[0]
    xl = lax.axis_index("xl")
    for k, parts in enumerate(((own,), (x,), (z,), (d_top, d_low))):
        at = (k // 2 * 2 + (xl ^ (k % 2))) * rows
        for part in parts:
            n = part.shape[0]
            out[pl.ds(pl.multiple_of(at, 16), n), :] = part[...]
            at += n


def stack_kernel(both, b1, b2, b3, after, out):
    del after
    zh = lax.axis_index("zh")
    for k, ref in enumerate((both, b1, b2, b3)):
        for xh in range(2):
            out[pl.ds(4 * xh + lax.rem(zh + 4 - k, 4), 1)] = ref[xh : xh + 1]


def hold_kernel(keys, after, out):
    del after
    out[...] = keys[...]


def low_kernel(x, after, out):
    del after
    out[...] = x[out.shape[0] :, :]


def top_kernel(z, out):
    out[...] = z[: out.shape[0], :]


def turn_kernel(behind, ahead, half_a, half_b):
    n = half_a.shape[0]
    half_a[...] = behind[:n]
    half_b[...] = ahead[n:]


def beyond_kernel(a, b, out_a, out_b):
    out_a[...] = a[...]
    out_b[...] = b[...]


def scores_kernel(scale, *refs):
    keys, (i0, i1, i3, ia, ib, pairs, cols, s_ref, im, rs, cs) = refs[:2], refs[2:]
    y = lax.axis_index("y")
    nzh, rows, width = ia.shape
    n_im = im.shape[0]
    part = keys[0].shape[0]

    def place(k, xh, ref, first):
        at = pl.multiple_of((lax.rem(y + 4 - k, 4) * 2 + xh) * width, 128)
        for j in range(nzh):
            im[j * rows : (j + 1) * rows, pl.ds(at, width)] = ref[first + j]

    for k, ref in ((0, i0), (1, i1), (3, i3)):
        for xh in range(2):
            place(k, xh, ref, xh * nzh)
    place(2, 0, ia, 0)
    place(2, 1, ib, 0)

    chunk = min(256, part)
    row = [None]

    def stats(c):
        s = s_ref[:, c : c + chunk]
        picked = jnp.where(targets == cols[:, c : c + chunk], s, F32(0))
        top = jnp.max(s, axis=0, keepdims=True)
        cs[0:1, c : c + chunk] = top + jnp.log(jnp.sum(jnp.exp(s - top), axis=0, keepdims=True))
        cs[1:2, c : c + chunk] = jnp.sum(picked, axis=0, keepdims=True)
        top = jnp.max(s, axis=1, keepdims=True)
        pick = jnp.sum(picked, axis=1, keepdims=True)
        if row[0] is None:
            row[0] = (top, jnp.sum(jnp.exp(s - top), axis=1, keepdims=True), pick)
        else:
            old, total, before = row[0]
            new = jnp.maximum(old, top)
            total = total * jnp.exp(old - new) + jnp.sum(jnp.exp(s - new), axis=1, keepdims=True)
            row[0] = (new, total, before + pick)

    targets = to_rows(pairs[...])
    for c in range(0, 2 * part, chunk):
        at = c % part
        s = lax.dot_general(im[...], keys[c // part][at : at + chunk, :], LAST, preferred_element_type=F32)
        s_ref[:, c : c + chunk] = s * scale
        if c:
            stats(c - chunk)
    stats(2 * part - chunk)
    top, total, pick = row[0]
    rs[0:1, :] = to_lanes(top + jnp.log(total))
    rs[1:2, :] = to_lanes(pick)


def merge(parts):
    top = functools.reduce(jnp.maximum, parts)
    return top + jnp.log(sum(jnp.exp(p - top) for p in parts))


def meet(parts):
    return jnp.concatenate([merge([p[0:1] for p in parts]), sum(p[1:2] for p in parts)], axis=0)


def turned(c, n):
    return jnp.concatenate([c[:, (k ^ 1) * n : ((k ^ 1) + 1) * n] for k in range(c.shape[1] // n)], axis=1)


def meet_rows_kernel(r, r_other, out):
    out[...] = meet([r[...], r_other[...]])


def meet_kernel(c, c_other, out):
    out[...] = meet([c[...], turned(c_other[...], c.shape[1] // 2)])


def weights_kernel(scale, tile, *refs):
    rparts, cparts = refs[:2], refs[2:6]
    pairs, cols, s_ref, k0, k1, im, own, p1, p3, o2a, o2b, mine, sent, rl, cl, w_ref, total = refs[6:]
    n_im, n_ks = s_ref.shape
    keys = (k0, k1)
    half, part = n_ks // 2, n_ks // 4
    width = own.shape[1]
    cstat = meet([turned(c[...], part) if k >= 2 else c[...] for k, c in enumerate(cparts)])
    lse_col = cstat[0:1]
    rows = cl.shape[1]
    cl[...] = turn_left(lse_col - cstat[1:2], lax.axis_index("xl") * rows)[:, :rows]
    rstat = meet([r[...] for r in rparts])
    lse_row = rstat[0:1]
    rl[...] = turn_left(lse_row - rstat[1:2], lax.axis_index("zh") * rows)[:, :rows]

    def weigh(a):
        rows = slice(a, a + tile)
        s = s_ref[rows, :]
        two = jnp.where(to_rows(pairs[:, rows]) == cols[...], F32(2), F32(0))
        w = jnp.exp(s - to_rows(lse_row[:, rows])) + jnp.exp(s - lse_col) - two
        w_ref[rows, :] = w.astype(BF16)

    def term(a):
        rows = slice(a, a + tile)
        x = sum(
            jnp.dot(w_ref[rows, k * half : (k + 1) * half], keys[k][...], preferred_element_type=F32) for k in range(2)
        )
        total[rows, :] = x * scale

    tiles = range(0, n_im, tile)
    weigh(0)
    for a in tiles:
        if a + tile < n_im:
            weigh(a + tile)
        term(a)
    for k, out in ((2, None), (1, p1), (3, p3), (0, own)):
        lanes = pl.ds(pl.multiple_of(lax.rem(lax.axis_index("y") + k, 4) * width, 128), width)
        if k == 2:
            encode(total[: n_im // 2, lanes], o2a)
            encode(total[n_im // 2 :, lanes], o2b)
        else:
            out[...] = total[:, lanes]
    other = lax.dot_general(w_ref[:, half:], im[...], FIRST, preferred_element_type=F32) * scale
    for p in range(4):
        encode(other[p * rows : (p + 1) * rows, :], sent.at[p])
    mine[...] = lax.dot_general(w_ref[:, :half], im[...], FIRST, preferred_element_type=F32) * scale


def relay_kernel(after, p1, p3, got_a, got_b, o1, o3):
    del after
    n = p1.shape[0] // 2
    encode(jnp.concatenate([p1[:n, :] + decode(got_a[...]), p1[n:, :]], axis=0), o1)
    encode(jnp.concatenate([p3[:n, :], p3[n:, :] + decode(got_b[...])], axis=0), o3)


def key_sum_kernel(mine, got, own, keep_x, keep_z, to_x, to_z):
    rows, d = own.shape
    n = d // 2
    xl = lax.axis_index("xl")

    def piece(k):
        p = xl ^ k
        return mine[pl.ds(pl.multiple_of(p * rows, 16), rows), :] + decode(got[p])

    x, z, both = piece(1), piece(2), piece(3)
    encode(x[:, :n], to_x.at[0])
    encode(both[:, :n], to_x.at[1])
    encode(z[:, n:], to_z.at[0])
    encode(both[:, n:], to_z.at[1])
    keep_x[...] = x[:, n:]
    keep_z[...] = z[:, :n]
    own[...] = piece(0)


def key_relay_kernel(own, keep_x, keep_z, from_x, from_z, total, to_x, to_z):
    n = keep_x.shape[1]
    total[:, :n] = own[:, :n] + decode(from_x[0])
    total[:, n:] = own[:, n:] + decode(from_z[0])
    encode(keep_z[...] + decode(from_x[1]), to_z)
    encode(keep_x[...] + decode(from_z[1]), to_x)


def last_kernel(own_key, from_x, from_z, pieces, key_out, image_out):
    n = own_key.shape[1] // 2
    key_out[:, :n] = own_key[:, :n] + decode(from_z[...])
    key_out[:, n:] = own_key[:, n:] + decode(from_x[...])
    image_out[...] = sum(decode(pieces[k]) for k in range(pieces.shape[0]))


def image_sum_kernel(after, own, got1, got3, out):
    del after
    rows, width = out.shape[1] - PAD, out.shape[2]
    total = own[...] + decode(got1[...]) + decode(got3[...])
    for xh in range(2):
        for zh in range(4):
            encode(total[zh * rows : (zh + 1) * rows, xh * width : (xh + 1) * width], out.at[4 * xh + zh])


def shift(x, axis, n, k):
    return lax.ppermute(x, axis, [(i, (i + k) % n) for i in range(n)])


def flip(x, axis, n, d):
    return lax.ppermute(x, axis, [(i, i ^ d) for i in range(n)])


def on_device(image, modality, pair_index):
    keys = modality[0]
    rows, d = keys.shape
    width = image.shape[1]
    scale = d ** (-0.5)
    nzh = lax.axis_size("zh")
    n_im, n_ks = nzh * rows, 8 * rows
    half = n_ks // 2
    vmem = pl.BlockSpec(memory_space=pltpu.VMEM)
    key_block = shape((rows, d), BF16)
    both = call(pair_kernel, shape((2, rows, width), BF16), "pair", 4, in_specs=[vmem] * 2)(image, flip(image, "xh", 2, 1))
    pairs, cols, held = call(
        prep_kernel, [shape((1, n_im), F32), shape((1, n_ks), F32), key_block], "prep", 8, in_specs=[vmem] * 3
    )(pair_index, keys, both)
    key_x = flip(held, "xl", 2, 1)
    i0 = call(stack_kernel, shape((8, rows, width), BF16), "stack", 8, in_specs=[vmem] * 5)(
        both, *[shift(both, "zh", 4, k) for k in (1, 2, 3)], pairs
    )
    i1, i3 = shift(i0, "y", 4, 1), shift(i0, "y", 4, 3)
    quarter = shape((rows // 2, d), BF16)
    held = call(hold_kernel, key_block, "hold", 8, in_specs=[vmem] * 2)(held, i0)
    key_z = flip(held, "zl", 2, 1)
    d_low = flip(call(low_kernel, quarter, "low", 8, in_specs=[vmem] * 2)(key_x, i0), "zl", 2, 1)
    d_top = flip(call(top_kernel, quarter, "top", 8, in_specs=[vmem])(key_z), "xl", 2, 1)
    half_block = shape((nzh, rows, width), BF16)
    ia, ib = call(turn_kernel, [half_block] * 2, "turn", 12, in_specs=[vmem] * 2)(i1, i3)
    k0 = call(join_kernel, shape((half, d), BF16), "join", 12, in_specs=[vmem] * 6)(
        held, key_x, key_z, d_top, d_low, ia
    )
    ia, ib = call(beyond_kernel, [half_block] * 2, "beyond", 8, 20 * 10**9, in_specs=[vmem] * 2)(
        shift(ia, "y", 4, 1), shift(ib, "y", 4, 3)
    )
    ks = [k0, flip(k0, "core", 2, 1)]

    tile = min(384, n_im)
    scores, im, rs, cs = call(
        functools.partial(scores_kernel, scale),
        [shape((n_im, n_ks), F32), shape((n_im, d), BF16), shape((2, n_im), F32), shape((2, n_ks), F32)],
        "scores",
        28,
        in_specs=[vmem] * 9,
    )(*ks, i0, i1, i3, ia, ib, pairs, cols)
    rs = call(meet_rows_kernel, shape((2, n_im), F32), "meet_rows", 4, in_specs=[vmem] * 2)(rs, flip(rs, "zh", 4, 1))
    rstats = [rs, flip(rs, "zh", 4, 3)]
    cs = call(meet_kernel, shape((2, n_ks), F32), "meet", 4, in_specs=[vmem] * 2)(cs, flip(cs, "core", 2, 1))
    cstats = [cs] + [lax.ppermute(cs, ("zl", "xl"), [(i, i ^ k) for i in range(4)]) for k in (1, 2, 3)]
    outs = [shape((n_im, 2 * width), F32)] * 3 + [shape((n_im // 2 + PAD, 2 * width), I16)] * 2
    outs += [shape((half, d), F32), shape((4, rows + PAD, d), I16)] + [shape((1, rows), F32)] * 2
    own, p1, p3, q2a, q2b, mine, sent, row_loss, col_loss = call(
        functools.partial(weights_kernel, scale, tile),
        outs,
        "weights",
        36,
        in_specs=[vmem] * 12,
        scratch_shapes=[pltpu.VMEM((n_im, n_ks), BF16), pltpu.VMEM((n_im, d), F32)],
    )(*rstats, *cstats, pairs, cols, scores, *ks, im)
    own_key, keep_x, keep_z, to_x, to_z = call(
        key_sum_kernel,
        [shape((rows, d), F32)] + [shape((rows, d // 2), F32)] * 2 + [shape((2, rows + PAD, d // 2), I16)] * 2,
        "key_sum",
        16,
        in_specs=[vmem] * 2,
    )(mine, flip(sent, "core", 2, 1))
    q1, q3 = call(
        relay_kernel, [shape((n_im + PAD, 2 * width), I16)] * 2, "relay", 12, 20 * 10**9, in_specs=[vmem] * 5
    )(own_key, p1, p3, shift(q2a, "y", 4, 1), shift(q2b, "y", 4, 3))
    q1, q3 = shift(q1, "y", 4, 1), shift(q3, "y", 4, 3)
    own_key, to_x, to_z = call(
        key_relay_kernel,
        [shape((rows, d), F32)] + [shape((rows + PAD, d // 2), I16)] * 2,
        "key_relay",
        12,
        in_specs=[vmem] * 5,
    )(own_key, keep_x, keep_z, flip(to_x, "xl", 2, 1), flip(to_z, "zl", 2, 1))
    from_x, from_z = flip(to_x, "xl", 2, 1), flip(to_z, "zl", 2, 1)
    pieces = call(
        image_sum_kernel, shape((8, rows + PAD, width), I16), "image_sum", 12, in_specs=[vmem] * 4
    )(own_key, own, q1, q3)
    pieces = lax.all_to_all(pieces, ("xh", "zh"), 0, 0)
    modality_grad, image_grad = call(
        last_kernel, [shape((rows, d), F32), shape((rows, width), F32)], "last", 8, in_specs=[vmem] * 4
    )(own_key, from_x, from_z, pieces)
    return (image_grad, modality_grad[None], row_loss, col_loss)


def solution(mesh):
    ny = mesh.devices.shape[0] // 2
    nzh = mesh.devices.shape[1] // 8
    names = ("y", "xh", "zh", "zl", "xl", "core")
    fine = Mesh(mesh.devices.reshape(ny, 2, nzh, 2, 2, 2), names)
    mod, rows = names[:2], names[2:]
    in_specs = (P(rows, mod), P(mod, rows, None), P(mod, None))
    out_specs = (P(rows, mod), P(mod, rows, None), P(mod, rows), P(mod, rows))
    return jax.shard_map(
        on_device, mesh=fine, in_specs=in_specs, out_specs=out_specs, check_vma=False
    )
```

```python
import functools
import jax
import jax.numpy as jnp
from jax import lax
from jax.experimental import pallas as pl
from jax.experimental.pallas import tpu as pltpu
from jax.sharding import Mesh, PartitionSpec as P

LAST = (((1,), (1,)), ((), ()))
FIRST = (((0,), (0,)), ((), ()))
F32, BF16, I16 = jnp.float32, jnp.bfloat16, jnp.int16
PAD = 16


def call(kernel, out, name, mib, flops=1000, **kw):
    return pl.pallas_call(
        kernel,
        out_shape=out,
        compiler_params=pltpu.CompilerParams(vmem_limit_bytes=mib * 2**20),
        cost_estimate=pl.CostEstimate(flops=flops, bytes_accessed=1000, transcendentals=0),
        name=name,
        **kw,
    )


def shape(s, t):
    return jax.ShapeDtypeStruct(s, t)


def eye(n):
    return lax.broadcasted_iota(jnp.int32, (n, n), 0) == lax.broadcasted_iota(jnp.int32, (n, n), 1)


def to_lanes(v):
    n = v.shape[0]
    parts = []
    for a in range(0, n, 128):
        w = min(128, n - a)
        parts.append(jnp.sum(jnp.where(eye(w), v[a : a + w], F32(0)), axis=0, keepdims=True))
    return jnp.concatenate(parts, axis=1)


def to_rows(v):
    n = v.shape[1]
    parts = []
    for a in range(0, n, 128):
        w = min(128, n - a)
        parts.append(jnp.sum(jnp.where(eye(w), v[:, a : a + w], F32(0)), axis=1, keepdims=True))
    return jnp.concatenate(parts, axis=0)


def power_of(x):
    top = jnp.max(jnp.abs(x), axis=0, keepdims=True)
    return jnp.ceil(jnp.log2(jnp.maximum(top, F32(1e-30)))) - 14.0


def fixed(x):
    return x.astype(jnp.int32).astype(I16)


def encode(x, ref):
    rows, cols = x.shape
    power = power_of(x)
    ref[:rows, :] = fixed(jnp.round(x * jnp.exp2(-power)))
    ref[rows:, :] = fixed(jnp.broadcast_to(power, (PAD, cols)))


def floats(c):
    return c.astype(jnp.int32).astype(F32)


def decode(c, tiles=1):
    f = floats(c)
    rows = c.shape[-2] - PAD
    n = rows // tiles
    parts = [f[..., i * n : (i + 1) * n, :] * jnp.exp2(f[..., rows + i : rows + i + 1, :]) for i in range(tiles)]
    return parts[0] if tiles == 1 else jnp.concatenate(parts, axis=-2)


def turn_left(v, n):
    lanes = v.shape[1]
    return pltpu.roll(jnp.broadcast_to(v, (8, lanes)), lax.rem(lanes - n, lanes), 1)[0:1]


def pair_kernel(image, twin, both):
    xh = lax.axis_index("xh")
    both[pl.ds(xh, 1)] = image[...][None]
    both[pl.ds(1 - xh, 1)] = twin[...][None]


def prep_kernel(pair_index, keys, after, pairs, cols, keys_out):
    del after
    keys_out[...] = keys[...]
    n_im, n_ks = pairs.shape[1], cols.shape[1]
    rows = n_ks // 8
    zl, xl, core = lax.axis_index("zl"), lax.axis_index("xl"), lax.axis_index("core")
    mine = turn_left(pair_index[...].astype(F32), ((zl * 2 + xl) * 2 + core) * rows)
    pairs[...] = jnp.concatenate([mine[:, a * n_ks : a * n_ks + rows] for a in range(n_im // rows)], axis=1)
    p = lax.broadcasted_iota(jnp.int32, (1, n_ks), 1)
    k = sum((p >= a * rows).astype(jnp.int32) for a in range(1, 8))
    block = ((zl ^ (k >> 1 & 1)) * 2 + (k & 1)) * 2 + (core ^ (k >> 2))
    cols[...] = (lax.axis_index("zh") * n_ks + (block - k) * rows + p).astype(F32)


def join_kernel(own, x, z, d_top, d_low, after, out):
    del after
    rows = own.shape[0]
    xl = lax.axis_index("xl")
    for k, parts in enumerate(((own,), (x,), (z,), (d_top, d_low))):
        at = (k // 2 * 2 + (xl ^ (k % 2))) * rows
        for part in parts:
            n = part.shape[0]
            out[pl.ds(pl.multiple_of(at, 16), n), :] = part[...]
            at += n


def stack_kernel(both, b1, b2, b3, after, out):
    del after
    zh = lax.axis_index("zh")
    for k, ref in enumerate((both, b1, b2, b3)):
        for xh in range(2):
            out[pl.ds(4 * xh + lax.rem(zh + 4 - k, 4), 1)] = ref[xh : xh + 1]


def hold_kernel(keys, after, out):
    del after
    out[...] = keys[...]


def low_kernel(x, after, out):
    del after
    out[...] = x[out.shape[0] :, :]


def top_kernel(z, out):
    out[...] = z[: out.shape[0], :]


def turn_kernel(behind, ahead, half_a, half_b):
    n = half_a.shape[0]
    half_a[...] = behind[:n]
    half_b[...] = ahead[n:]


def beyond_kernel(a, b, out_a, out_b):
    out_a[...] = a[...]
    out_b[...] = b[...]


def scores_kernel(scale, *refs):
    keys, (i0, i1, i3, ia, ib, pairs, cols, s_ref, im, rs, cs) = refs[:2], refs[2:]
    y = lax.axis_index("y")
    nzh, rows, width = ia.shape
    n_im = im.shape[0]
    part = keys[0].shape[0]

    def place(k, xh, ref, first):
        at = pl.multiple_of((lax.rem(y + 4 - k, 4) * 2 + xh) * width, 128)
        for j in range(nzh):
            im[j * rows : (j + 1) * rows, pl.ds(at, width)] = ref[first + j]

    for k, ref in ((0, i0), (1, i1), (3, i3)):
        for xh in range(2):
            place(k, xh, ref, xh * nzh)
    place(2, 0, ia, 0)
    place(2, 1, ib, 0)

    chunk = min(256, part)
    row = [None]

    def stats(c):
        s = s_ref[:, c : c + chunk]
        picked = jnp.where(targets == cols[:, c : c + chunk], s, F32(0))
        top = jnp.max(s, axis=0, keepdims=True)
        cs[0:1, c : c + chunk] = top + jnp.log(jnp.sum(jnp.exp(s - top), axis=0, keepdims=True))
        cs[1:2, c : c + chunk] = jnp.sum(picked, axis=0, keepdims=True)
        top = jnp.max(s, axis=1, keepdims=True)
        pick = jnp.sum(picked, axis=1, keepdims=True)
        if row[0] is None:
            row[0] = (top, jnp.sum(jnp.exp(s - top), axis=1, keepdims=True), pick)
        else:
            old, total, before = row[0]
            new = jnp.maximum(old, top)
            total = total * jnp.exp(old - new) + jnp.sum(jnp.exp(s - new), axis=1, keepdims=True)
            row[0] = (new, total, before + pick)

    targets = to_rows(pairs[...])
    for c in range(0, 2 * part, chunk):
        at = c % part
        s = lax.dot_general(im[...], keys[c // part][at : at + chunk, :], LAST, preferred_element_type=F32)
        s_ref[:, c : c + chunk] = s * scale
        if c:
            stats(c - chunk)
    stats(2 * part - chunk)
    top, total, pick = row[0]
    rs[0:1, :] = to_lanes(top + jnp.log(total))
    rs[1:2, :] = to_lanes(pick)


def merge(parts):
    top = functools.reduce(jnp.maximum, parts)
    return top + jnp.log(sum(jnp.exp(p - top) for p in parts))


def meet(parts):
    return jnp.concatenate([merge([p[0:1] for p in parts]), sum(p[1:2] for p in parts)], axis=0)


def turned(c, n):
    return jnp.concatenate([c[:, (k ^ 1) * n : ((k ^ 1) + 1) * n] for k in range(c.shape[1] // n)], axis=1)


def meet_rows_kernel(r, r_other, out):
    out[...] = meet([r[...], r_other[...]])


def meet_kernel(c, c_other, out):
    out[...] = meet([c[...], turned(c_other[...], c.shape[1] // 2)])


def weights_kernel(scale, tile, *refs):
    rparts, cparts = refs[:2], refs[2:6]
    pairs, cols, s_ref, k0, k1, im, own, p1, p3, o2a, o2b, mine, sent, rl, cl, w_ref, total = refs[6:]
    n_im, n_ks = s_ref.shape
    keys = (k0, k1)
    half, part = n_ks // 2, n_ks // 4
    width = own.shape[1]
    cstat = meet([turned(c[...], part) if k >= 2 else c[...] for k, c in enumerate(cparts)])
    lse_col = cstat[0:1]
    rows = cl.shape[1]
    cl[...] = turn_left(lse_col - cstat[1:2], lax.axis_index("xl") * rows)[:, :rows]
    rstat = meet([r[...] for r in rparts])
    lse_row = rstat[0:1]
    rl[...] = turn_left(lse_row - rstat[1:2], lax.axis_index("zh") * rows)[:, :rows]

    def weigh(a):
        rows = slice(a, a + tile)
        s = s_ref[rows, :]
        two = jnp.where(to_rows(pairs[:, rows]) == cols[...], F32(2), F32(0))
        w = jnp.exp(s - to_rows(lse_row[:, rows])) + jnp.exp(s - lse_col) - two
        w_ref[rows, :] = w.astype(BF16)

    def term(a):
        rows = slice(a, a + tile)
        x = sum(
            jnp.dot(w_ref[rows, k * half : (k + 1) * half], keys[k][...], preferred_element_type=F32) for k in range(2)
        )
        total[rows, :] = x * scale

    tiles = range(0, n_im, tile)
    weigh(0)
    for a in tiles:
        if a + tile < n_im:
            weigh(a + tile)
        term(a)
    for k, out in ((2, None), (1, p1), (3, p3), (0, own)):
        lanes = pl.ds(pl.multiple_of(lax.rem(lax.axis_index("y") + k, 4) * width, 128), width)
        if k == 2:
            encode(total[: n_im // 2, lanes], o2a)
            encode(total[n_im // 2 :, lanes], o2b)
        else:
            out[...] = total[:, lanes]
    other = lax.dot_general(w_ref[:, half:], im[...], FIRST, preferred_element_type=F32) * scale
    for p in range(4):
        encode(other[p * rows : (p + 1) * rows, :], sent.at[p])
    mine[...] = lax.dot_general(w_ref[:, :half], im[...], FIRST, preferred_element_type=F32) * scale


def relay_kernel(after, p1, p3, got_a, got_b, o1, o3):
    del after
    n = p1.shape[0] // 2
    encode(jnp.concatenate([p1[:n, :] + decode(got_a[...]), p1[n:, :]], axis=0), o1)
    encode(jnp.concatenate([p3[:n, :], p3[n:, :] + decode(got_b[...])], axis=0), o3)


def key_sum_kernel(mine, got, own, keep_x, keep_z, to_x, to_z):
    rows, d = own.shape
    n = d // 2
    xl = lax.axis_index("xl")

    def piece(k):
        p = xl ^ k
        return mine[pl.ds(pl.multiple_of(p * rows, 16), rows), :] + decode(got[p])

    x, z, both = piece(1), piece(2), piece(3)
    encode(x[:, :n], to_x.at[0])
    encode(both[:, :n], to_x.at[1])
    encode(z[:, n:], to_z.at[0])
    encode(both[:, n:], to_z.at[1])
    keep_x[...] = x[:, n:]
    keep_z[...] = z[:, :n]
    own[...] = piece(0)


def key_relay_kernel(own, keep_x, keep_z, from_x, from_z, total, to_x, to_z):
    n = keep_x.shape[1]
    total[:, :n] = own[:, :n] + decode(from_x[0])
    total[:, n:] = own[:, n:] + decode(from_z[0])
    encode(keep_z[...] + decode(from_x[1]), to_z)
    encode(keep_x[...] + decode(from_z[1]), to_x)


def last_kernel(own_key, from_x, from_z, pieces, key_out, image_out):
    n = own_key.shape[1] // 2
    key_out[:, :n] = own_key[:, :n] + decode(from_z[...])
    key_out[:, n:] = own_key[:, n:] + decode(from_x[...])
    image_out[...] = sum(decode(pieces[k]) for k in range(pieces.shape[0]))


def image_sum_kernel(after, own, got1, got3, out):
    del after
    out[...] = own[...] + decode(got1[...]) + decode(got3[...])


def image_code_kernel(after_x, after_z, total, out):
    del after_x, after_z
    rows, width = out.shape[1] - PAD, out.shape[2]
    for xh in range(2):
        for zh in range(4):
            encode(total[zh * rows : (zh + 1) * rows, xh * width : (xh + 1) * width], out.at[4 * xh + zh])


def shift(x, axis, n, k):
    return lax.ppermute(x, axis, [(i, (i + k) % n) for i in range(n)])


def flip(x, axis, n, d):
    return lax.ppermute(x, axis, [(i, i ^ d) for i in range(n)])


def on_device(image, modality, pair_index):
    keys = modality[0]
    rows, d = keys.shape
    width = image.shape[1]
    scale = d ** (-0.5)
    nzh = lax.axis_size("zh")
    n_im, n_ks = nzh * rows, 8 * rows
    half = n_ks // 2
    vmem = pl.BlockSpec(memory_space=pltpu.VMEM)
    key_block = shape((rows, d), BF16)
    both = call(pair_kernel, shape((2, rows, width), BF16), "pair", 4, in_specs=[vmem] * 2)(image, flip(image, "xh", 2, 1))
    pairs, cols, held = call(
        prep_kernel, [shape((1, n_im), F32), shape((1, n_ks), F32), key_block], "prep", 8, in_specs=[vmem] * 3
    )(pair_index, keys, both)
    key_x = flip(held, "xl", 2, 1)
    i0 = call(stack_kernel, shape((8, rows, width), BF16), "stack", 8, in_specs=[vmem] * 5)(
        both, *[shift(both, "zh", 4, k) for k in (1, 2, 3)], pairs
    )
    i1, i3 = shift(i0, "y", 4, 1), shift(i0, "y", 4, 3)
    quarter = shape((rows // 2, d), BF16)
    held = call(hold_kernel, key_block, "hold", 8, in_specs=[vmem] * 2)(held, i0)
    key_z = flip(held, "zl", 2, 1)
    d_low = flip(call(low_kernel, quarter, "low", 8, in_specs=[vmem] * 2)(key_x, i0), "zl", 2, 1)
    d_top = flip(call(top_kernel, quarter, "top", 8, in_specs=[vmem])(key_z), "xl", 2, 1)
    half_block = shape((nzh, rows, width), BF16)
    ia, ib = call(turn_kernel, [half_block] * 2, "turn", 12, in_specs=[vmem] * 2)(i1, i3)
    k0 = call(join_kernel, shape((half, d), BF16), "join", 12, in_specs=[vmem] * 6)(
        held, key_x, key_z, d_top, d_low, ia
    )
    ia, ib = call(beyond_kernel, [half_block] * 2, "beyond", 8, 20 * 10**9, in_specs=[vmem] * 2)(
        shift(ia, "y", 4, 1), shift(ib, "y", 4, 3)
    )
    ks = [k0, flip(k0, "core", 2, 1)]

    tile = min(384, n_im)
    scores, im, rs, cs = call(
        functools.partial(scores_kernel, scale),
        [shape((n_im, n_ks), F32), shape((n_im, d), BF16), shape((2, n_im), F32), shape((2, n_ks), F32)],
        "scores",
        28,
        in_specs=[vmem] * 9,
    )(*ks, i0, i1, i3, ia, ib, pairs, cols)
    rs = call(meet_rows_kernel, shape((2, n_im), F32), "meet_rows", 4, in_specs=[vmem] * 2)(rs, flip(rs, "zh", 4, 1))
    rstats = [rs, flip(rs, "zh", 4, 3)]
    cs = call(meet_kernel, shape((2, n_ks), F32), "meet", 4, in_specs=[vmem] * 2)(cs, flip(cs, "core", 2, 1))
    cstats = [cs] + [lax.ppermute(cs, ("zl", "xl"), [(i, i ^ k) for i in range(4)]) for k in (1, 2, 3)]
    outs = [shape((n_im, 2 * width), F32)] * 3 + [shape((n_im // 2 + PAD, 2 * width), I16)] * 2
    outs += [shape((half, d), F32), shape((4, rows + PAD, d), I16)] + [shape((1, rows), F32)] * 2
    own, p1, p3, q2a, q2b, mine, sent, row_loss, col_loss = call(
        functools.partial(weights_kernel, scale, tile),
        outs,
        "weights",
        36,
        in_specs=[vmem] * 12,
        scratch_shapes=[pltpu.VMEM((n_im, n_ks), BF16), pltpu.VMEM((n_im, d), F32)],
    )(*rstats, *cstats, pairs, cols, scores, *ks, im)
    own_key, keep_x, keep_z, to_x, to_z = call(
        key_sum_kernel,
        [shape((rows, d), F32)] + [shape((rows, d // 2), F32)] * 2 + [shape((2, rows + PAD, d // 2), I16)] * 2,
        "key_sum",
        16,
        in_specs=[vmem] * 2,
    )(mine, flip(sent, "core", 2, 1))
    q1, q3 = call(
        relay_kernel, [shape((n_im + PAD, 2 * width), I16)] * 2, "relay", 12, 20 * 10**9, in_specs=[vmem] * 5
    )(own_key, p1, p3, shift(q2a, "y", 4, 1), shift(q2b, "y", 4, 3))
    q1, q3 = shift(q1, "y", 4, 1), shift(q3, "y", 4, 3)
    own_key, to_x, to_z = call(
        key_relay_kernel,
        [shape((rows, d), F32)] + [shape((rows + PAD, d // 2), I16)] * 2,
        "key_relay",
        12,
        in_specs=[vmem] * 5,
    )(own_key, keep_x, keep_z, flip(to_x, "xl", 2, 1), flip(to_z, "zl", 2, 1))
    from_x, from_z = flip(to_x, "xl", 2, 1), flip(to_z, "zl", 2, 1)
    total = call(image_sum_kernel, shape((n_im, 2 * width), F32), "image_sum", 12, in_specs=[vmem] * 4)(
        own_key, own, q1, q3
    )
    pieces = call(image_code_kernel, shape((8, rows + PAD, width), I16), "image_code", 12, in_specs=[vmem] * 3)(
        from_x, from_z, total
    )
    pieces = lax.all_to_all(pieces, ("xh", "zh"), 0, 0)
    modality_grad, image_grad = call(
        last_kernel, [shape((rows, d), F32), shape((rows, width), F32)], "last", 8, in_specs=[vmem] * 4
    )(own_key, from_x, from_z, pieces)
    return (image_grad, modality_grad[None], row_loss, col_loss)


def solution(mesh):
    ny = mesh.devices.shape[0] // 2
    nzh = mesh.devices.shape[1] // 8
    names = ("y", "xh", "zh", "zl", "xl", "core")
    fine = Mesh(mesh.devices.reshape(ny, 2, nzh, 2, 2, 2), names)
    mod, rows = names[:2], names[2:]
    in_specs = (P(rows, mod), P(mod, rows, None), P(mod, None))
    out_specs = (P(rows, mod), P(mod, rows, None), P(mod, rows), P(mod, rows))
    return jax.shard_map(
        on_device, mesh=fine, in_specs=in_specs, out_specs=out_specs, check_vma=False
    )
```

```python
import functools
import jax
import jax.numpy as jnp
from jax import lax
from jax.experimental import pallas as pl
from jax.experimental.pallas import tpu as pltpu
from jax.sharding import Mesh, PartitionSpec as P

LAST = (((1,), (1,)), ((), ()))
FIRST = (((0,), (0,)), ((), ()))
F32, BF16, I16 = jnp.float32, jnp.bfloat16, jnp.int16
PAD = 16


def call(kernel, out, name, mib, flops=1000, **kw):
    return pl.pallas_call(
        kernel,
        out_shape=out,
        compiler_params=pltpu.CompilerParams(vmem_limit_bytes=mib * 2**20),
        cost_estimate=pl.CostEstimate(flops=flops, bytes_accessed=1000, transcendentals=0),
        name=name,
        **kw,
    )


def shape(s, t):
    return jax.ShapeDtypeStruct(s, t)


def eye(n):
    return lax.broadcasted_iota(jnp.int32, (n, n), 0) == lax.broadcasted_iota(jnp.int32, (n, n), 1)


def to_lanes(v):
    n = v.shape[0]
    parts = []
    for a in range(0, n, 128):
        w = min(128, n - a)
        parts.append(jnp.sum(jnp.where(eye(w), v[a : a + w], F32(0)), axis=0, keepdims=True))
    return jnp.concatenate(parts, axis=1)


def to_rows(v):
    n = v.shape[1]
    parts = []
    for a in range(0, n, 128):
        w = min(128, n - a)
        parts.append(jnp.sum(jnp.where(eye(w), v[:, a : a + w], F32(0)), axis=1, keepdims=True))
    return jnp.concatenate(parts, axis=0)


def power_of(x):
    top = jnp.max(jnp.abs(x), axis=0, keepdims=True)
    return jnp.ceil(jnp.log2(jnp.maximum(top, F32(1e-30)))) - 14.0


def fixed(x):
    return x.astype(jnp.int32).astype(I16)


def encode(x, ref):
    rows, cols = x.shape
    power = power_of(x)
    ref[:rows, :] = fixed(jnp.round(x * jnp.exp2(-power)))
    ref[rows:, :] = fixed(jnp.broadcast_to(power, (PAD, cols)))


def floats(c):
    return c.astype(jnp.int32).astype(F32)


def decode(c, tiles=1):
    f = floats(c)
    rows = c.shape[-2] - PAD
    n = rows // tiles
    parts = [f[..., i * n : (i + 1) * n, :] * jnp.exp2(f[..., rows + i : rows + i + 1, :]) for i in range(tiles)]
    return parts[0] if tiles == 1 else jnp.concatenate(parts, axis=-2)


def turn_left(v, n):
    lanes = v.shape[1]
    return pltpu.roll(jnp.broadcast_to(v, (8, lanes)), lax.rem(lanes - n, lanes), 1)[0:1]


def pair_kernel(image, twin, both):
    xh = lax.axis_index("xh")
    both[pl.ds(xh, 1)] = image[...][None]
    both[pl.ds(1 - xh, 1)] = twin[...][None]


def prep_kernel(pair_index, keys, after, pairs, cols, keys_out):
    del after
    keys_out[...] = keys[...]
    n_im, n_ks = pairs.shape[1], cols.shape[1]
    rows = n_ks // 8
    zl, xl, core = lax.axis_index("zl"), lax.axis_index("xl"), lax.axis_index("core")
    mine = turn_left(pair_index[...].astype(F32), ((zl * 2 + xl) * 2 + core) * rows)
    pairs[...] = jnp.concatenate([mine[:, a * n_ks : a * n_ks + rows] for a in range(n_im // rows)], axis=1)
    p = lax.broadcasted_iota(jnp.int32, (1, n_ks), 1)
    k = sum((p >= a * rows).astype(jnp.int32) for a in range(1, 8))
    block = ((zl ^ (k >> 1 & 1)) * 2 + (k & 1)) * 2 + (core ^ (k >> 2))
    cols[...] = (lax.axis_index("zh") * n_ks + (block - k) * rows + p).astype(F32)


def join_kernel(own, x, z, d_top, d_low, after, out):
    del after
    rows = own.shape[0]
    xl = lax.axis_index("xl")
    for k, parts in enumerate(((own,), (x,), (z,), (d_top, d_low))):
        at = (k // 2 * 2 + (xl ^ (k % 2))) * rows
        for part in parts:
            n = part.shape[0]
            out[pl.ds(pl.multiple_of(at, 16), n), :] = part[...]
            at += n


def stack_kernel(both, b1, b2, b3, after, out):
    del after
    zh = lax.axis_index("zh")
    for k, ref in enumerate((both, b1, b2, b3)):
        for xh in range(2):
            out[pl.ds(4 * xh + lax.rem(zh + 4 - k, 4), 1)] = ref[xh : xh + 1]


def hold_kernel(keys, after, out):
    del after
    out[...] = keys[...]


def low_kernel(x, after, out):
    del after
    out[...] = x[out.shape[0] :, :]


def top_kernel(z, out):
    out[...] = z[: out.shape[0], :]


def turn_kernel(behind, ahead, half_a, half_b):
    n = half_a.shape[0]
    half_a[...] = behind[:n]
    half_b[...] = ahead[n:]


def beyond_kernel(a, b, out_a, out_b):
    out_a[...] = a[...]
    out_b[...] = b[...]


def scores_kernel(scale, *refs):
    keys, (i0, i1, i3, ia, ib, pairs, cols, s_ref, im, rs, cs) = refs[:2], refs[2:]
    y = lax.axis_index("y")
    nzh, rows, width = ia.shape
    n_im = im.shape[0]
    part = keys[0].shape[0]

    def place(k, xh, ref, first):
        at = pl.multiple_of((lax.rem(y + 4 - k, 4) * 2 + xh) * width, 128)
        for j in range(nzh):
            im[j * rows : (j + 1) * rows, pl.ds(at, width)] = ref[first + j]

    for k, ref in ((0, i0), (1, i1), (3, i3)):
        for xh in range(2):
            place(k, xh, ref, xh * nzh)
    place(2, 0, ia, 0)
    place(2, 1, ib, 0)

    chunk = min(256, part)
    row = [None]

    def stats(c):
        s = s_ref[:, c : c + chunk]
        picked = jnp.where(targets == cols[:, c : c + chunk], s, F32(0))
        top = jnp.max(s, axis=0, keepdims=True)
        cs[0:1, c : c + chunk] = top + jnp.log(jnp.sum(jnp.exp(s - top), axis=0, keepdims=True))
        cs[1:2, c : c + chunk] = jnp.sum(picked, axis=0, keepdims=True)
        top = jnp.max(s, axis=1, keepdims=True)
        pick = jnp.sum(picked, axis=1, keepdims=True)
        if row[0] is None:
            row[0] = (top, jnp.sum(jnp.exp(s - top), axis=1, keepdims=True), pick)
        else:
            old, total, before = row[0]
            new = jnp.maximum(old, top)
            total = total * jnp.exp(old - new) + jnp.sum(jnp.exp(s - new), axis=1, keepdims=True)
            row[0] = (new, total, before + pick)

    targets = to_rows(pairs[...])
    for c in range(0, 2 * part, chunk):
        at = c % part
        s = lax.dot_general(im[...], keys[c // part][at : at + chunk, :], LAST, preferred_element_type=F32)
        s_ref[:, c : c + chunk] = s * scale
        if c:
            stats(c - chunk)
    stats(2 * part - chunk)
    top, total, pick = row[0]
    rs[0:1, :] = to_lanes(top + jnp.log(total))
    rs[1:2, :] = to_lanes(pick)


def merge(parts):
    top = functools.reduce(jnp.maximum, parts)
    return top + jnp.log(sum(jnp.exp(p - top) for p in parts))


def meet(parts):
    return jnp.concatenate([merge([p[0:1] for p in parts]), sum(p[1:2] for p in parts)], axis=0)


def turned(c, n):
    return jnp.concatenate([c[:, (k ^ 1) * n : ((k ^ 1) + 1) * n] for k in range(c.shape[1] // n)], axis=1)


def meet_rows_kernel(r, r_other, out):
    out[...] = meet([r[...], r_other[...]])


def meet_kernel(c, c_other, out):
    out[...] = meet([c[...], turned(c_other[...], c.shape[1] // 2)])


def weights_kernel(scale, tile, *refs):
    rparts, cparts = refs[:2], refs[2:6]
    pairs, cols, s_ref, k0, k1, im, own, p1, p3, o2a, o2b, mine, sent, rl, cl, w_ref, total = refs[6:]
    n_im, n_ks = s_ref.shape
    keys = (k0, k1)
    half, part = n_ks // 2, n_ks // 4
    width = own.shape[1]
    cstat = meet([turned(c[...], part) if k >= 2 else c[...] for k, c in enumerate(cparts)])
    lse_col = cstat[0:1]
    rows = cl.shape[1]
    cl[...] = turn_left(lse_col - cstat[1:2], lax.axis_index("xl") * rows)[:, :rows]
    rstat = meet([r[...] for r in rparts])
    lse_row = rstat[0:1]
    rl[...] = turn_left(lse_row - rstat[1:2], lax.axis_index("zh") * rows)[:, :rows]

    def weigh(a):
        rows = slice(a, a + tile)
        s = s_ref[rows, :]
        two = jnp.where(to_rows(pairs[:, rows]) == cols[...], F32(2), F32(0))
        w = jnp.exp(s - to_rows(lse_row[:, rows])) + jnp.exp(s - lse_col) - two
        w_ref[rows, :] = w.astype(BF16)

    def term(a):
        rows = slice(a, a + tile)
        x = sum(
            jnp.dot(w_ref[rows, k * half : (k + 1) * half], keys[k][...], preferred_element_type=F32) for k in range(2)
        )
        total[rows, :] = x * scale

    tiles = range(0, n_im, tile)
    weigh(0)
    for a in tiles:
        if a + tile < n_im:
            weigh(a + tile)
        term(a)
    for k, out in ((2, None), (1, p1), (3, p3), (0, own)):
        lanes = pl.ds(pl.multiple_of(lax.rem(lax.axis_index("y") + k, 4) * width, 128), width)
        if k == 2:
            encode(total[: n_im // 2, lanes], o2a)
            encode(total[n_im // 2 :, lanes], o2b)
        else:
            out[...] = total[:, lanes]
    other = lax.dot_general(w_ref[:, half:], im[...], FIRST, preferred_element_type=F32) * scale
    for p in range(4):
        encode(other[p * rows : (p + 1) * rows, :], sent.at[p])
    mine[...] = lax.dot_general(w_ref[:, :half], im[...], FIRST, preferred_element_type=F32) * scale


def relay_kernel(after, p1, p3, got_a, got_b, o1, o3):
    del after
    n = p1.shape[0] // 2
    encode(jnp.concatenate([p1[:n, :] + decode(got_a[...]), p1[n:, :]], axis=0), o1)
    encode(jnp.concatenate([p3[:n, :], p3[n:, :] + decode(got_b[...])], axis=0), o3)


def key_sum_kernel(mine, got, own, keep_x, keep_z, to_x, to_z):
    rows, d = own.shape
    n = d // 2
    xl = lax.axis_index("xl")

    def piece(k):
        p = xl ^ k
        return mine[pl.ds(pl.multiple_of(p * rows, 16), rows), :] + decode(got[p])

    x, z, both = piece(1), piece(2), piece(3)
    encode(x[:, :n], to_x.at[0])
    encode(both[:, :n], to_x.at[1])
    encode(z[:, n:], to_z.at[0])
    encode(both[:, n:], to_z.at[1])
    keep_x[...] = x[:, n:]
    keep_z[...] = z[:, :n]
    own[...] = piece(0)


def key_relay_kernel(own, keep_x, keep_z, from_x, from_z, total, to_x, to_z):
    n = keep_x.shape[1]
    total[:, :n] = own[:, :n] + decode(from_x[0])
    total[:, n:] = own[:, n:] + decode(from_z[0])
    encode(keep_z[...] + decode(from_x[1]), to_z)
    encode(keep_x[...] + decode(from_z[1]), to_x)


def last_kernel(own_key, from_x, from_z, pieces, key_out, image_out):
    n = own_key.shape[1] // 2
    key_out[:, :n] = own_key[:, :n] + decode(from_z[...])
    key_out[:, n:] = own_key[:, n:] + decode(from_x[...])
    image_out[...] = sum(decode(pieces[k]) for k in range(pieces.shape[0]))


def image_sum_kernel(after, own, got1, got3, out):
    del after
    out[...] = own[...] + decode(got1[...]) + decode(got3[...])


def image_code_kernel(after_x, after_z, total, out):
    del after_x, after_z
    rows, width = out.shape[1] - PAD, out.shape[2]
    for xh in range(2):
        for zh in range(4):
            encode(total[zh * rows : (zh + 1) * rows, xh * width : (xh + 1) * width], out.at[4 * xh + zh])


def shift(x, axis, n, k):
    return lax.ppermute(x, axis, [(i, (i + k) % n) for i in range(n)])


def flip(x, axis, n, d):
    return lax.ppermute(x, axis, [(i, i ^ d) for i in range(n)])


def on_device(image, modality, pair_index):
    keys = modality[0]
    rows, d = keys.shape
    width = image.shape[1]
    scale = d ** (-0.5)
    nzh = lax.axis_size("zh")
    n_im, n_ks = nzh * rows, 8 * rows
    half = n_ks // 2
    vmem = pl.BlockSpec(memory_space=pltpu.VMEM)
    key_block = shape((rows, d), BF16)
    both = call(pair_kernel, shape((2, rows, width), BF16), "pair", 4, in_specs=[vmem] * 2)(image, flip(image, "xh", 2, 1))
    pairs, cols, held = call(
        prep_kernel, [shape((1, n_im), F32), shape((1, n_ks), F32), key_block], "prep", 8, in_specs=[vmem] * 3
    )(pair_index, keys, both)
    key_x = flip(held, "xl", 2, 1)
    i0 = call(stack_kernel, shape((8, rows, width), BF16), "stack", 8, in_specs=[vmem] * 5)(
        both, *[shift(both, "zh", 4, k) for k in (1, 2, 3)], pairs
    )
    i1, i3 = shift(i0, "y", 4, 1), shift(i0, "y", 4, 3)
    quarter = shape((rows // 2, d), BF16)
    held = call(hold_kernel, key_block, "hold", 8, in_specs=[vmem] * 2)(held, i0)
    key_z = flip(held, "zl", 2, 1)
    d_low = flip(call(low_kernel, quarter, "low", 8, in_specs=[vmem] * 2)(key_x, i0), "zl", 2, 1)
    d_top = flip(call(top_kernel, quarter, "top", 8, in_specs=[vmem])(key_z), "xl", 2, 1)
    half_block = shape((nzh, rows, width), BF16)
    ia, ib = call(turn_kernel, [half_block] * 2, "turn", 12, in_specs=[vmem] * 2)(i1, i3)
    k0 = call(join_kernel, shape((half, d), BF16), "join", 12, in_specs=[vmem] * 6)(
        held, key_x, key_z, d_top, d_low, ia
    )
    ia, ib = call(beyond_kernel, [half_block] * 2, "beyond", 8, 20 * 10**9, in_specs=[vmem] * 2)(
        shift(ia, "y", 4, 1), shift(ib, "y", 4, 3)
    )
    ks = [k0, flip(k0, "core", 2, 1)]

    tile = n_im
    scores, im, rs, cs = call(
        functools.partial(scores_kernel, scale),
        [shape((n_im, n_ks), F32), shape((n_im, d), BF16), shape((2, n_im), F32), shape((2, n_ks), F32)],
        "scores",
        28,
        in_specs=[vmem] * 9,
    )(*ks, i0, i1, i3, ia, ib, pairs, cols)
    rs = call(meet_rows_kernel, shape((2, n_im), F32), "meet_rows", 4, in_specs=[vmem] * 2)(rs, flip(rs, "zh", 4, 1))
    rstats = [rs, flip(rs, "zh", 4, 3)]
    cs = call(meet_kernel, shape((2, n_ks), F32), "meet", 4, in_specs=[vmem] * 2)(cs, flip(cs, "core", 2, 1))
    cstats = [cs] + [lax.ppermute(cs, ("zl", "xl"), [(i, i ^ k) for i in range(4)]) for k in (1, 2, 3)]
    outs = [shape((n_im, 2 * width), F32)] * 3 + [shape((n_im // 2 + PAD, 2 * width), I16)] * 2
    outs += [shape((half, d), F32), shape((4, rows + PAD, d), I16)] + [shape((1, rows), F32)] * 2
    own, p1, p3, q2a, q2b, mine, sent, row_loss, col_loss = call(
        functools.partial(weights_kernel, scale, tile),
        outs,
        "weights",
        36,
        in_specs=[vmem] * 12,
        scratch_shapes=[pltpu.VMEM((n_im, n_ks), BF16), pltpu.VMEM((n_im, d), F32)],
    )(*rstats, *cstats, pairs, cols, scores, *ks, im)
    own_key, keep_x, keep_z, to_x, to_z = call(
        key_sum_kernel,
        [shape((rows, d), F32)] + [shape((rows, d // 2), F32)] * 2 + [shape((2, rows + PAD, d // 2), I16)] * 2,
        "key_sum",
        16,
        in_specs=[vmem] * 2,
    )(mine, flip(sent, "core", 2, 1))
    q1, q3 = call(
        relay_kernel, [shape((n_im + PAD, 2 * width), I16)] * 2, "relay", 12, 20 * 10**9, in_specs=[vmem] * 5
    )(own_key, p1, p3, shift(q2a, "y", 4, 1), shift(q2b, "y", 4, 3))
    q1, q3 = shift(q1, "y", 4, 1), shift(q3, "y", 4, 3)
    own_key, to_x, to_z = call(
        key_relay_kernel,
        [shape((rows, d), F32)] + [shape((rows + PAD, d // 2), I16)] * 2,
        "key_relay",
        12,
        in_specs=[vmem] * 5,
    )(own_key, keep_x, keep_z, flip(to_x, "xl", 2, 1), flip(to_z, "zl", 2, 1))
    from_x, from_z = flip(to_x, "xl", 2, 1), flip(to_z, "zl", 2, 1)
    total = call(image_sum_kernel, shape((n_im, 2 * width), F32), "image_sum", 12, in_specs=[vmem] * 4)(
        own_key, own, q1, q3
    )
    pieces = call(image_code_kernel, shape((8, rows + PAD, width), I16), "image_code", 12, in_specs=[vmem] * 3)(
        from_x, from_z, total
    )
    pieces = lax.all_to_all(pieces, ("xh", "zh"), 0, 0)
    modality_grad, image_grad = call(
        last_kernel, [shape((rows, d), F32), shape((rows, width), F32)], "last", 8, in_specs=[vmem] * 4
    )(own_key, from_x, from_z, pieces)
    return (image_grad, modality_grad[None], row_loss, col_loss)


def solution(mesh):
    ny = mesh.devices.shape[0] // 2
    nzh = mesh.devices.shape[1] // 8
    names = ("y", "xh", "zh", "zl", "xl", "core")
    fine = Mesh(mesh.devices.reshape(ny, 2, nzh, 2, 2, 2), names)
    mod, rows = names[:2], names[2:]
    in_specs = (P(rows, mod), P(mod, rows, None), P(mod, None))
    out_specs = (P(rows, mod), P(mod, rows, None), P(mod, rows), P(mod, rows))
    return jax.shard_map(
        on_device, mesh=fine, in_specs=in_specs, out_specs=out_specs, check_vma=False
    )
```

```python
import functools
import jax
import jax.numpy as jnp
from jax import lax
from jax.experimental import pallas as pl
from jax.experimental.pallas import tpu as pltpu
from jax.sharding import Mesh, PartitionSpec as P

LAST = (((1,), (1,)), ((), ()))
FIRST = (((0,), (0,)), ((), ()))
F32, BF16, I16 = jnp.float32, jnp.bfloat16, jnp.int16
PAD = 16


def call(kernel, out, name, mib, flops=1000, **kw):
    return pl.pallas_call(
        kernel,
        out_shape=out,
        compiler_params=pltpu.CompilerParams(vmem_limit_bytes=mib * 2**20),
        cost_estimate=pl.CostEstimate(flops=flops, bytes_accessed=1000, transcendentals=0),
        name=name,
        **kw,
    )


def shape(s, t):
    return jax.ShapeDtypeStruct(s, t)


def eye(n):
    return lax.broadcasted_iota(jnp.int32, (n, n), 0) == lax.broadcasted_iota(jnp.int32, (n, n), 1)


def to_lanes(v):
    n = v.shape[0]
    parts = []
    for a in range(0, n, 128):
        w = min(128, n - a)
        parts.append(jnp.sum(jnp.where(eye(w), v[a : a + w], F32(0)), axis=0, keepdims=True))
    return jnp.concatenate(parts, axis=1)


def to_rows(v):
    n = v.shape[1]
    parts = []
    for a in range(0, n, 128):
        w = min(128, n - a)
        parts.append(jnp.sum(jnp.where(eye(w), v[:, a : a + w], F32(0)), axis=1, keepdims=True))
    return jnp.concatenate(parts, axis=0)


def power_of(x):
    top = jnp.max(jnp.abs(x), axis=0, keepdims=True)
    return jnp.ceil(jnp.log2(jnp.maximum(top, F32(1e-30)))) - 14.0


def fixed(x):
    return x.astype(jnp.int32).astype(I16)


def encode(x, ref):
    rows, cols = x.shape
    power = power_of(x)
    ref[:rows, :] = fixed(jnp.round(x * jnp.exp2(-power)))
    ref[rows:, :] = fixed(jnp.broadcast_to(power, (PAD, cols)))


def floats(c):
    return c.astype(jnp.int32).astype(F32)


def decode(c, tiles=1):
    f = floats(c)
    rows = c.shape[-2] - PAD
    n = rows // tiles
    parts = [f[..., i * n : (i + 1) * n, :] * jnp.exp2(f[..., rows + i : rows + i + 1, :]) for i in range(tiles)]
    return parts[0] if tiles == 1 else jnp.concatenate(parts, axis=-2)


def turn_left(v, n):
    lanes = v.shape[1]
    return pltpu.roll(jnp.broadcast_to(v, (8, lanes)), lax.rem(lanes - n, lanes), 1)[0:1]


def pair_kernel(image, twin, both):
    xh = lax.axis_index("xh")
    both[pl.ds(xh, 1)] = image[...][None]
    both[pl.ds(1 - xh, 1)] = twin[...][None]


def prep_kernel(pair_index, keys, after, pairs, cols, keys_out):
    del after
    keys_out[...] = keys[...]
    n_im, n_ks = pairs.shape[1], cols.shape[1]
    rows = n_ks // 8
    zl, xl, core = lax.axis_index("zl"), lax.axis_index("xl"), lax.axis_index("core")
    mine = turn_left(pair_index[...].astype(F32), ((zl * 2 + xl) * 2 + core) * rows)
    pairs[...] = jnp.concatenate([mine[:, a * n_ks : a * n_ks + rows] for a in range(n_im // rows)], axis=1)
    p = lax.broadcasted_iota(jnp.int32, (1, n_ks), 1)
    k = sum((p >= a * rows).astype(jnp.int32) for a in range(1, 8))
    block = ((zl ^ (k >> 1 & 1)) * 2 + (k & 1)) * 2 + (core ^ (k >> 2))
    cols[...] = (lax.axis_index("zh") * n_ks + (block - k) * rows + p).astype(F32)


def join_kernel(own, x, z, d_top, d_low, after, out):
    del after
    rows = own.shape[0]
    xl = lax.axis_index("xl")
    for k, parts in enumerate(((own,), (x,), (z,), (d_top, d_low))):
        at = (k // 2 * 2 + (xl ^ (k % 2))) * rows
        for part in parts:
            n = part.shape[0]
            out[pl.ds(pl.multiple_of(at, 16), n), :] = part[...]
            at += n


def stack_kernel(both, b1, b2, b3, after, out):
    del after
    zh = lax.axis_index("zh")
    for k, ref in enumerate((both, b1, b2, b3)):
        for xh in range(2):
            out[pl.ds(4 * xh + lax.rem(zh + 4 - k, 4), 1)] = ref[xh : xh + 1]


def hold_kernel(keys, after, out):
    del after
    out[...] = keys[...]


def low_kernel(x, after, out):
    del after
    out[...] = x[out.shape[0] :, :]


def top_kernel(z, out):
    out[...] = z[: out.shape[0], :]


def turn_kernel(behind, ahead, half_a, half_b):
    n = half_a.shape[0]
    half_a[...] = behind[:n]
    half_b[...] = ahead[n:]


def beyond_kernel(a, b, out_a, out_b):
    out_a[...] = a[...]
    out_b[...] = b[...]


def scores_kernel(scale, *refs):
    keys, (i0, i1, i3, ia, ib, pairs, cols, s_ref, im, rs, cs) = refs[:2], refs[2:]
    y = lax.axis_index("y")
    nzh, rows, width = ia.shape
    n_im = im.shape[0]
    part = keys[0].shape[0]

    def place(k, xh, ref, first):
        at = pl.multiple_of((lax.rem(y + 4 - k, 4) * 2 + xh) * width, 128)
        for j in range(nzh):
            im[j * rows : (j + 1) * rows, pl.ds(at, width)] = ref[first + j]

    for k, ref in ((0, i0), (1, i1), (3, i3)):
        for xh in range(2):
            place(k, xh, ref, xh * nzh)
    place(2, 0, ia, 0)
    place(2, 1, ib, 0)

    chunk = min(256, part)
    row = [None]

    def stats(c):
        s = s_ref[:, c : c + chunk]
        picked = jnp.where(targets == cols[:, c : c + chunk], s, F32(0))
        top = jnp.max(s, axis=0, keepdims=True)
        cs[0:1, c : c + chunk] = top + jnp.log(jnp.sum(jnp.exp(s - top), axis=0, keepdims=True))
        cs[1:2, c : c + chunk] = jnp.sum(picked, axis=0, keepdims=True)
        top = jnp.max(s, axis=1, keepdims=True)
        pick = jnp.sum(picked, axis=1, keepdims=True)
        if row[0] is None:
            row[0] = (top, jnp.sum(jnp.exp(s - top), axis=1, keepdims=True), pick)
        else:
            old, total, before = row[0]
            new = jnp.maximum(old, top)
            total = total * jnp.exp(old - new) + jnp.sum(jnp.exp(s - new), axis=1, keepdims=True)
            row[0] = (new, total, before + pick)

    targets = to_rows(pairs[...])
    for c in range(0, 2 * part, chunk):
        at = c % part
        s = lax.dot_general(im[...], keys[c // part][at : at + chunk, :], LAST, preferred_element_type=F32)
        s_ref[:, c : c + chunk] = s * scale
        if c:
            stats(c - chunk)
    stats(2 * part - chunk)
    top, total, pick = row[0]
    rs[0:1, :] = to_lanes(top + jnp.log(total))
    rs[1:2, :] = to_lanes(pick)


def merge(parts):
    top = functools.reduce(jnp.maximum, parts)
    return top + jnp.log(sum(jnp.exp(p - top) for p in parts))


def meet(parts):
    return jnp.concatenate([merge([p[0:1] for p in parts]), sum(p[1:2] for p in parts)], axis=0)


def turned(c, n):
    return jnp.concatenate([c[:, (k ^ 1) * n : ((k ^ 1) + 1) * n] for k in range(c.shape[1] // n)], axis=1)


def meet_rows_kernel(r, r_other, out):
    out[...] = meet([r[...], r_other[...]])


def meet_kernel(c, c_other, out):
    out[...] = meet([c[...], turned(c_other[...], c.shape[1] // 2)])


def weights_kernel(scale, tile, *refs):
    rparts, cparts = refs[:2], refs[2:6]
    pairs, cols, s_ref, k0, k1, im, own, p1, p3, o2a, o2b, mine, sent, rl, cl, w_ref, total = refs[6:]
    n_im, n_ks = s_ref.shape
    keys = (k0, k1)
    half, part = n_ks // 2, n_ks // 4
    width = own.shape[1]
    cstat = meet([turned(c[...], part) if k >= 2 else c[...] for k, c in enumerate(cparts)])
    lse_col = cstat[0:1]
    rows = cl.shape[1]
    cl[...] = turn_left(lse_col - cstat[1:2], lax.axis_index("xl") * rows)[:, :rows]
    rstat = meet([r[...] for r in rparts])
    lse_row = rstat[0:1]
    rl[...] = turn_left(lse_row - rstat[1:2], lax.axis_index("zh") * rows)[:, :rows]

    def weigh(a):
        rows = slice(a, a + tile)
        s = s_ref[rows, :]
        two = jnp.where(to_rows(pairs[:, rows]) == cols[...], F32(2), F32(0))
        w = jnp.exp(s - to_rows(lse_row[:, rows])) + jnp.exp(s - lse_col) - two
        w_ref[rows, :] = w.astype(BF16)

    def term(a):
        rows = slice(a, a + tile)
        x = sum(
            jnp.dot(w_ref[rows, k * half : (k + 1) * half], keys[k][...], preferred_element_type=F32) for k in range(2)
        )
        total[rows, :] = x * scale

    tiles = range(0, n_im, tile)
    weigh(0)
    for a in tiles:
        if a + tile < n_im:
            weigh(a + tile)
        term(a)
    for k, out in ((2, None), (1, p1), (3, p3), (0, own)):
        lanes = pl.ds(pl.multiple_of(lax.rem(lax.axis_index("y") + k, 4) * width, 128), width)
        if k == 2:
            encode(total[: n_im // 2, lanes], o2a)
            encode(total[n_im // 2 :, lanes], o2b)
        else:
            out[...] = total[:, lanes]
    other = lax.dot_general(w_ref[:, half:], im[...], FIRST, preferred_element_type=F32) * scale
    for p in range(4):
        encode(other[p * rows : (p + 1) * rows, :], sent.at[p])
    mine[...] = lax.dot_general(w_ref[:, :half], im[...], FIRST, preferred_element_type=F32) * scale


def relay_kernel(after, p1, p3, got_a, got_b, o1, o3):
    del after
    n = p1.shape[0] // 2
    encode(jnp.concatenate([p1[:n, :] + decode(got_a[...]), p1[n:, :]], axis=0), o1)
    encode(jnp.concatenate([p3[:n, :], p3[n:, :] + decode(got_b[...])], axis=0), o3)


def key_sum_kernel(mine, got, own, keep_x, keep_z, to_x, to_z):
    rows, d = own.shape
    n = d // 2
    xl = lax.axis_index("xl")

    def piece(k):
        p = xl ^ k
        return mine[pl.ds(pl.multiple_of(p * rows, 16), rows), :] + decode(got[p])

    x, z, both = piece(1), piece(2), piece(3)
    encode(x[:, :n], to_x.at[0])
    encode(both[:, :n], to_x.at[1])
    encode(z[:, n:], to_z.at[0])
    encode(both[:, n:], to_z.at[1])
    keep_x[...] = x[:, n:]
    keep_z[...] = z[:, :n]
    own[...] = piece(0)


def key_relay_kernel(own, keep_x, keep_z, from_x, from_z, total, to_x, to_z):
    n = keep_x.shape[1]
    total[:, :n] = own[:, :n] + decode(from_x[0])
    total[:, n:] = own[:, n:] + decode(from_z[0])
    encode(keep_z[...] + decode(from_x[1]), to_z)
    encode(keep_x[...] + decode(from_z[1]), to_x)


def last_kernel(own_key, from_x, from_z, pieces, key_out, image_out):
    n = own_key.shape[1] // 2
    key_out[:, :n] = own_key[:, :n] + decode(from_z[...])
    key_out[:, n:] = own_key[:, n:] + decode(from_x[...])
    image_out[...] = sum(decode(pieces[k]) for k in range(pieces.shape[0]))


def image_sum_kernel(after, own, got1, got3, out):
    del after
    out[...] = own[...] + decode(got1[...]) + decode(got3[...])


def image_code_kernel(after, total, out):
    del after
    rows, width = out.shape[1] - PAD, out.shape[2]
    for xh in range(2):
        for zh in range(4):
            encode(total[zh * rows : (zh + 1) * rows, xh * width : (xh + 1) * width], out.at[4 * xh + zh])


def shift(x, axis, n, k):
    return lax.ppermute(x, axis, [(i, (i + k) % n) for i in range(n)])


def flip(x, axis, n, d):
    return lax.ppermute(x, axis, [(i, i ^ d) for i in range(n)])


def on_device(image, modality, pair_index):
    keys = modality[0]
    rows, d = keys.shape
    width = image.shape[1]
    scale = d ** (-0.5)
    nzh = lax.axis_size("zh")
    n_im, n_ks = nzh * rows, 8 * rows
    half = n_ks // 2
    vmem = pl.BlockSpec(memory_space=pltpu.VMEM)
    key_block = shape((rows, d), BF16)
    both = call(pair_kernel, shape((2, rows, width), BF16), "pair", 4, in_specs=[vmem] * 2)(image, flip(image, "xh", 2, 1))
    pairs, cols, held = call(
        prep_kernel, [shape((1, n_im), F32), shape((1, n_ks), F32), key_block], "prep", 8, in_specs=[vmem] * 3
    )(pair_index, keys, both)
    key_x = flip(held, "xl", 2, 1)
    i0 = call(stack_kernel, shape((8, rows, width), BF16), "stack", 8, in_specs=[vmem] * 5)(
        both, *[shift(both, "zh", 4, k) for k in (1, 2, 3)], pairs
    )
    i1, i3 = shift(i0, "y", 4, 1), shift(i0, "y", 4, 3)
    quarter = shape((rows // 2, d), BF16)
    held = call(hold_kernel, key_block, "hold", 8, in_specs=[vmem] * 2)(held, i0)
    key_z = flip(held, "zl", 2, 1)
    d_low = flip(call(low_kernel, quarter, "low", 8, in_specs=[vmem] * 2)(key_x, i0), "zl", 2, 1)
    d_top = flip(call(top_kernel, quarter, "top", 8, in_specs=[vmem])(key_z), "xl", 2, 1)
    half_block = shape((nzh, rows, width), BF16)
    ia, ib = call(turn_kernel, [half_block] * 2, "turn", 12, in_specs=[vmem] * 2)(i1, i3)
    k0 = call(join_kernel, shape((half, d), BF16), "join", 12, in_specs=[vmem] * 6)(
        held, key_x, key_z, d_top, d_low, ia
    )
    ia, ib = call(beyond_kernel, [half_block] * 2, "beyond", 8, 20 * 10**9, in_specs=[vmem] * 2)(
        shift(ia, "y", 4, 1), shift(ib, "y", 4, 3)
    )
    ks = [k0, flip(k0, "core", 2, 1)]

    tile = min(384, n_im)
    scores, im, rs, cs = call(
        functools.partial(scores_kernel, scale),
        [shape((n_im, n_ks), F32), shape((n_im, d), BF16), shape((2, n_im), F32), shape((2, n_ks), F32)],
        "scores",
        28,
        in_specs=[vmem] * 9,
    )(*ks, i0, i1, i3, ia, ib, pairs, cols)
    rs = call(meet_rows_kernel, shape((2, n_im), F32), "meet_rows", 4, in_specs=[vmem] * 2)(rs, flip(rs, "zh", 4, 1))
    rstats = [rs, flip(rs, "zh", 4, 3)]
    cs = call(meet_kernel, shape((2, n_ks), F32), "meet", 4, in_specs=[vmem] * 2)(cs, flip(cs, "core", 2, 1))
    cstats = [cs] + [lax.ppermute(cs, ("zl", "xl"), [(i, i ^ k) for i in range(4)]) for k in (1, 2, 3)]
    outs = [shape((n_im, 2 * width), F32)] * 3 + [shape((n_im // 2 + PAD, 2 * width), I16)] * 2
    outs += [shape((half, d), F32), shape((4, rows + PAD, d), I16)] + [shape((1, rows), F32)] * 2
    own, p1, p3, q2a, q2b, mine, sent, row_loss, col_loss = call(
        functools.partial(weights_kernel, scale, tile),
        outs,
        "weights",
        36,
        in_specs=[vmem] * 12,
        scratch_shapes=[pltpu.VMEM((n_im, n_ks), BF16), pltpu.VMEM((n_im, d), F32)],
    )(*rstats, *cstats, pairs, cols, scores, *ks, im)
    own_key, keep_x, keep_z, to_x, to_z = call(
        key_sum_kernel,
        [shape((rows, d), F32)] + [shape((rows, d // 2), F32)] * 2 + [shape((2, rows + PAD, d // 2), I16)] * 2,
        "key_sum",
        16,
        in_specs=[vmem] * 2,
    )(mine, flip(sent, "core", 2, 1))
    q1, q3 = call(
        relay_kernel, [shape((n_im + PAD, 2 * width), I16)] * 2, "relay", 12, 20 * 10**9, in_specs=[vmem] * 5
    )(own_key, p1, p3, shift(q2a, "y", 4, 1), shift(q2b, "y", 4, 3))
    q1, q3 = shift(q1, "y", 4, 1), shift(q3, "y", 4, 3)
    own_key, to_x, to_z = call(
        key_relay_kernel,
        [shape((rows, d), F32)] + [shape((rows + PAD, d // 2), I16)] * 2,
        "key_relay",
        12,
        in_specs=[vmem] * 5,
    )(own_key, keep_x, keep_z, flip(to_x, "xl", 2, 1), flip(to_z, "zl", 2, 1))
    from_x, from_z = flip(to_x, "xl", 2, 1), flip(to_z, "zl", 2, 1)
    total = call(image_sum_kernel, shape((n_im, 2 * width), F32), "image_sum", 12, in_specs=[vmem] * 4)(
        own_key, own, q1, q3
    )
    pieces = call(image_code_kernel, shape((8, rows + PAD, width), I16), "image_code", 12, in_specs=[vmem] * 2)(
        from_x, total
    )
    pieces = lax.all_to_all(pieces, ("xh", "zh"), 0, 0)
    modality_grad, image_grad = call(
        last_kernel, [shape((rows, d), F32), shape((rows, width), F32)], "last", 8, in_specs=[vmem] * 4
    )(own_key, from_x, from_z, pieces)
    return (image_grad, modality_grad[None], row_loss, col_loss)


def solution(mesh):
    ny = mesh.devices.shape[0] // 2
    nzh = mesh.devices.shape[1] // 8
    names = ("y", "xh", "zh", "zl", "xl", "core")
    fine = Mesh(mesh.devices.reshape(ny, 2, nzh, 2, 2, 2), names)
    mod, rows = names[:2], names[2:]
    in_specs = (P(rows, mod), P(mod, rows, None), P(mod, None))
    out_specs = (P(rows, mod), P(mod, rows, None), P(mod, rows), P(mod, rows))
    return jax.shard_map(
        on_device, mesh=fine, in_specs=in_specs, out_specs=out_specs, check_vma=False
    )
```
